32 devices in a mesh: fsdp: 4 (over x, core), ctx: 8 (over z, y).
Axes of the slice: x: 2, y: 2, z: 4, core: 2. Of those that a mesh axis runs over, the one named last changes fastest.
Arguments:
- tokens: bfloat16 [8, 2048, 1280], P('fsdp', 'ctx'), may hold values from -6 to 6
- cotangent: bfloat16 [8, 2048, 1280], P('fsdp', 'ctx'), may hold values from -6 to 6
- lengths: int32 [8, 20], P('fsdp'), may hold values from 0 to 2048, as said below
- widths: int32 [8, 20], P('fsdp'), may hold values from 8 to 32
- weight_qkv: float32 [1280, 3840], P('fsdp'), may hold values from -0.25 to 0.25
- moment_qkv: float32 [1280, 3840], P('fsdp')
- square_qkv: float32 [1280, 3840], P('fsdp'), as said below
- weight_out: float32 [1280, 1280], P('fsdp'), may hold values from -0.625 to 0.625
- moment_out: float32 [1280, 1280], P('fsdp')
- square_out: float32 [1280, 1280], P('fsdp'), as said below
- weight_up: float32 [1280, 5120], P('fsdp'), may hold values from -0.15625 to 0.15625
- moment_up: float32 [1280, 5120], P('fsdp')
- square_up: float32 [1280, 5120], P('fsdp'), as said below
- weight_down: float32 [5120, 1280], P('fsdp'), may hold values from -0.125 to 0.125
- moment_down: float32 [5120, 1280], P('fsdp')
- square_down: float32 [5120, 1280], P('fsdp'), as said below
- vectors: float32 [16640], P('fsdp')
- moment_vectors: float32 [16640], P('fsdp')
- square_vectors: float32 [16640], P('fsdp'), as said below
Outputs:
- output: bfloat16 [8, 2048, 1280], P('fsdp', 'ctx')
- input_grad: float32 [8, 2048, 1280], P('fsdp', 'ctx')
- grad_norm: float32 [], replicated
- new_weight_qkv: float32 [1280, 3840], P('fsdp')
- new_moment_qkv: float32 [1280, 3840], P('fsdp')
- new_square_qkv: float32 [1280, 3840], P('fsdp')
- new_weight_out: float32 [1280, 1280], P('fsdp')
- new_moment_out: float32 [1280, 1280], P('fsdp')
- new_square_out: float32 [1280, 1280], P('fsdp')
- new_weight_up: float32 [1280, 5120], P('fsdp')
- new_moment_up: float32 [1280, 5120], P('fsdp')
- new_square_up: float32 [1280, 5120], P('fsdp')
- new_weight_down: float32 [5120, 1280], P('fsdp')
- new_moment_down: float32 [5120, 1280], P('fsdp')
- new_square_down: float32 [5120, 1280], P('fsdp')
- new_vectors: float32 [16640], P('fsdp')
- new_moment_vectors: float32 [16640], P('fsdp')
- new_square_vectors: float32 [16640], P('fsdp')
The draws below stay inside these ranges and needn't reach their ends.
Inputs may be any that keep to these rules, and one draw needn't show every extreme that they name: `lengths`: each row lists its pictures in order, then zeros. In a row of several pictures, the pictures fill the first slots, every picture but the last holds 100 to 1024 patches, and the padding after them is at most 256 slots. In each aligned block of 2 rows exactly one row holds a single picture of all 2048 slots. `square_qkv`: positive. `square_out`: positive. `square_up`: positive. `square_down`: positive. `square_vectors`: positive.
All inputs are finite; a program needn't handle non-finite values.
Results may differ from the reference program's by a relative error of at most 0.025.
Values may be sent and summed in bfloat16 or wider, within the bound.
A program may use at most 448 MiB of HBM per device.

```python
import jax
import jax.numpy as jnp
from jax import lax

D = 1280
HEADS = 16
HEAD_DIM = 80
FF = 5120
SLOTS = 2048
R_DEV = 2
PICS = 20
MINPIC = 100
MAXPIC = 1024
STEP = 5
ROWS = 8
NPARAM = 19677440


def first_moment(key, shape, factor):
    return factor * NPARAM ** (-0.5) / 9.0 * jax.random.normal(key, shape, jnp.float32)


def second_moment(key, shape, factor):
    spread = jax.random.uniform(key, shape, jnp.float32, 0.0, 1.0)
    return factor * factor / NPARAM / 999.0 * jnp.exp(jnp.log(4.0) * spread)


def draw_lengths(key, part):
    key = jax.random.fold_in(key, 11)
    key_drawn, key_pad, key_pick = jax.random.split(key, 3)
    drawn = jax.random.randint(key_drawn, (ROWS, PICS), MINPIC, MAXPIC + 1)
    padding = jax.random.randint(key_pad, (ROWS, 1), 0, SLOTS // 8 + 1)
    filled = SLOTS - padding
    before = jnp.cumsum(drawn, axis=1) - drawn
    pieces = jnp.clip(filled - before, 0, drawn)
    chosen = jax.random.randint(key_pick, (ROWS // R_DEV, 1), 0, R_DEV)
    row_ids = jnp.arange(ROWS).reshape(ROWS // R_DEV, R_DEV)
    whole_row = (row_ids % R_DEV == chosen).reshape(ROWS, 1)
    single = jnp.where(jnp.arange(PICS)[None, :] == 0, SLOTS, 0)
    return jnp.where(whole_row, single, pieces).astype(jnp.int32)


def draw_vectors(key, part):
    key = jax.random.fold_in(key, 5)
    key_noise, key_jitter = jax.random.split(key)
    extent = 9 * D + FF
    places = jnp.arange(extent)
    noise = jax.random.normal(key_noise, (extent,), jnp.float32)
    jitter = jax.random.uniform(key_jitter, (extent,), jnp.float32, 0.8, 1.2)
    gain_low, gain_high = (0.6, 1.8)
    fraction = (places % D).astype(jnp.float32) / (D - 1)
    gains = (gain_low + (gain_high - gain_low) * fraction) * jitter
    is_gain = (places < D) | (places >= 6 * D) & (places < 7 * D)
    return jnp.where(is_gain, gains, 0.3 * noise)


def draw_moment_qkv(key, part):
    key = jax.random.fold_in(key, 21)
    return first_moment(key, (D, 3 * D), 1.0)


def draw_square_qkv(key, part):
    key = jax.random.fold_in(key, 22)
    return second_moment(key, (D, 3 * D), 1.0)


def draw_moment_out(key, part):
    key = jax.random.fold_in(key, 23)
    return first_moment(key, (D, D), 1.0)


def draw_square_out(key, part):
    key = jax.random.fold_in(key, 24)
    return second_moment(key, (D, D), 1.0)


def draw_moment_up(key, part):
    key = jax.random.fold_in(key, 25)
    return first_moment(key, (D, FF), 1.0)


def draw_square_up(key, part):
    key = jax.random.fold_in(key, 26)
    return second_moment(key, (D, FF), 1.0)


def draw_moment_down(key, part):
    key = jax.random.fold_in(key, 27)
    return first_moment(key, (FF, D), 1.0)


def draw_square_down(key, part):
    key = jax.random.fold_in(key, 28)
    return second_moment(key, (FF, D), 1.0)


def draw_moment_vectors(key, part):
    key = jax.random.fold_in(key, 29)
    return first_moment(key, (9 * D + FF,), 3.0)


def draw_square_vectors(key, part):
    key = jax.random.fold_in(key, 30)
    return second_moment(key, (9 * D + FF,), 3.0)


def place_ends(array, own_key, low, high):
    spot = [jax.random.randint(jax.random.fold_in(own_key, axis), (), 0, length) for axis, length in enumerate(array.shape)]
    longest = array.shape.index(max(array.shape))
    next_to = spot[:longest] + [(spot[longest] + 1) % array.shape[longest]] + spot[longest + 1:]
    return array.at[tuple(spot)].set(low).at[tuple(next_to)].set(high)


def shard_levels(key, shape, cuts, low, largest):
    def one(dim, blocks):
        draws = jax.random.uniform(jax.random.fold_in(jax.random.fold_in(key, 6), dim), (blocks,), jnp.float32, low / len(cuts), largest / len(cuts))
        return jnp.repeat(jnp.exp(draws), shape[dim] // blocks).reshape((-1,) + (1,) * (len(shape) - dim - 1))

    gain = one(*cuts[0])
    for cut in cuts[1:]:
        gain = gain * one(*cut)
    return gain


def gaussian(rng, shape, scale, reach, cuts=(), held_as=jnp.bfloat16):
    entries = jax.random.normal(rng, shape, jnp.float32) * scale
    if len(cuts) > 0:
        entries = shard_levels(rng, shape, cuts, -0.22, 0.18) * entries
    return jnp.clip(entries, min=-reach, max=reach).astype(held_as)


def setup_inputs(seed: int = 0) -> dict:
    splits = jax.random.split(jax.random.key(seed), 20)
    return {
        "tokens": gaussian(splits[0], (ROWS, SLOTS, D), 1.0, 6.0, ((0, 4), (1, 8))),
        "cotangent": gaussian(splits[1], (ROWS, SLOTS, D), 1.0, 6.0, ((0, 4), (1, 8))),
        "lengths": draw_lengths(jax.random.fold_in(splits[19], 71), 0),
        "widths": place_ends(jax.random.randint(splits[3], (ROWS, PICS), 8, 33), jax.random.fold_in(splits[3], 1), 8, 32).astype(jnp.int32),
        "weight_qkv": gaussian(splits[4], (D, 3 * D), (D // 2) ** -0.5, 0.25, ((0, 4),), jnp.float32),
        "moment_qkv": draw_moment_qkv(jax.random.fold_in(splits[19], 71), 0),
        "square_qkv": draw_square_qkv(jax.random.fold_in(splits[19], 71), 0),
        "weight_out": gaussian(splits[7], (D, D), (D // 16) ** -0.5, 0.625, ((0, 4),), jnp.float32),
        "moment_out": draw_moment_out(jax.random.fold_in(splits[19], 71), 0),
        "square_out": draw_square_out(jax.random.fold_in(splits[19], 71), 0),
        "weight_up": gaussian(splits[10], (D, FF), D ** -0.5, 0.15625, ((0, 4),), jnp.float32),
        "moment_up": draw_moment_up(jax.random.fold_in(splits[19], 71), 0),
        "square_up": draw_square_up(jax.random.fold_in(splits[19], 71), 0),
        "weight_down": gaussian(splits[13], (FF, D), (FF // 2) ** -0.5, 0.125, ((0, 4),), jnp.float32),
        "moment_down": draw_moment_down(jax.random.fold_in(splits[19], 71), 0),
        "square_down": draw_square_down(jax.random.fold_in(splits[19], 71), 0),
        "vectors": draw_vectors(jax.random.fold_in(splits[19], 71), 0),
        "moment_vectors": draw_moment_vectors(jax.random.fold_in(splits[19], 71), 0),
        "square_vectors": draw_square_vectors(jax.random.fold_in(splits[19], 71), 0),
    }


@jax.custom_vjp
def low(v):
    return lax.optimization_barrier(v.astype(jnp.bfloat16)).astype(jnp.float32)

@jax.custom_vjp
def low_back(v):
    return v

def low_keep(v):
    return (low(v), None)

def low_pass(kept, grad):
    return (grad,)

def back_keep(v):
    return (v, None)

def back_low(kept, grad):
    return (low(grad),)
low.defvjp(low_keep, low_pass)
low_back.defvjp(back_keep, back_low)
highest = lax.Precision.HIGHEST
eps_norm = 1e-06
beta_one = 0.9
beta_two = 0.999
adam_eps = 1e-08
decay_matrix = 0.05
rate_matrix = 0.04
rate_vector = 0.3
clip_level = 1.0

def layout(lengths, widths, extent):
    piece_ends = jnp.cumsum(lengths, axis=1).astype(jnp.int32)
    piece_starts = piece_ends - lengths
    places = jnp.arange(extent, dtype=jnp.int32)
    picture = lax.optimization_barrier(jnp.sum((places[None, :, None] >= piece_ends[:, None, :]).astype(jnp.int32), axis=2)).astype(jnp.int32)
    numbers = jnp.arange(lengths.shape[1], dtype=jnp.int32)
    onehot = (picture[:, :, None] == numbers[None, None, :]).astype(jnp.int32)
    start_of = lax.optimization_barrier(jnp.sum(onehot * piece_starts[:, None, :], axis=2)).astype(jnp.int32)
    width_of = jnp.maximum(lax.optimization_barrier(jnp.sum(onehot * widths[:, None, :], axis=2)), 1).astype(jnp.int32)
    inside = places[None, :] - start_of
    return (picture, inside // width_of, inside % width_of, picture < lengths.shape[1])

def rotary_tables(row_pos, col_pos):
    quarter = HEAD_DIM // 4
    inverse = 10000.0 ** (-(2.0 * jnp.arange(quarter, dtype=jnp.float32)) / (HEAD_DIM // 2))
    angles = jnp.concatenate([row_pos.astype(jnp.float32)[..., None] * inverse, col_pos.astype(jnp.float32)[..., None] * inverse], axis=-1)
    angles = jnp.concatenate([angles, angles], axis=-1)
    return (jnp.cos(angles), jnp.sin(angles))

def turn_half(values):
    half_dim = values.shape[-1] // 2
    return jnp.concatenate([-values[..., half_dim:], values[..., :half_dim]], axis=-1)

def split_vector(vector, width, hidden_units):
    return (vector[:width], vector[width:2 * width], vector[2 * width:5 * width], vector[5 * width:6 * width], vector[6 * width:7 * width], vector[7 * width:8 * width], vector[8 * width:8 * width + hidden_units], vector[8 * width + hidden_units:])

def product(left, right):
    return jnp.dot(left, right, precision=highest, preferred_element_type=jnp.float32)

def layer_norm(inputs, gain_vector, shift_vector):
    center = inputs - lax.optimization_barrier(jnp.mean(inputs, axis=-1, keepdims=True))
    scaled = center * lax.rsqrt(lax.optimization_barrier(jnp.mean(center * center, axis=-1, keepdims=True)) + eps_norm)
    return scaled * gain_vector + shift_vector

def attend_row(query_rows, key_rows, value_rows, picture_row):
    scores = jnp.einsum('qhd,khd->hqk', query_rows, key_rows, precision=highest) * HEAD_DIM ** (-0.5)
    scores = low_back(scores)
    same_picture = picture_row[:, None] == picture_row[None, :]
    scores = jnp.where(same_picture[None], scores, -1e+30)
    row_peak = lax.optimization_barrier(jnp.max(scores, axis=-1, keepdims=True))
    raised = jnp.exp(scores - row_peak)
    attention = low(raised / lax.optimization_barrier(jnp.sum(raised, axis=-1, keepdims=True)))
    return jnp.einsum('hqk,khd->qhd', attention, value_rows, precision=highest)

def attend_items(items):
    return attend_row(items[0], items[1], items[2], items[3])

def adam_update(weight, moment, square, grad, factor, rate, decay):
    clipped = grad * factor
    moment = beta_one * moment + (1.0 - beta_one) * clipped
    square = beta_two * square + (1.0 - beta_two) * clipped * clipped
    fixed_moment = moment / (1.0 - beta_one ** STEP)
    fixed_square = square / (1.0 - beta_two ** STEP)
    weight = weight - rate * (fixed_moment / (jnp.sqrt(fixed_square) + adam_eps) + decay * weight)
    return (weight, moment, square)

def reference(tokens, cotangent, lengths, widths, weight_qkv, moment_qkv, square_qkv, weight_out, moment_out, square_out, weight_up, moment_up, square_up, weight_down, moment_down, square_down, vectors, moment_vectors, square_vectors):
    picture, row_pos, col_pos, valid_slots = layout(lengths, widths, SLOTS)
    cosine_table, sine_table = rotary_tables(row_pos, col_pos)
    cosine_table = cosine_table[:, :, None, :]
    sine_table = sine_table[:, :, None, :]
    shape_heads = (ROWS, SLOTS, HEADS, HEAD_DIM)

    def forward(inputs, vector_all, matrix_qkv, matrix_out, matrix_up, matrix_down):
        vector_all = low(vector_all)
        matrix_qkv = low(matrix_qkv)
        matrix_out = low(matrix_out)
        matrix_up = low(matrix_up)
        matrix_down = low(matrix_down)
        gain_one, shift_one, bias_qkv, bias_out, gain_two, shift_two, bias_up, bias_down = split_vector(vector_all, D, FF)
        flat_tokens = inputs.reshape(ROWS * SLOTS, D)
        first_normed = low(layer_norm(flat_tokens, gain_one, shift_one))
        joined = low_back(product(first_normed, matrix_qkv) + bias_qkv)
        query_raw = joined[:, :D].reshape(shape_heads)
        keys_raw = joined[:, D:2 * D].reshape(shape_heads)
        query_turned = low(query_raw * cosine_table + turn_half(query_raw) * sine_table)
        keys_turned = low(keys_raw * cosine_table + turn_half(keys_raw) * sine_table)
        values_low = low(joined[:, 2 * D:].reshape(shape_heads))
        mixed = lax.map(jax.checkpoint(attend_items), (query_turned, keys_turned, values_low, picture))
        mixed = low(low_back(mixed.reshape(ROWS * SLOTS, D)))
        hidden = flat_tokens + low_back(product(mixed, matrix_out) + bias_out)
        second_normed = low(layer_norm(hidden, gain_two, shift_two))
        upper = low_back(product(second_normed, matrix_up) + bias_up)
        active = low(upper * jax.nn.sigmoid(1.702 * upper))
        result = hidden + product(active, matrix_down) + bias_down
        return result.reshape(ROWS, SLOTS, D)
    result, pullback = jax.vjp(forward, tokens.astype(jnp.float32), vectors, weight_qkv, weight_out, weight_up, weight_down)
    grad_result = cotangent.astype(jnp.float32) * valid_slots[..., None].astype(jnp.float32)
    input_grad, grad_vector, grad_qkv, grad_outw, grad_up, grad_down = pullback(grad_result)
    squares = jnp.sum(grad_qkv * grad_qkv) + jnp.sum(grad_outw * grad_outw) + jnp.sum(grad_up * grad_up) + jnp.sum(grad_down * grad_down) + jnp.sum(grad_vector * grad_vector)
    grad_norm = jnp.sqrt(squares)
    factor = jnp.minimum(1.0, clip_level / grad_norm)
    new_qkv = adam_update(weight_qkv, moment_qkv, square_qkv, grad_qkv, factor, rate_matrix, decay_matrix)
    new_out = adam_update(weight_out, moment_out, square_out, grad_outw, factor, rate_matrix, decay_matrix)
    new_up = adam_update(weight_up, moment_up, square_up, grad_up, factor, rate_matrix, decay_matrix)
    new_down = adam_update(weight_down, moment_down, square_down, grad_down, factor, rate_matrix, decay_matrix)
    new_vec = adam_update(vectors, moment_vectors, square_vectors, grad_vector, factor, rate_vector, 0.0)
    return (result.astype(jnp.bfloat16), input_grad, grad_norm, new_qkv[0], new_qkv[1], new_qkv[2], new_out[0], new_out[1], new_out[2], new_up[0], new_up[1], new_up[2], new_down[0], new_down[1], new_down[2], new_vec[0], new_vec[1], new_vec[2])
```

```python
import functools

import jax
import jax.numpy as jnp
from jax import lax
from jax.experimental import pallas as pl
from jax.experimental.pallas import tpu as pltpu
from jax.sharding import PartitionSpec as P

HEADS = 16
HEAD_DIM = 80
STEP = 5


eps_norm = 1e-06
beta_one = 0.9
beta_two = 0.999
adam_eps = 1e-08
decay_matrix = 0.05
rate_matrix = 0.04
rate_vector = 0.3
clip_level = 1.0


LOG2E = 1.4426950408889634


MESH = pl.DeviceIdType.MESH


def exchange_kernel(source, target, send_sem, recv_sem, own_sem, *, count):
    group, me = lax.axis_index("fsdp"), lax.axis_index("ctx")
    barrier = pltpu.get_barrier_semaphore()
    for step in range(1, count):
        other = lax.rem(me + step, count)
        pl.semaphore_signal(barrier, inc=1, device_id=(group, other), device_id_type=MESH)
    pl.semaphore_wait(barrier, count - 1)
    copies = []
    for step in range(1, count):
        other = lax.rem(me + step, count)
        copy = pltpu.make_async_remote_copy(
            src_ref=source.at[:, other],
            dst_ref=target.at[:, me],
            send_sem=send_sem.at[step],
            recv_sem=recv_sem.at[step],
            device_id=(group, other),
            device_id_type=MESH,
        )
        copy.start()
        copies.append(copy)
    own = pltpu.make_async_copy(source.at[:, me], target.at[:, me], own_sem)
    own.start()
    own.wait()
    for copy in copies:
        copy.wait()


def exchange(source, number):
    count = source.shape[1]
    return pl.pallas_call(
        functools.partial(exchange_kernel, count=count),
        out_shape=jax.ShapeDtypeStruct(source.shape, source.dtype),
        in_specs=[pl.BlockSpec(memory_space=pl.ANY)],
        out_specs=pl.BlockSpec(memory_space=pl.ANY),
        scratch_shapes=[
            pltpu.SemaphoreType.DMA((count,)),
            pltpu.SemaphoreType.DMA((count,)),
            pltpu.SemaphoreType.DMA,
        ],
        compiler_params=pltpu.CompilerParams(collective_id=number, has_side_effects=True),
        name="exchange",
    )(source)


def attend_kernel(span, qkv, low_high, out, stat, keys, *, heads, size, extent):
    row, block = pl.program_id(0), pl.program_id(1)
    blocks = extent // size
    scale = HEAD_DIM ** (-0.5) * LOG2E

    @pl.when(block == 0)
    def _():
        for h in range(heads):
            for b in range(blocks):
                keys[h, b * size:(b + 1) * size, :] = qkv[1, b, h * HEAD_DIM:(h + 1) * HEAD_DIM, :].T

    first, last, plain = span[row, block, 0], span[row, block, 1], span[row, block, 2]
    query = [qkv[0, block, h * HEAD_DIM:(h + 1) * HEAD_DIM, :] for h in range(heads)]
    low, high = low_high[0, 0:1, :], low_high[0, 1:2, :]

    def step(b, carry, masked):
        peaks, totals, sums = carry
        if masked:
            places = lax.broadcasted_iota(jnp.int32, (size, size), 0) + b * size
            keep = (places >= low) & (places < high)
        scores = []
        for h in range(heads):
            s = jnp.dot(keys[h, pl.ds(pl.multiple_of(b * size, size), size), :], query[h],
                        preferred_element_type=jnp.float32) * scale
            if masked:
                s = jnp.where(keep, s, -1e30)
            scores.append(s)
        new_p, new_t, new_s = [], [], []
        for h in range(heads):
            peak = jnp.maximum(peaks[h], jnp.max(scores[h], axis=0, keepdims=True))
            fade = jnp.exp2(peaks[h] - peak)
            raised = jnp.exp2(scores[h] - peak)
            new_t.append(totals[h] * fade + jnp.sum(raised, axis=0, keepdims=True))
            values = qkv[2, b, h * HEAD_DIM:(h + 1) * HEAD_DIM, :]
            new_s.append(sums[h] * fade + jnp.dot(values, raised.astype(jnp.bfloat16),
                                                  preferred_element_type=jnp.float32))
            new_p.append(peak)
        return tuple(new_p), tuple(new_t), tuple(new_s)

    def finish(carry):
        peaks, totals, sums = carry
        for h in range(heads):
            out[0, h * HEAD_DIM:(h + 1) * HEAD_DIM, :] = (sums[h] / totals[h]).astype(jnp.bfloat16)
            stat[0, h:h + 1, :] = peaks[h] + jnp.log2(totals[h])

    start = (
        tuple(jnp.full((1, size), -1e30, jnp.float32) for _ in range(heads)),
        tuple(jnp.zeros((1, size), jnp.float32) for _ in range(heads)),
        tuple(jnp.zeros((HEAD_DIM, size), jnp.float32) for _ in range(heads)),
    )

    @pl.when(plain == 1)
    def _():
        finish(lax.fori_loop(first, last, functools.partial(step, masked=False), start))

    @pl.when(plain == 0)
    def _():
        finish(lax.fori_loop(first, last, functools.partial(step, masked=True), start))


def attend(span, qkv, low_high):
    _, blocks, width, lanes = qkv.shape
    rows = span.shape[0]
    size = lanes // rows
    heads = width // HEAD_DIM
    grid_spec = pltpu.PrefetchScalarGridSpec(
        num_scalar_prefetch=1,
        grid=(rows, blocks),
        in_specs=[
            pl.BlockSpec((3, blocks, width, size), lambda r, b, s: (0, 0, 0, r)),
            pl.BlockSpec((1, 2, size), lambda r, b, s: (b, 0, r)),
        ],
        out_specs=[
            pl.BlockSpec((1, width, size), lambda r, b, s: (b, 0, r)),
            pl.BlockSpec((1, heads, size), lambda r, b, s: (b, 0, r)),
        ],
        scratch_shapes=[pltpu.VMEM((heads, blocks * size, HEAD_DIM), jnp.bfloat16)],
    )
    return pl.pallas_call(
        functools.partial(attend_kernel, heads=heads, size=size, extent=blocks * size),
        grid_spec=grid_spec,
        out_shape=[
            jax.ShapeDtypeStruct((blocks, width, lanes), jnp.bfloat16),
            jax.ShapeDtypeStruct((blocks, heads, lanes), jnp.float32),
        ],
        compiler_params=pltpu.CompilerParams(vmem_limit_bytes=48 * 1024 * 1024),
        name="attend",
    )(span, qkv, low_high)


def attend_back_kernel(span, qkv, low_high, mixed, d_mixed, stat, cosine, sine, out, keys, values, d_keys, d_values,
                       *, heads, size, extent):
    row, block = pl.program_id(0), pl.program_id(1)
    blocks = extent // size
    scale = HEAD_DIM ** (-0.5)
    half = HEAD_DIM // 2

    @pl.when(block == 0)
    def _():
        d_keys[...] = jnp.zeros_like(d_keys)
        d_values[...] = jnp.zeros_like(d_values)
        for h in range(heads):
            for b in range(blocks):
                keys[h, b * size:(b + 1) * size, :] = qkv[1, b, h * HEAD_DIM:(h + 1) * HEAD_DIM, :].T
                values[h, b * size:(b + 1) * size, :] = qkv[2, b, h * HEAD_DIM:(h + 1) * HEAD_DIM, :].T

    def turn_back(v, cos, sin):
        upper, lower = v[half:], v[:half]
        return jnp.concatenate([lower * cos + upper * sin, upper * cos - lower * sin], axis=0)

    first, last, plain = span[row, block, 0], span[row, block, 1], span[row, block, 2]
    low, high = low_high[0, 0:1, :], low_high[0, 1:2, :]
    part = [slice(h * HEAD_DIM, (h + 1) * HEAD_DIM) for h in range(heads)]
    query = [qkv[0, block, part[h], :] for h in range(heads)]
    query_n = [q.T for q in query]
    grad = [d_mixed[0, part[h], :] for h in range(heads)]
    grad_n = [g.T for g in grad]
    delta = [jnp.sum(grad[h].astype(jnp.float32) * mixed[0, part[h], :].astype(jnp.float32), axis=0, keepdims=True)
             for h in range(heads)]
    lse = [stat[0, h:h + 1, :] for h in range(heads)]

    def step(b, carry, masked):
        if masked:
            places = lax.broadcasted_iota(jnp.int32, (size, size), 0) + b * size
            keep = (places >= low) & (places < high)
        here = pl.ds(pl.multiple_of(b * size, size), size)
        scores = [jnp.dot(keys[h, here, :], query[h], preferred_element_type=jnp.float32) for h in range(heads)]
        d_probs = [jnp.dot(values[h, here, :], grad[h], preferred_element_type=jnp.float32) for h in range(heads)]
        new = []
        for h in range(heads):
            exact = jnp.exp2(scores[h] * (scale * LOG2E) - lse[h])
            if masked:
                exact = jnp.where(keep, exact, 0.0)
            d_scores = (exact * (d_probs[h] - delta[h])).astype(jnp.bfloat16)
            exact = exact.astype(jnp.bfloat16)
            d_values[h, here, :] += jnp.dot(exact, grad_n[h], preferred_element_type=jnp.float32)
            d_keys[h, here, :] += jnp.dot(d_scores, query_n[h], preferred_element_type=jnp.float32)
            new.append(carry[h] + jnp.dot(qkv[1, b, part[h], :], d_scores, preferred_element_type=jnp.float32))
        return tuple(new)

    def finish(carry):
        cos, sin = cosine[block], sine[block]
        for h in range(heads):
            out[0, block, part[h], :] = turn_back(carry[h] * scale, cos, sin).astype(jnp.bfloat16)

    start = tuple(jnp.zeros((HEAD_DIM, size), jnp.float32) for _ in range(heads))

    @pl.when(plain == 1)
    def _():
        finish(lax.fori_loop(first, last, functools.partial(step, masked=False), start))

    @pl.when(plain == 0)
    def _():
        finish(lax.fori_loop(first, last, functools.partial(step, masked=True), start))

    @pl.when(block == blocks - 1)
    def _():
        for h in range(heads):
            for b in range(blocks):
                here = slice(b * size, (b + 1) * size)
                out[1, b, part[h], :] = turn_back(d_keys[h, here, :].T * scale, cosine[b], sine[b]).astype(jnp.bfloat16)
                out[2, b, part[h], :] = d_values[h, here, :].T.astype(jnp.bfloat16)


def attend_back(span, qkv, low_high, mixed, d_mixed, stat, cosine, sine):
    _, blocks, width, lanes = qkv.shape
    rows = span.shape[0]
    size = lanes // rows
    heads = width // HEAD_DIM
    per = lambda r, b, s: (b, 0, r)
    whole = lambda r, b, s: (0, 0, r)
    grid_spec = pltpu.PrefetchScalarGridSpec(
        num_scalar_prefetch=1,
        grid=(rows, blocks),
        in_specs=[
            pl.BlockSpec((3, blocks, width, size), lambda r, b, s: (0, 0, 0, r)),
            pl.BlockSpec((1, 2, size), per),
            pl.BlockSpec((1, width, size), per),
            pl.BlockSpec((1, width, size), per),
            pl.BlockSpec((1, heads, size), per),
            pl.BlockSpec((blocks, HEAD_DIM // 2, size), whole),
            pl.BlockSpec((blocks, HEAD_DIM // 2, size), whole),
        ],
        out_specs=pl.BlockSpec((3, blocks, width, size), lambda r, b, s: (0, 0, 0, r)),
        scratch_shapes=[
            pltpu.VMEM((heads, blocks * size, HEAD_DIM), jnp.bfloat16),
            pltpu.VMEM((heads, blocks * size, HEAD_DIM), jnp.bfloat16),
            pltpu.VMEM((heads, blocks * size, HEAD_DIM), jnp.float32),
            pltpu.VMEM((heads, blocks * size, HEAD_DIM), jnp.float32),
        ],
    )
    return pl.pallas_call(
        functools.partial(attend_back_kernel, heads=heads, size=size, extent=blocks * size),
        grid_spec=grid_spec,
        out_shape=jax.ShapeDtypeStruct(qkv.shape, jnp.bfloat16),
        compiler_params=pltpu.CompilerParams(vmem_limit_bytes=56 * 1024 * 1024),
        name="attend_back",
    )(span, qkv, low_high, mixed, d_mixed, stat, cosine, sine)


def layout(lengths, widths, extent):
    piece_ends = jnp.cumsum(lengths, axis=1)
    piece_starts = piece_ends - lengths
    places = jnp.arange(extent, dtype=jnp.int32)[None, :, None]
    inside = (places >= piece_starts[:, None, :]) & (places < piece_ends[:, None, :])
    pick = lambda table: jnp.sum(jnp.where(inside, table[:, None, :], 0), axis=2)
    filled = piece_ends[:, -1:]
    valid = places[..., 0] < filled
    start_of = jnp.where(valid, pick(piece_starts), filled)
    end_of = jnp.where(valid, pick(piece_ends), extent)
    width_of = jnp.where(valid, pick(widths), 1)
    within = places[..., 0] - start_of
    return within // width_of, within % width_of, valid, start_of, end_of


def by_block(table, size):
    rows, extent = table.shape
    return table.reshape(rows, extent // size, size).transpose(1, 0, 2).reshape(extent // size, rows * size)


def rotary_tables(row_pos, col_pos):
    quarter = HEAD_DIM // 4
    inverse = 10000.0 ** (-(2.0 * jnp.arange(quarter, dtype=jnp.float32)) / (HEAD_DIM // 2))
    angles = jnp.concatenate(
        [
            row_pos.astype(jnp.float32)[:, None, :] * inverse[None, :, None],
            col_pos.astype(jnp.float32)[:, None, :] * inverse[None, :, None],
        ],
        axis=1,
    )
    return (jnp.cos(angles), jnp.sin(angles))


def split_vector(vector, width, hidden_units):
    return (
        vector[:width],
        vector[width : 2 * width],
        vector[2 * width : 5 * width],
        vector[5 * width : 6 * width],
        vector[6 * width : 7 * width],
        vector[7 * width : 8 * width],
        vector[8 * width : 8 * width + hidden_units],
        vector[8 * width + hidden_units :],
    )


def standardize(inputs):
    center = inputs - jnp.mean(inputs, axis=-1, keepdims=True)
    root_inverse = lax.rsqrt(jnp.mean(center * center, axis=-1, keepdims=True) + eps_norm)
    return (center * root_inverse, root_inverse)


def norm_back(d_norm, gain_vector, scaled, root_inverse):
    effect = d_norm * gain_vector
    inner = jnp.mean(effect, axis=-1, keepdims=True)
    along = jnp.mean(effect * scaled, axis=-1, keepdims=True)
    return root_inverse * (effect - inner - scaled * along)


def adam_update(weight, moment, square, grad, factor, rate, decay):
    clipped = grad * factor
    moment = beta_one * moment + (1.0 - beta_one) * clipped
    square = beta_two * square + (1.0 - beta_two) * clipped * clipped
    fixed_moment = moment / (1.0 - beta_one**STEP)
    fixed_square = square / (1.0 - beta_two**STEP)
    weight = weight - rate * (fixed_moment / (jnp.sqrt(fixed_square) + adam_eps) + decay * weight)
    return (weight, moment, square)


def transpose_dot(left, right):
    return jnp.einsum("ti,to->io", left, right, preferred_element_type=jnp.float32)


def on_device(
    tokens,
    cotangent,
    lengths,
    widths,
    weight_qkv,
    moment_qkv,
    square_qkv,
    weight_out,
    moment_out,
    square_out,
    weight_up,
    moment_up,
    square_up,
    weight_down,
    moment_down,
    square_down,
    vectors,
    moment_vectors,
    square_vectors,
):
    full_qkv, full_out, full_up, full_down, full_vector = (
        lax.all_gather(weight_qkv.astype(jnp.bfloat16), "fsdp", axis=0, tiled=True),
        lax.all_gather(weight_out.astype(jnp.bfloat16), "fsdp", axis=0, tiled=True),
        lax.all_gather(weight_up.astype(jnp.bfloat16), "fsdp", axis=0, tiled=True),
        lax.all_gather(weight_down.astype(jnp.bfloat16), "fsdp", axis=0, tiled=True),
        lax.all_gather(vectors.astype(jnp.bfloat16), "fsdp", axis=0, tiled=True),
    )
    model_width = tokens.shape[2]
    hidden_units = full_up.shape[1]
    gain_one, shift_one, bias_qkv, bias_out, gain_two, shift_two, bias_up, bias_down = split_vector(
        full_vector.astype(jnp.float32), model_width, hidden_units
    )
    row_count = tokens.shape[0]
    slots_here = tokens.shape[1]
    slots_all = slots_here * lax.axis_size("ctx")
    token_count = row_count * slots_here
    ranks = lax.axis_size("ctx")
    here = lax.axis_index("ctx")
    local_heads = HEADS // ranks
    width = local_heads * HEAD_DIM
    row_pos, col_pos, valid_slots, start_of, end_of = layout(lengths, widths, slots_all)
    valid_here = lax.dynamic_slice_in_dim(valid_slots, here * slots_here, slots_here, 1)
    cosine_table, sine_table = rotary_tables(by_block(row_pos, slots_here), by_block(col_pos, slots_here))
    cosine_here = lax.dynamic_index_in_dim(cosine_table, here, 0, keepdims=False)
    sine_here = lax.dynamic_index_in_dim(sine_table, here, 0, keepdims=False)
    low_high = jnp.stack([by_block(start_of, slots_here), by_block(end_of, slots_here)], axis=1)
    starts = start_of.reshape(row_count, ranks, slots_here)
    ends = end_of.reshape(row_count, ranks, slots_here)
    first_block = jnp.min(starts, axis=2) // slots_here
    last_block = (jnp.max(ends, axis=2) + slots_here - 1) // slots_here
    plain = (jnp.max(starts, axis=2) <= first_block * slots_here) & (
        jnp.min(ends, axis=2) >= last_block * slots_here
    )
    span = jnp.stack([first_block, last_block, plain.astype(jnp.int32)], axis=-1).astype(jnp.int32)
    flat_tokens = tokens.reshape(token_count, model_width).astype(jnp.float32)
    scaled_one, root_one = standardize(flat_tokens)
    first_normed = (scaled_one * gain_one + shift_one).astype(jnp.bfloat16)
    joined = (
        jnp.einsum("df,td->ft", full_qkv, first_normed, preferred_element_type=jnp.float32)
        + bias_qkv[:, None]
    )
    pairs = joined[: 2 * model_width].reshape(2, HEADS, 2, HEAD_DIM // 2, token_count)
    lower, upper_half = pairs[:, :, 0], pairs[:, :, 1]
    turned = jnp.stack(
        [lower * cosine_here - upper_half * sine_here, upper_half * cosine_here + lower * sine_here],
        axis=2,
    ).reshape(2 * model_width, token_count)
    heads_out = (
        jnp.concatenate([turned, joined[2 * model_width :]], axis=0)
        .astype(jnp.bfloat16)
        .reshape(3, ranks, width, token_count)
    )
    heads_in = exchange(heads_out, 0)
    attended, lse = attend(span, heads_in, low_high)
    mixed = exchange(attended[None], 1)[0].reshape(model_width, token_count)
    hidden = flat_tokens + jnp.einsum("it,io->to", mixed, full_out, preferred_element_type=jnp.float32) + bias_out
    scaled_two, root_two = standardize(hidden)
    second_normed = (scaled_two * gain_two + shift_two).astype(jnp.bfloat16)
    upper = jnp.dot(second_normed, full_up, preferred_element_type=jnp.float32) + bias_up
    sigma = jax.nn.sigmoid(1.702 * upper)
    active = (upper * sigma).astype(jnp.bfloat16)
    result = hidden + jnp.dot(active, full_down, preferred_element_type=jnp.float32) + bias_down
    output = result.astype(jnp.bfloat16).reshape(tokens.shape)
    back_qkv, back_out, back_up, back_down = (
        lax.all_gather(weight_qkv.astype(jnp.bfloat16), "fsdp", axis=0, tiled=True),
        lax.all_gather(weight_out.astype(jnp.bfloat16), "fsdp", axis=0, tiled=True),
        lax.all_gather(weight_up.astype(jnp.bfloat16), "fsdp", axis=0, tiled=True),
        lax.all_gather(weight_down.astype(jnp.bfloat16), "fsdp", axis=0, tiled=True),
    )
    grad_result = cotangent.reshape(token_count, model_width).astype(
        jnp.float32
    ) * valid_here.reshape(token_count, 1).astype(jnp.float32)
    grad_low = grad_result.astype(jnp.bfloat16)
    d_bias_down = jnp.sum(grad_result, axis=0)
    d_weight_down = transpose_dot(active, grad_low)
    d_active = jnp.einsum("td,fd->tf", grad_low, back_down, preferred_element_type=jnp.float32)
    d_upper = (d_active * (sigma + 1.702 * upper * sigma * (1.0 - sigma))).astype(jnp.bfloat16)
    d_bias_up = jnp.sum(d_upper, axis=0, dtype=jnp.float32)
    d_weight_up = transpose_dot(second_normed, d_upper)
    d_second = jnp.einsum("tf,df->td", d_upper, back_up, preferred_element_type=jnp.float32)
    d_gain_two = jnp.sum(d_second * scaled_two, axis=0)
    d_shift_two = jnp.sum(d_second, axis=0)
    d_hidden = grad_result + norm_back(d_second, gain_two, scaled_two, root_two)
    d_branch = d_hidden.astype(jnp.bfloat16)
    d_bias_out = jnp.sum(d_branch, axis=0, dtype=jnp.float32)
    d_weight_out = jnp.einsum("it,to->io", mixed, d_branch, preferred_element_type=jnp.float32)
    d_mixed = (
        jnp.einsum("to,io->it", d_branch, back_out, preferred_element_type=jnp.float32)
        .astype(jnp.bfloat16)
        .reshape(1, ranks, width, token_count)
    )
    d_attended = exchange(d_mixed, 1)[0]
    d_heads = attend_back(
        span, heads_in, low_high, attended, d_attended, lse, cosine_table, sine_table
    )
    d_joined = exchange(d_heads, 0).reshape(3 * model_width, token_count)
    d_bias_qkv = jnp.sum(d_joined, axis=1, dtype=jnp.float32)
    d_weight_qkv = jnp.einsum(
        "td,jt->dj", first_normed, d_joined, preferred_element_type=jnp.float32
    )
    d_first = jnp.einsum("jt,dj->td", d_joined, back_qkv, preferred_element_type=jnp.float32)
    d_gain_one = jnp.sum(d_first * scaled_one, axis=0)
    d_shift_one = jnp.sum(d_first, axis=0)
    input_grad = (d_hidden + norm_back(d_first, gain_one, scaled_one, root_one)).reshape(
        tokens.shape
    )
    d_vectors = jnp.concatenate(
        [
            d_gain_one,
            d_shift_one,
            d_bias_qkv,
            d_bias_out,
            d_gain_two,
            d_shift_two,
            d_bias_up,
            d_bias_down,
        ]
    )
    group_qkv, group_out, group_up, group_down, group_vectors = (
        lax.psum_scatter(
            d_weight_qkv.astype(jnp.bfloat16), "fsdp", scatter_dimension=0, tiled=True
        ).astype(jnp.float32),
        lax.psum_scatter(
            d_weight_out.astype(jnp.bfloat16), "fsdp", scatter_dimension=0, tiled=True
        ).astype(jnp.float32),
        lax.psum_scatter(
            d_weight_up.astype(jnp.bfloat16), "fsdp", scatter_dimension=0, tiled=True
        ).astype(jnp.float32),
        lax.psum_scatter(
            d_weight_down.astype(jnp.bfloat16), "fsdp", scatter_dimension=0, tiled=True
        ).astype(jnp.float32),
        lax.psum_scatter(
            d_vectors.astype(jnp.bfloat16), "fsdp", scatter_dimension=0, tiled=True
        ).astype(jnp.float32),
    )
    grad_qkv, grad_outw, grad_up, grad_down, grad_vectors = (
        lax.psum(group_qkv.astype(jnp.bfloat16), "ctx").astype(jnp.float32),
        lax.psum(group_out.astype(jnp.bfloat16), "ctx").astype(jnp.float32),
        lax.psum(group_up.astype(jnp.bfloat16), "ctx").astype(jnp.float32),
        lax.psum(group_down.astype(jnp.bfloat16), "ctx").astype(jnp.float32),
        lax.psum(group_vectors.astype(jnp.bfloat16), "ctx").astype(jnp.float32),
    )
    squares = (
        jnp.sum(grad_qkv * grad_qkv)
        + jnp.sum(grad_outw * grad_outw)
        + jnp.sum(grad_up * grad_up)
        + jnp.sum(grad_down * grad_down)
        + jnp.sum(grad_vectors * grad_vectors)
    )
    total_squares = lax.psum(squares, "fsdp")
    grad_norm = jnp.sqrt(total_squares)
    factor = jnp.minimum(1.0, clip_level / grad_norm)
    new_qkv = adam_update(
        weight_qkv, moment_qkv, square_qkv, grad_qkv, factor, rate_matrix, decay_matrix
    )
    new_out = adam_update(
        weight_out, moment_out, square_out, grad_outw, factor, rate_matrix, decay_matrix
    )
    new_up = adam_update(
        weight_up, moment_up, square_up, grad_up, factor, rate_matrix, decay_matrix
    )
    new_down = adam_update(
        weight_down, moment_down, square_down, grad_down, factor, rate_matrix, decay_matrix
    )
    new_vec = adam_update(
        vectors, moment_vectors, square_vectors, grad_vectors, factor, rate_vector, 0.0
    )
    return (
        output,
        input_grad,
        grad_norm,
        new_qkv[0],
        new_qkv[1],
        new_qkv[2],
        new_out[0],
        new_out[1],
        new_out[2],
        new_up[0],
        new_up[1],
        new_up[2],
        new_down[0],
        new_down[1],
        new_down[2],
        new_vec[0],
        new_vec[1],
        new_vec[2],
    )


def solution(mesh):
    placed = (
        P("fsdp", "ctx", None),
        P("fsdp", "ctx", None),
        P("fsdp", None),
        P("fsdp", None),
        P("fsdp", None),
        P("fsdp", None),
        P("fsdp", None),
        P("fsdp", None),
        P("fsdp", None),
        P("fsdp", None),
        P("fsdp", None),
        P("fsdp", None),
        P("fsdp", None),
        P("fsdp", None),
        P("fsdp", None),
        P("fsdp", None),
        P("fsdp"),
        P("fsdp"),
        P("fsdp"),
    )
    return jax.shard_map(
        on_device,
        mesh=mesh,
        in_specs=placed,
        out_specs=(
            P("fsdp", "ctx", None),
            P("fsdp", "ctx", None),
            P(),
            P("fsdp", None),
            P("fsdp", None),
            P("fsdp", None),
            P("fsdp", None),
            P("fsdp", None),
            P("fsdp", None),
            P("fsdp", None),
            P("fsdp", None),
            P("fsdp", None),
            P("fsdp", None),
            P("fsdp", None),
            P("fsdp", None),
            P("fsdp"),
            P("fsdp"),
            P("fsdp"),
        ),
        check_vma=False,
    )
```

```python
import functools

import jax
import jax.numpy as jnp
from jax import lax
from jax.experimental import pallas as pl
from jax.experimental.pallas import tpu as pltpu
from jax.sharding import PartitionSpec as P

HEADS = 16
HEAD_DIM = 80
STEP = 5


eps_norm = 1e-06
beta_one = 0.9
beta_two = 0.999
adam_eps = 1e-08
decay_matrix = 0.05
rate_matrix = 0.04
rate_vector = 0.3
clip_level = 1.0


LOG2E = 1.4426950408889634


def exchange(source):
    return lax.all_to_all(source, "ctx", 0, 0)


def after(value, *others):
    return lax.optimization_barrier((value,) + others)[0]


def attend_kernel(span, qkv, low_high, out, stat, keys, values, *, size, tile, extent, step_size):
    row, place = pl.program_id(0), pl.program_id(1)
    blocks = extent // size
    group = tile // size
    scale = HEAD_DIM ** (-0.5) * LOG2E

    @pl.when(place == 0)
    def _():
        for b in range(blocks):
            keys[b * size:(b + 1) * size, :] = qkv[b, 1].T
            values[:, b * size:(b + 1) * size] = qkv[b, 2]

    first, last, plain = span[row, place, 0], span[row, place, 1], span[row, place, 2]
    query = jnp.concatenate([qkv[place * group + i, 0] for i in range(group)], axis=1)

    def finish(peak, total, mixed):
        mixed = (mixed / total).astype(jnp.bfloat16)
        lse = peak + jnp.log2(total)
        for i in range(group):
            out[i] = mixed[:, i * size:(i + 1) * size]
            stat[i] = lse[:, i * size:(i + 1) * size]

    def step(start, carry, keep=None):
        peak, total, mixed = carry
        s = jnp.dot(keys[pl.ds(start, step_size), :], query, preferred_element_type=jnp.float32) * scale
        if keep is not None:
            s = jnp.where(keep, s, -1e30)
        top = jnp.maximum(peak, jnp.max(s, axis=0, keepdims=True))
        fade = jnp.exp2(peak - top)
        raised = jnp.exp2(s - top)
        total = total * fade + jnp.sum(raised, axis=0, keepdims=True)
        mixed = mixed * fade + jnp.dot(values[:, pl.ds(start, step_size)], raised.astype(jnp.bfloat16),
                                       preferred_element_type=jnp.float32)
        return top, total, mixed

    begin = (
        jnp.full((1, tile), -1e30, jnp.float32),
        jnp.zeros((1, tile), jnp.float32),
        jnp.zeros((HEAD_DIM, tile), jnp.float32),
    )

    @pl.when(plain == 1)
    def _():
        carry = begin
        for b in range(extent // step_size):
            carry = step(b * step_size, carry)
        finish(*carry)

    @pl.when(plain == 0)
    def _():
        low = jnp.concatenate([low_high[i, 0:1, :] for i in range(group)], axis=1)
        high = jnp.concatenate([low_high[i, 1:2, :] for i in range(group)], axis=1)

        def masked(b, carry):
            start = pl.multiple_of(b * step_size, step_size)
            places = lax.broadcasted_iota(jnp.int32, (step_size, tile), 0) + start
            return step(start, carry, (places >= low) & (places < high))

        finish(*lax.fori_loop(first, last, masked, begin))


def attend(span, qkv, low_high):
    blocks, _, width, lanes = qkv.shape
    rows = span.shape[0]
    size = lanes // rows
    group = blocks // span.shape[1]
    tile = group * size
    grid_spec = pltpu.PrefetchScalarGridSpec(
        num_scalar_prefetch=1,
        grid=(rows, blocks // group),
        in_specs=[
            pl.BlockSpec((blocks, 3, width, size), lambda r, b, s: (0, 0, 0, r)),
            pl.BlockSpec((group, 2, size), lambda r, b, s: (b, 0, r)),
        ],
        out_specs=[
            pl.BlockSpec((group, width, size), lambda r, b, s: (b, 0, r)),
            pl.BlockSpec((group, 1, size), lambda r, b, s: (b, 0, r)),
        ],
        scratch_shapes=[pltpu.VMEM((blocks * size, HEAD_DIM), jnp.bfloat16), pltpu.VMEM((HEAD_DIM, blocks * size), jnp.bfloat16)],
    )
    return pl.pallas_call(
        functools.partial(attend_kernel, size=size, tile=tile, extent=blocks * size, step_size=tile),
        grid_spec=grid_spec,
        out_shape=[
            jax.ShapeDtypeStruct((blocks, width, lanes), jnp.bfloat16),
            jax.ShapeDtypeStruct((blocks, 1, lanes), jnp.float32),
        ],
        cost_estimate=pl.CostEstimate(
            flops=4 * rows * (blocks * size) ** 2 * 256,
            bytes_accessed=5 * blocks * width * lanes * 2,
            transcendentals=rows * (blocks * size) ** 2,
        ),
        compiler_params=pltpu.CompilerParams(vmem_limit_bytes=48 * 1024 * 1024),
        name="attend",
    )(span, qkv, low_high)


def attend_back_kernel(span, qkv, low_high, mixed, d_mixed, stat, cosine, sine, out, keys, values, keys_t, d_keys, d_values,
                       *, size, tile, extent, step_size):
    row, place = pl.program_id(0), pl.program_id(1)
    blocks = extent // size
    group = tile // size
    scale = HEAD_DIM ** (-0.5)
    half = HEAD_DIM // 2

    @pl.when(place == 0)
    def _():
        d_keys[...] = jnp.zeros_like(d_keys)
        d_values[...] = jnp.zeros_like(d_values)
        for b in range(blocks):
            keys[b * size:(b + 1) * size, :] = qkv[b, 1].T
            values[b * size:(b + 1) * size, :] = qkv[b, 2].T
            keys_t[:, b * size:(b + 1) * size] = qkv[b, 1]

    def turn_back(v, cos, sin):
        upper, lower = v[half:], v[:half]
        return jnp.concatenate([lower * cos + upper * sin, upper * cos - lower * sin], axis=0)

    side = lambda parts: jnp.concatenate(parts, axis=1)
    first, last, plain = span[row, place, 0], span[row, place, 1], span[row, place, 2]
    query = side([qkv[place * group + i, 0] for i in range(group)])
    grad = side([d_mixed[i] for i in range(group)])
    query_n, grad_n = query.T, grad.T
    delta = jnp.sum(grad.astype(jnp.float32) * side([mixed[i] for i in range(group)]).astype(jnp.float32), axis=0, keepdims=True)
    lse = side([stat[i] for i in range(group)])

    def step(start, d_query, keep=None):
        here = pl.ds(start, step_size)
        s = jnp.dot(keys[here, :], query, preferred_element_type=jnp.float32)
        d_probs = jnp.dot(values[here, :], grad, preferred_element_type=jnp.float32)
        exact = jnp.exp2(s * (scale * LOG2E) - lse)
        if keep is not None:
            exact = jnp.where(keep, exact, 0.0)
        d_scores = (exact * (d_probs - delta)).astype(jnp.bfloat16)
        d_values[here, :] += jnp.dot(exact.astype(jnp.bfloat16), grad_n, preferred_element_type=jnp.float32)
        d_keys[here, :] += jnp.dot(d_scores, query_n, preferred_element_type=jnp.float32)
        return d_query + jnp.dot(keys_t[:, here], d_scores, preferred_element_type=jnp.float32)

    def finish(d_query):
        for i in range(group):
            b = place * group + i
            out[b, 0] = turn_back(d_query[:, i * size:(i + 1) * size] * scale, cosine[b], sine[b]).astype(jnp.bfloat16)

    begin = jnp.zeros((HEAD_DIM, tile), jnp.float32)

    @pl.when(plain == 1)
    def _():
        d_query = begin
        for b in range(extent // step_size):
            d_query = step(b * step_size, d_query)
        finish(d_query)

    @pl.when(plain == 0)
    def _():
        low = side([low_high[i, 0:1, :] for i in range(group)])
        high = side([low_high[i, 1:2, :] for i in range(group)])

        def masked(b, d_query):
            start = pl.multiple_of(b * step_size, step_size)
            places = lax.broadcasted_iota(jnp.int32, (step_size, tile), 0) + start
            return step(start, d_query, (places >= low) & (places < high))

        finish(lax.fori_loop(first, last, masked, begin))

    @pl.when(place == blocks // group - 1)
    def _():
        for b in range(blocks):
            here = slice(b * size, (b + 1) * size)
            out[b, 1] = turn_back(d_keys[here, :].T * scale, cosine[b], sine[b]).astype(jnp.bfloat16)
            out[b, 2] = d_values[here, :].T.astype(jnp.bfloat16)


def attend_back(span, qkv, low_high, mixed, d_mixed, stat, cosine, sine):
    blocks, _, width, lanes = qkv.shape
    rows = span.shape[0]
    size = lanes // rows
    group = blocks // span.shape[1]
    tile = group * size
    per = lambda r, b, s: (b, 0, r)
    whole = lambda r, b, s: (0, 0, r)
    grid_spec = pltpu.PrefetchScalarGridSpec(
        num_scalar_prefetch=1,
        grid=(rows, blocks // group),
        in_specs=[
            pl.BlockSpec((blocks, 3, width, size), lambda r, b, s: (0, 0, 0, r)),
            pl.BlockSpec((group, 2, size), per),
            pl.BlockSpec((group, width, size), per),
            pl.BlockSpec((group, width, size), per),
            pl.BlockSpec((group, 1, size), per),
            pl.BlockSpec((blocks, HEAD_DIM // 2, size), whole),
            pl.BlockSpec((blocks, HEAD_DIM // 2, size), whole),
        ],
        out_specs=pl.BlockSpec((blocks, 3, width, size), lambda r, b, s: (0, 0, 0, r)),
        scratch_shapes=[
            pltpu.VMEM((blocks * size, HEAD_DIM), jnp.bfloat16),
            pltpu.VMEM((blocks * size, HEAD_DIM), jnp.bfloat16),
            pltpu.VMEM((HEAD_DIM, blocks * size), jnp.bfloat16),
            pltpu.VMEM((blocks * size, HEAD_DIM), jnp.float32),
            pltpu.VMEM((blocks * size, HEAD_DIM), jnp.float32),
        ],
    )
    return pl.pallas_call(
        functools.partial(attend_back_kernel, size=size, tile=tile, extent=blocks * size, step_size=tile),
        grid_spec=grid_spec,
        out_shape=jax.ShapeDtypeStruct(qkv.shape, jnp.bfloat16),
        cost_estimate=pl.CostEstimate(
            flops=10 * rows * (blocks * size) ** 2 * 256,
            bytes_accessed=10 * blocks * width * lanes * 2,
            transcendentals=rows * (blocks * size) ** 2,
        ),
        compiler_params=pltpu.CompilerParams(vmem_limit_bytes=56 * 1024 * 1024),
        name="attend_back",
    )(span, qkv, low_high, mixed, d_mixed, stat, cosine, sine)


def layout(lengths, widths, extent):
    piece_ends = jnp.cumsum(lengths, axis=1)
    piece_starts = piece_ends - lengths
    places = jnp.arange(extent, dtype=jnp.int32)[None, :, None]
    inside = (places >= piece_starts[:, None, :]) & (places < piece_ends[:, None, :])
    pick = lambda table: jnp.sum(jnp.where(inside, table[:, None, :], 0), axis=2)
    filled = piece_ends[:, -1:]
    valid = places[..., 0] < filled
    start_of = jnp.where(valid, pick(piece_starts), filled)
    end_of = jnp.where(valid, pick(piece_ends), extent)
    width_of = jnp.where(valid, pick(widths), 1)
    within = places[..., 0] - start_of
    return within // width_of, within % width_of, valid, start_of, end_of


def by_block(table, size):
    rows, extent = table.shape
    return table.reshape(rows, extent // size, size).transpose(1, 0, 2).reshape(extent // size, rows * size)


def rotary_tables(row_pos, col_pos):
    quarter = HEAD_DIM // 4
    inverse = 10000.0 ** (-(2.0 * jnp.arange(quarter, dtype=jnp.float32)) / (HEAD_DIM // 2))
    angles = jnp.concatenate(
        [
            row_pos.astype(jnp.float32)[:, None, :] * inverse[None, :, None],
            col_pos.astype(jnp.float32)[:, None, :] * inverse[None, :, None],
        ],
        axis=1,
    )
    return (jnp.cos(angles), jnp.sin(angles))


def split_vector(vector, width, hidden_units):
    return (
        vector[:width],
        vector[width : 2 * width],
        vector[2 * width : 5 * width],
        vector[5 * width : 6 * width],
        vector[6 * width : 7 * width],
        vector[7 * width : 8 * width],
        vector[8 * width : 8 * width + hidden_units],
        vector[8 * width + hidden_units :],
    )


def standardize(inputs):
    center = inputs - jnp.mean(inputs, axis=-1, keepdims=True)
    root_inverse = lax.rsqrt(jnp.mean(center * center, axis=-1, keepdims=True) + eps_norm)
    return (center * root_inverse, root_inverse)


def norm_back(d_norm, gain_vector, scaled, root_inverse):
    effect = d_norm * gain_vector
    inner = jnp.mean(effect, axis=-1, keepdims=True)
    along = jnp.mean(effect * scaled, axis=-1, keepdims=True)
    return root_inverse * (effect - inner - scaled * along)


def adam_update(weight, moment, square, grad, factor, rate, decay):
    clipped = grad * factor
    moment = beta_one * moment + (1.0 - beta_one) * clipped
    square = beta_two * square + (1.0 - beta_two) * clipped * clipped
    fixed_moment = moment / (1.0 - beta_one**STEP)
    fixed_square = square / (1.0 - beta_two**STEP)
    weight = weight - rate * (fixed_moment / (jnp.sqrt(fixed_square) + adam_eps) + decay * weight)
    return (weight, moment, square)


def swap(value, axis, bit):
    count = lax.axis_size(axis)
    return lax.ppermute(value, axis, [(i, i ^ (1 << bit)) for i in range(count)])


def bit_of(axis, bit):
    return lax.rem(lax.axis_index(axis) // (1 << bit), 2)


def bits(axis):
    return range(lax.axis_size(axis).bit_length() - 1)


def owner_order(value, dim):
    count = lax.axis_size("fsdp")
    depth = value.shape[dim] // count
    order = sorted(range(count), key=lambda j: tuple(1 - (j >> b) % 2 for b in bits("fsdp")))
    me = lax.axis_index("fsdp")
    return jnp.concatenate(
        [lax.dynamic_slice_in_dim(value, (me ^ j) * depth, depth, dim) for j in order], axis=dim
    )


def add_up(parts):
    return functools.reduce(jnp.add, [part.astype(jnp.float32) for part in parts])


class Reduction:
    def __init__(self, left, right, form, dim):
        self.left, self.right, self.form, self.dim = left, right, form, dim
        self.total = left.shape[dim]
        self.stop = 0
        self.bit = 0
        self.taken = []

    def rows(self, start, stop):
        part = lax.slice_in_dim(self.left, start, stop, axis=self.dim)
        own = jnp.einsum(self.form, part, self.right, preferred_element_type=jnp.float32)
        return [own] + [
            lax.slice_in_dim(value, start - begin, stop - begin, axis=0) for begin, value in self.taken
        ]

    def leave(self):
        start, self.stop = self.stop, (self.stop + self.total) // 2
        sent = add_up(self.rows(start, self.stop)).astype(jnp.bfloat16)
        self.taken.append((self.stop, swap(sent, "fsdp", self.bit)))
        self.bit += 1
        if self.bit == len(bits("fsdp")):
            last = self.taken.pop()[1]
            self.parts = [add_up(self.rows(self.stop, self.total)).astype(jnp.bfloat16), last]
            self.bit = 0
        return sent

    def leave_ctx(self):
        half = self.parts[0].shape[0] // 2
        mine = bit_of("ctx", self.bit)
        pick = lambda side: [lax.dynamic_slice_in_dim(part, side * half, half, 0) for part in self.parts]
        sent = add_up(pick(1 - mine)).astype(jnp.bfloat16)
        self.parts = pick(mine) + [swap(sent, "ctx", self.bit)]
        self.bit += 1
        return sent

    def piece(self):
        while self.bit < len(bits("ctx")):
            self.leave_ctx()
        return add_up(self.parts).astype(jnp.bfloat16)


def gather_ctx(value):
    for bit in reversed(bits("ctx")):
        other = swap(value, "ctx", bit)
        value = jnp.where(
            bit_of("ctx", bit) == 0,
            jnp.concatenate([value, other], axis=0),
            jnp.concatenate([other, value], axis=0),
        )
    return value


def on_device(
    tokens,
    cotangent,
    lengths,
    widths,
    weight_qkv,
    moment_qkv,
    square_qkv,
    weight_out,
    moment_out,
    square_out,
    weight_up,
    moment_up,
    square_up,
    weight_down,
    moment_down,
    square_down,
    vectors,
    moment_vectors,
    square_vectors,
):
    full_qkv, full_out, full_up, full_down, full_vector = (
        lax.all_gather(weight_qkv.astype(jnp.bfloat16), "fsdp", axis=0, tiled=True),
        lax.all_gather(weight_out.astype(jnp.bfloat16), "fsdp", axis=0, tiled=True),
        lax.all_gather(weight_up.astype(jnp.bfloat16), "fsdp", axis=0, tiled=True),
        lax.all_gather(weight_down.astype(jnp.bfloat16), "fsdp", axis=0, tiled=True),
        lax.all_gather(vectors.astype(jnp.bfloat16), "fsdp", axis=0, tiled=True),
    )
    model_width = tokens.shape[2]
    hidden_units = full_up.shape[1]
    gain_one, shift_one, bias_qkv, bias_out, gain_two, shift_two, bias_up, bias_down = split_vector(
        full_vector.astype(jnp.float32), model_width, hidden_units
    )
    row_count = tokens.shape[0]
    slots_here = tokens.shape[1]
    slots_all = slots_here * lax.axis_size("ctx")
    token_count = row_count * slots_here
    ranks = lax.axis_size("ctx")
    here = lax.axis_index("ctx")
    local_heads = HEADS // ranks
    row_pos, col_pos, valid_slots, start_of, end_of = layout(lengths, widths, slots_all)
    valid_here = lax.dynamic_slice_in_dim(valid_slots, here * slots_here, slots_here, 1)
    cosine_table, sine_table = rotary_tables(by_block(row_pos, slots_here), by_block(col_pos, slots_here))
    cosine_here = lax.dynamic_index_in_dim(cosine_table, here, 0, keepdims=False)
    sine_here = lax.dynamic_index_in_dim(sine_table, here, 0, keepdims=False)
    low_high = jnp.stack([by_block(start_of, slots_here), by_block(end_of, slots_here)], axis=1)
    tile = slots_here * max(1, min(512 // slots_here, ranks))
    starts = start_of.reshape(row_count, slots_all // tile, tile)
    ends = end_of.reshape(row_count, slots_all // tile, tile)
    plain = (jnp.max(starts, axis=2) == 0) & (jnp.min(ends, axis=2) == slots_all)
    span = jnp.stack(
        [
            jnp.min(starts, axis=2) // tile,
            (jnp.max(ends, axis=2) + tile - 1) // tile,
            plain.astype(jnp.int32),
        ],
        axis=-1,
    ).astype(jnp.int32)
    flat_tokens = tokens.reshape(token_count, model_width).astype(jnp.float32)
    scaled_one, root_one = standardize(flat_tokens)
    first_normed = (scaled_one * gain_one + shift_one).astype(jnp.bfloat16)
    joined = (
        jnp.einsum("df,td->ft", full_qkv, first_normed, preferred_element_type=jnp.float32)
        + bias_qkv[:, None]
    )
    pairs = joined[: 2 * model_width].reshape(2, HEADS, 2, HEAD_DIM // 2, token_count)
    lower, upper_half = pairs[:, :, 0], pairs[:, :, 1]
    turned = jnp.stack(
        [lower * cosine_here - upper_half * sine_here, upper_half * cosine_here + lower * sine_here],
        axis=2,
    ).reshape(2 * model_width, token_count)
    heads_out = (
        jnp.concatenate([turned, joined[2 * model_width :]], axis=0)
        .astype(jnp.bfloat16)
        .reshape(3, ranks, local_heads, HEAD_DIM, token_count)
        .transpose(2, 1, 0, 3, 4)
    )
    heads_in = [exchange(heads_out[h]) for h in range(local_heads)]
    attended, lse, mixed = [], [], []
    for h in range(local_heads):
        result, stat = attend(span, heads_in[h], low_high)
        attended.append(result)
        lse.append(stat)
        mixed.append(exchange(result))
    mixed = jnp.stack(mixed, axis=1).reshape(model_width, token_count)
    hidden = flat_tokens + jnp.einsum("it,io->to", mixed, full_out, preferred_element_type=jnp.float32) + bias_out
    scaled_two, root_two = standardize(hidden)
    second_normed = (scaled_two * gain_two + shift_two).astype(jnp.bfloat16)
    upper = jnp.dot(second_normed, full_up, preferred_element_type=jnp.float32) + bias_up
    sigma = jax.nn.sigmoid(1.702 * upper)
    active = (upper * sigma).astype(jnp.bfloat16)
    result = hidden + jnp.dot(active, full_down, preferred_element_type=jnp.float32) + bias_down
    output = result.astype(jnp.bfloat16).reshape(tokens.shape)
    back_qkv, back_out, back_up, back_down = (
        lax.all_gather(weight_qkv.astype(jnp.bfloat16), "fsdp", axis=0, tiled=True),
        lax.all_gather(weight_out.astype(jnp.bfloat16), "fsdp", axis=0, tiled=True),
        lax.all_gather(weight_up.astype(jnp.bfloat16), "fsdp", axis=0, tiled=True),
        lax.all_gather(weight_down.astype(jnp.bfloat16), "fsdp", axis=0, tiled=True),
    )
    grad_result = cotangent.reshape(token_count, model_width).astype(
        jnp.float32
    ) * valid_here.reshape(token_count, 1).astype(jnp.float32)
    grad_low = grad_result.astype(jnp.bfloat16)
    d_bias_down = jnp.sum(grad_result, axis=0)
    others = range(1, len(bits("fsdp")))
    sum_down = Reduction(owner_order(active, 1), grad_low, "ti,to->io", 1)
    grad_low = after(grad_low, sum_down.leave())
    d_active = jnp.einsum("td,fd->tf", grad_low, back_down, preferred_element_type=jnp.float32)
    d_upper = (d_active * (sigma + 1.702 * upper * sigma * (1.0 - sigma))).astype(jnp.bfloat16)
    d_bias_up = jnp.sum(d_upper, axis=0, dtype=jnp.float32)
    sum_up = Reduction(owner_order(second_normed, 1), d_upper, "ti,to->io", 1)
    d_upper = after(d_upper, sum_up.leave(), *[sum_down.leave() for _ in others])
    d_second = jnp.einsum("tf,df->td", d_upper, back_up, preferred_element_type=jnp.float32)
    d_gain_two = jnp.sum(d_second * scaled_two, axis=0)
    d_shift_two = jnp.sum(d_second, axis=0)
    d_hidden = grad_result + norm_back(d_second, gain_two, scaled_two, root_two)
    d_branch = d_hidden.astype(jnp.bfloat16)
    d_bias_out = jnp.sum(d_branch, axis=0, dtype=jnp.float32)
    sum_out = Reduction(owner_order(mixed, 0), d_branch, "it,to->io", 0)
    d_branch = after(d_branch, sum_out.leave(), *[sum_up.leave() for _ in others])
    d_mixed = (
        jnp.einsum("to,io->it", d_branch, back_out, preferred_element_type=jnp.float32)
        .astype(jnp.bfloat16)
        .reshape(ranks, local_heads, HEAD_DIM, token_count)
    )
    d_heads = []
    for h in range(local_heads):
        d_attended = exchange(d_mixed[:, h])
        if h == 0:
            d_attended = after(d_attended, *[sum_out.leave() for _ in others])
        d_head = attend_back(
            span, heads_in[h], low_high, attended[h], d_attended, lse[h], cosine_table, sine_table
        )
        if h == local_heads - 1:
            d_head = after(d_head, sum_down.leave_ctx())
        d_heads.append(exchange(d_head))
    sum_qkv = []
    normed_owners = owner_order(first_normed, 1)
    for h in range(local_heads):
        if h > 0:
            d_heads[h] = after(d_heads[h], sum_qkv[-1].leave(), sum_down.leave_ctx())
        right = d_heads[h].reshape(3 * model_width // local_heads, token_count)
        sum_qkv.append(Reduction(normed_owners, right, "ti,ot->io", 1))
    last = sum_qkv[-1].leave()
    d_joined = (
        jnp.stack(d_heads, axis=1).transpose(2, 0, 1, 3, 4).reshape(3 * model_width, token_count)
    )
    d_joined = after(
        d_joined, last, sum_up.leave_ctx(), *[value.leave() for value in sum_qkv[:-1] for _ in others]
    )
    for _ in others:
        sum_qkv[-1].leave()
    d_bias_qkv = jnp.sum(d_joined, axis=1, dtype=jnp.float32)
    d_first = jnp.einsum("jt,dj->td", d_joined, back_qkv, preferred_element_type=jnp.float32)
    d_gain_one = jnp.sum(d_first * scaled_one, axis=0)
    d_shift_one = jnp.sum(d_first, axis=0)
    input_grad = (d_hidden + norm_back(d_first, gain_one, scaled_one, root_one)).reshape(
        tokens.shape
    )
    everywhere = ("fsdp", "ctx")
    early = lax.psum(
        jnp.concatenate([d_bias_out, d_gain_two, d_shift_two, d_bias_up, d_bias_down]), everywhere
    )
    late = lax.psum(
        jnp.concatenate([d_gain_one, d_shift_one, d_bias_qkv]).astype(jnp.bfloat16), everywhere
    )
    total_vectors = jnp.concatenate([late.astype(jnp.float32), early])
    piece_down, piece_up, piece_out = [value.piece() for value in (sum_down, sum_up, sum_out)]
    grad_down, grad_up, grad_outw = [
        gather_ctx(piece).astype(jnp.float32) for piece in (piece_down, piece_up, piece_out)
    ]
    piece_qkv = jnp.stack([value.piece() for value in sum_qkv], axis=1)
    depth = piece_qkv.shape[0]
    piece_qkv = (
        piece_qkv.reshape(depth, local_heads, ranks, 3, HEAD_DIM)
        .transpose(0, 3, 2, 1, 4)
        .reshape(depth, 3 * model_width)
    )
    squares = functools.reduce(
        jnp.add,
        [
            jnp.sum(jnp.square(piece.astype(jnp.float32)))
            for piece in (piece_qkv, piece_out, piece_up, piece_down)
        ],
    )
    total_squares = lax.psum(squares, everywhere) + jnp.sum(jnp.square(total_vectors))
    grad_vectors = lax.dynamic_slice_in_dim(
        total_vectors, lax.axis_index("fsdp") * vectors.shape[0], vectors.shape[0], 0
    )
    grad_qkv = gather_ctx(piece_qkv).astype(jnp.float32)
    grad_norm = jnp.sqrt(total_squares)
    factor = jnp.minimum(1.0, clip_level / grad_norm)
    new_qkv = adam_update(
        weight_qkv, moment_qkv, square_qkv, grad_qkv, factor, rate_matrix, decay_matrix
    )
    new_out = adam_update(
        weight_out, moment_out, square_out, grad_outw, factor, rate_matrix, decay_matrix
    )
    new_up = adam_update(
        weight_up, moment_up, square_up, grad_up, factor, rate_matrix, decay_matrix
    )
    new_down = adam_update(
        weight_down, moment_down, square_down, grad_down, factor, rate_matrix, decay_matrix
    )
    new_vec = adam_update(
        vectors, moment_vectors, square_vectors, grad_vectors, factor, rate_vector, 0.0
    )
    return (
        output,
        input_grad,
        grad_norm,
        new_qkv[0],
        new_qkv[1],
        new_qkv[2],
        new_out[0],
        new_out[1],
        new_out[2],
        new_up[0],
        new_up[1],
        new_up[2],
        new_down[0],
        new_down[1],
        new_down[2],
        new_vec[0],
        new_vec[1],
        new_vec[2],
    )


def solution(mesh):
    placed = (
        P("fsdp", "ctx", None),
        P("fsdp", "ctx", None),
        P("fsdp", None),
        P("fsdp", None),
        P("fsdp", None),
        P("fsdp", None),
        P("fsdp", None),
        P("fsdp", None),
        P("fsdp", None),
        P("fsdp", None),
        P("fsdp", None),
        P("fsdp", None),
        P("fsdp", None),
        P("fsdp", None),
        P("fsdp", None),
        P("fsdp", None),
        P("fsdp"),
        P("fsdp"),
        P("fsdp"),
    )
    return jax.shard_map(
        on_device,
        mesh=mesh,
        in_specs=placed,
        out_specs=(
            P("fsdp", "ctx", None),
            P("fsdp", "ctx", None),
            P(),
            P("fsdp", None),
            P("fsdp", None),
            P("fsdp", None),
            P("fsdp", None),
            P("fsdp", None),
            P("fsdp", None),
            P("fsdp", None),
            P("fsdp", None),
            P("fsdp", None),
            P("fsdp", None),
            P("fsdp", None),
            P("fsdp", None),
            P("fsdp"),
            P("fsdp"),
            P("fsdp"),
        ),
        check_vma=False,
    )
```

```python
import functools

import jax
import jax.numpy as jnp
from jax import lax
from jax.experimental import pallas as pl
from jax.experimental.pallas import tpu as pltpu
from jax.sharding import PartitionSpec as P

HEADS = 16
HEAD_DIM = 80
STEP = 5


eps_norm = 1e-06
beta_one = 0.9
beta_two = 0.999
adam_eps = 1e-08
decay_matrix = 0.05
rate_matrix = 0.04
rate_vector = 0.3
clip_level = 1.0


LOG2E = 1.4426950408889634


def exchange(source):
    return lax.all_to_all(source, "ctx", 0, 0)


def after(value, *others):
    return lax.optimization_barrier((value,) + others)[0]


def attend_kernel(span, qkv, low_high, out, stat, keys, values, *, size, tile, extent, step_size):
    row, place = pl.program_id(0), pl.program_id(1)
    blocks = extent // size
    group = tile // size
    scale = HEAD_DIM ** (-0.5) * LOG2E

    @pl.when(place == 0)
    def _():
        for b in range(blocks):
            keys[b * size:(b + 1) * size, :] = qkv[b, 1].T
            values[:, b * size:(b + 1) * size] = qkv[b, 2]

    first, last, plain = span[row, place, 0], span[row, place, 1], span[row, place, 2]
    query = jnp.concatenate([qkv[place * group + i, 0] for i in range(group)], axis=1)

    def finish(peak, total, mixed):
        mixed = (mixed / total).astype(jnp.bfloat16)
        lse = peak + jnp.log2(total)
        for i in range(group):
            out[i] = mixed[:, i * size:(i + 1) * size]
            stat[i] = lse[:, i * size:(i + 1) * size]

    def step(start, carry, keep=None):
        peak, total, mixed = carry
        s = jnp.dot(keys[pl.ds(start, step_size), :], query, preferred_element_type=jnp.float32) * scale
        if keep is not None:
            s = jnp.where(keep, s, -1e30)
        top = jnp.maximum(peak, jnp.max(s, axis=0, keepdims=True))
        fade = jnp.exp2(peak - top)
        raised = jnp.exp2(s - top)
        total = total * fade + jnp.sum(raised, axis=0, keepdims=True)
        mixed = mixed * fade + jnp.dot(values[:, pl.ds(start, step_size)], raised.astype(jnp.bfloat16),
                                       preferred_element_type=jnp.float32)
        return top, total, mixed

    begin = (
        jnp.full((1, tile), -1e30, jnp.float32),
        jnp.zeros((1, tile), jnp.float32),
        jnp.zeros((HEAD_DIM, tile), jnp.float32),
    )

    @pl.when(plain == 1)
    def _():
        carry = begin
        for b in range(extent // step_size):
            carry = step(b * step_size, carry)
        finish(*carry)

    @pl.when(plain == 0)
    def _():
        low = jnp.concatenate([low_high[i, 0:1, :] for i in range(group)], axis=1)
        high = jnp.concatenate([low_high[i, 1:2, :] for i in range(group)], axis=1)

        def masked(b, carry):
            start = pl.multiple_of(b * step_size, step_size)
            places = lax.broadcasted_iota(jnp.int32, (step_size, tile), 0) + start
            return step(start, carry, (places >= low) & (places < high))

        finish(*lax.fori_loop(first, last, masked, begin))


def attend(span, qkv, low_high):
    blocks, _, width, lanes = qkv.shape
    rows = span.shape[0]
    size = lanes // rows
    group = blocks // span.shape[1]
    tile = group * size
    grid_spec = pltpu.PrefetchScalarGridSpec(
        num_scalar_prefetch=1,
        grid=(rows, blocks // group),
        in_specs=[
            pl.BlockSpec((blocks, 3, width, size), lambda r, b, s: (0, 0, 0, r)),
            pl.BlockSpec((group, 2, size), lambda r, b, s: (b, 0, r)),
        ],
        out_specs=[
            pl.BlockSpec((group, width, size), lambda r, b, s: (b, 0, r)),
            pl.BlockSpec((group, 1, size), lambda r, b, s: (b, 0, r)),
        ],
        scratch_shapes=[pltpu.VMEM((blocks * size, HEAD_DIM), jnp.bfloat16), pltpu.VMEM((HEAD_DIM, blocks * size), jnp.bfloat16)],
    )
    return pl.pallas_call(
        functools.partial(attend_kernel, size=size, tile=tile, extent=blocks * size, step_size=tile),
        grid_spec=grid_spec,
        out_shape=[
            jax.ShapeDtypeStruct((blocks, width, lanes), jnp.bfloat16),
            jax.ShapeDtypeStruct((blocks, 1, lanes), jnp.float32),
        ],
        cost_estimate=pl.CostEstimate(
            flops=4 * rows * (blocks * size) ** 2 * 256,
            bytes_accessed=5 * blocks * width * lanes * 2,
            transcendentals=rows * (blocks * size) ** 2,
        ),
        compiler_params=pltpu.CompilerParams(vmem_limit_bytes=48 * 1024 * 1024),
        name="attend",
    )(span, qkv, low_high)


def attend_back_kernel(span, qkv, low_high, mixed, d_mixed, stat, cosine, sine, out, keys, values, keys_t, d_keys, d_values,
                       *, size, tile, extent, step_size):
    row, place = pl.program_id(0), pl.program_id(1)
    blocks = extent // size
    group = tile // size
    scale = HEAD_DIM ** (-0.5)
    half = HEAD_DIM // 2

    @pl.when(place == 0)
    def _():
        d_keys[...] = jnp.zeros_like(d_keys)
        d_values[...] = jnp.zeros_like(d_values)
        for b in range(blocks):
            keys[b * size:(b + 1) * size, :] = qkv[b, 1].T
            values[b * size:(b + 1) * size, :] = qkv[b, 2].T
            keys_t[:, b * size:(b + 1) * size] = qkv[b, 1]

    def turn_back(v, cos, sin):
        upper, lower = v[half:], v[:half]
        return jnp.concatenate([lower * cos + upper * sin, upper * cos - lower * sin], axis=0)

    side = lambda parts: jnp.concatenate(parts, axis=1)
    first, last, plain = span[row, place, 0], span[row, place, 1], span[row, place, 2]
    query = side([qkv[place * group + i, 0] for i in range(group)])
    grad = side([d_mixed[i] for i in range(group)])
    query_n, grad_n = query.T, grad.T
    delta = jnp.sum(grad.astype(jnp.float32) * side([mixed[i] for i in range(group)]).astype(jnp.float32), axis=0, keepdims=True)
    lse = side([stat[i] for i in range(group)])

    def step(start, d_query, keep=None):
        here = pl.ds(start, step_size)
        s = jnp.dot(keys[here, :], query, preferred_element_type=jnp.float32)
        d_probs = jnp.dot(values[here, :], grad, preferred_element_type=jnp.float32)
        exact = jnp.exp2(s * (scale * LOG2E) - lse)
        if keep is not None:
            exact = jnp.where(keep, exact, 0.0)
        d_scores = (exact * (d_probs - delta)).astype(jnp.bfloat16)
        d_values[here, :] += jnp.dot(exact.astype(jnp.bfloat16), grad_n, preferred_element_type=jnp.float32)
        d_keys[here, :] += jnp.dot(d_scores, query_n, preferred_element_type=jnp.float32)
        return d_query + jnp.dot(keys_t[:, here], d_scores, preferred_element_type=jnp.float32)

    def finish(d_query):
        for i in range(group):
            b = place * group + i
            out[b, 0] = turn_back(d_query[:, i * size:(i + 1) * size] * scale, cosine[b], sine[b]).astype(jnp.bfloat16)

    begin = jnp.zeros((HEAD_DIM, tile), jnp.float32)

    @pl.when(plain == 1)
    def _():
        d_query = begin
        for b in range(extent // step_size):
            d_query = step(b * step_size, d_query)
        finish(d_query)

    @pl.when(plain == 0)
    def _():
        low = side([low_high[i, 0:1, :] for i in range(group)])
        high = side([low_high[i, 1:2, :] for i in range(group)])

        def masked(b, d_query):
            start = pl.multiple_of(b * step_size, step_size)
            places = lax.broadcasted_iota(jnp.int32, (step_size, tile), 0) + start
            return step(start, d_query, (places >= low) & (places < high))

        finish(lax.fori_loop(first, last, masked, begin))

    @pl.when(place == blocks // group - 1)
    def _():
        for b in range(blocks):
            here = slice(b * size, (b + 1) * size)
            out[b, 1] = turn_back(d_keys[here, :].T * scale, cosine[b], sine[b]).astype(jnp.bfloat16)
            out[b, 2] = d_values[here, :].T.astype(jnp.bfloat16)


def attend_back(span, qkv, low_high, mixed, d_mixed, stat, cosine, sine):
    blocks, _, width, lanes = qkv.shape
    rows = span.shape[0]
    size = lanes // rows
    group = blocks // span.shape[1]
    tile = group * size
    per = lambda r, b, s: (b, 0, r)
    whole = lambda r, b, s: (0, 0, r)
    grid_spec = pltpu.PrefetchScalarGridSpec(
        num_scalar_prefetch=1,
        grid=(rows, blocks // group),
        in_specs=[
            pl.BlockSpec((blocks, 3, width, size), lambda r, b, s: (0, 0, 0, r)),
            pl.BlockSpec((group, 2, size), per),
            pl.BlockSpec((group, width, size), per),
            pl.BlockSpec((group, width, size), per),
            pl.BlockSpec((group, 1, size), per),
            pl.BlockSpec((blocks, HEAD_DIM // 2, size), whole),
            pl.BlockSpec((blocks, HEAD_DIM // 2, size), whole),
        ],
        out_specs=pl.BlockSpec((blocks, 3, width, size), lambda r, b, s: (0, 0, 0, r)),
        scratch_shapes=[
            pltpu.VMEM((blocks * size, HEAD_DIM), jnp.bfloat16),
            pltpu.VMEM((blocks * size, HEAD_DIM), jnp.bfloat16),
            pltpu.VMEM((HEAD_DIM, blocks * size), jnp.bfloat16),
            pltpu.VMEM((blocks * size, HEAD_DIM), jnp.float32),
            pltpu.VMEM((blocks * size, HEAD_DIM), jnp.float32),
        ],
    )
    return pl.pallas_call(
        functools.partial(attend_back_kernel, size=size, tile=tile, extent=blocks * size, step_size=tile),
        grid_spec=grid_spec,
        out_shape=jax.ShapeDtypeStruct(qkv.shape, jnp.bfloat16),
        cost_estimate=pl.CostEstimate(
            flops=10 * rows * (blocks * size) ** 2 * 256,
            bytes_accessed=10 * blocks * width * lanes * 2,
            transcendentals=rows * (blocks * size) ** 2,
        ),
        compiler_params=pltpu.CompilerParams(vmem_limit_bytes=56 * 1024 * 1024),
        name="attend_back",
    )(span, qkv, low_high, mixed, d_mixed, stat, cosine, sine)


def layout(lengths, widths, extent):
    piece_ends = jnp.cumsum(lengths, axis=1)
    piece_starts = piece_ends - lengths
    places = jnp.arange(extent, dtype=jnp.int32)[None, :, None]
    inside = (places >= piece_starts[:, None, :]) & (places < piece_ends[:, None, :])
    pick = lambda table: jnp.sum(jnp.where(inside, table[:, None, :], 0), axis=2)
    filled = piece_ends[:, -1:]
    valid = places[..., 0] < filled
    start_of = jnp.where(valid, pick(piece_starts), filled)
    end_of = jnp.where(valid, pick(piece_ends), extent)
    width_of = jnp.where(valid, pick(widths), 1)
    within = places[..., 0] - start_of
    return within // width_of, within % width_of, valid, start_of, end_of


def by_block(table, size):
    rows, extent = table.shape
    return table.reshape(rows, extent // size, size).transpose(1, 0, 2).reshape(extent // size, rows * size)


def rotary_tables(row_pos, col_pos):
    quarter = HEAD_DIM // 4
    inverse = 10000.0 ** (-(2.0 * jnp.arange(quarter, dtype=jnp.float32)) / (HEAD_DIM // 2))
    angles = jnp.concatenate(
        [
            row_pos.astype(jnp.float32)[:, None, :] * inverse[None, :, None],
            col_pos.astype(jnp.float32)[:, None, :] * inverse[None, :, None],
        ],
        axis=1,
    )
    return (jnp.cos(angles), jnp.sin(angles))


def split_vector(vector, width, hidden_units):
    return (
        vector[:width],
        vector[width : 2 * width],
        vector[2 * width : 5 * width],
        vector[5 * width : 6 * width],
        vector[6 * width : 7 * width],
        vector[7 * width : 8 * width],
        vector[8 * width : 8 * width + hidden_units],
        vector[8 * width + hidden_units :],
    )


def standardize(inputs):
    center = inputs - jnp.mean(inputs, axis=-1, keepdims=True)
    root_inverse = lax.rsqrt(jnp.mean(center * center, axis=-1, keepdims=True) + eps_norm)
    return (center * root_inverse, root_inverse)


def norm_back(d_norm, gain_vector, scaled, root_inverse):
    effect = d_norm * gain_vector
    inner = jnp.mean(effect, axis=-1, keepdims=True)
    along = jnp.mean(effect * scaled, axis=-1, keepdims=True)
    return root_inverse * (effect - inner - scaled * along)


def adam_update(weight, moment, square, grad, factor, rate, decay):
    clipped = grad * factor
    moment = beta_one * moment + (1.0 - beta_one) * clipped
    square = beta_two * square + (1.0 - beta_two) * clipped * clipped
    fixed_moment = moment / (1.0 - beta_one**STEP)
    fixed_square = square / (1.0 - beta_two**STEP)
    weight = weight - rate * (fixed_moment / (jnp.sqrt(fixed_square) + adam_eps) + decay * weight)
    return (weight, moment, square)


def swap(value, axis, bit):
    count = lax.axis_size(axis)
    return lax.ppermute(value, axis, [(i, i ^ (1 << bit)) for i in range(count)])


def bit_of(axis, bit):
    return lax.rem(lax.axis_index(axis) // (1 << bit), 2)


def bits(axis):
    return range(lax.axis_size(axis).bit_length() - 1)


def owner_order(value, dim):
    count = lax.axis_size("fsdp")
    depth = value.shape[dim] // count
    order = sorted(range(count), key=lambda j: tuple(1 - (j >> b) % 2 for b in bits("fsdp")))
    me = lax.axis_index("fsdp")
    return jnp.concatenate(
        [lax.dynamic_slice_in_dim(value, (me ^ j) * depth, depth, dim) for j in order], axis=dim
    )


def add_up(parts):
    return functools.reduce(jnp.add, [part.astype(jnp.float32) for part in parts])


class Reduction:
    def __init__(self, left, right, form, dim):
        self.left, self.right, self.form, self.dim = left, right, form, dim
        self.total = left.shape[dim]
        self.rows = self.total // lax.axis_size("fsdp")
        self.columns = right.shape[0 if form[3] == "o" else 1]
        self.splits = splits_of(self.rows, self.columns)
        self.stop = self.bit = self.begun = 0
        self.taken = []

    def product(self, start, stop, left=None):
        part = lax.slice_in_dim(self.left if left is None else left, start, stop, axis=self.dim)
        return jnp.einsum(self.form, part, self.right, preferred_element_type=jnp.float32)

    def came(self, start, stop):
        return [lax.slice_in_dim(value, start - begin, stop - begin, axis=0) for begin, value in self.taken]

    def leave(self, *others):
        if self.taken and others:
            self.taken[-1] = (self.taken[-1][0], after(self.taken[-1][1], *others))
        start, self.stop = self.stop, (self.stop + self.total) // 2
        sent = add_up([self.product(start, self.stop)] + self.came(start, self.stop)).astype(jnp.bfloat16)
        self.taken.append((self.stop, swap(sent, "fsdp", self.bit)))
        self.bit += 1
        return sent

    def own(self, *others):
        while self.bit < len(bits("fsdp")):
            self.leave()
        last = self.taken.pop()[1]
        left = after(self.left, *others) if others else self.left
        own = [self.product(self.stop, self.total, left)] + self.came(self.stop, self.total)
        self.parts = [add_up(own).astype(jnp.bfloat16), last]
        return self.parts[0]

    def leave_ctx(self, *others):
        if others:
            self.parts[-1] = after(self.parts[-1], *others)
        dim = self.splits[self.begun]
        half = self.parts[0].shape[dim] // 2
        mine = bit_of("ctx", self.begun)
        pick = lambda side: [lax.dynamic_slice_in_dim(part, side * half, half, dim) for part in self.parts]
        sent = add_up(pick(1 - mine)).astype(jnp.bfloat16)
        own = add_up(pick(mine)).astype(jnp.bfloat16)
        self.parts = [own, swap(sent, "ctx", self.begun)]
        self.begun += 1
        return sent

    def state(self):
        return self.parts


class Joined:
    def __init__(self, sums, blocks):
        width = sums[0].columns // blocks
        self.parts = [
            jnp.concatenate(
                [value.parts[i][:, b * width : (b + 1) * width] for b in range(blocks) for value in sums], axis=1
            )
            for i in range(2)
        ]
        self.rows, self.columns = self.parts[0].shape
        self.splits = splits_of(self.rows, self.columns)
        self.begun = 0

    def state(self):
        return self.parts


def splits_of(rows, columns):
    dims = []
    for _ in bits("ctx"):
        if rows % 32 == 0:
            rows //= 2
            dims.append(0)
        elif columns % 256 == 0:
            columns //= 2
            dims.append(1)
        else:
            return None
    return dims


def plan(units, count):
    links, done, ready = {}, [], []
    for unit, (rows, columns, begun, spared) in enumerate(units):
        phases = [
            (min(bit, 1), rows * columns / 2 ** (bit + 1) * 2 ** max(bit - 1, 0)) for bit in range(count)
        ]
        ready.append((0.0, unit, begun, phases + phases[::-1][: count - spared]))
    while ready:
        ready.sort(key=lambda item: (max(item[0], links.get(item[3][item[2]][0], 0.0)), item[1]))
        time, unit, phase, phases = ready.pop(0)
        link, length = phases[phase]
        end = max(time, links.get(link, 0.0)) + length
        links[link] = end
        done.append((end, unit, phase))
        if phase + 1 < len(phases):
            ready.append((end, unit, phase + 1, phases))
    return [(unit, phase) for _, unit, phase in sorted(done)]


def settle_kernel(*refs, units, splits, count):
    number = len(units)
    sources, small, targets, total = (
        refs[:2 * number], refs[2 * number], refs[2 * number + 1:3 * number + 1], refs[3 * number + 1]
    )
    scratch = list(refs[3 * number + 2:])
    take = lambda wanted: [scratch.pop(0) for _ in range(wanted)]
    group, place = lax.axis_index("fsdp"), lax.axis_index("ctx")
    group_bit = [lax.rem(group // 2**b, 2) for b in bits("fsdp")]
    place_bit = [lax.rem(place // 2**b, 2) for b in range(count)]
    partner = {("ctx", b): (group, place + (1 - 2 * place_bit[b]) * 2**b) for b in range(count)}
    partner.update({("fsdp", b): (group + (1 - 2 * bit) * 2**b, place) for b, bit in enumerate(group_bit)})

    barrier = pltpu.get_barrier_semaphore()
    for other in partner.values():
        pl.semaphore_signal(barrier, inc=1, device_id=other, device_id_type=pl.DeviceIdType.MESH)
    pl.semaphore_wait(barrier, len(partner))

    local_sem, send_sem, recv_sem, squares, from_others = take(5)
    sent, local = [], [0]

    def send(link, source, target):
        copy = pltpu.make_async_remote_copy(
            src_ref=source,
            dst_ref=target,
            send_sem=send_sem.at[len(sent)],
            recv_sem=recv_sem.at[len(sent)],
            device_id=partner[link],
            device_id_type=pl.DeviceIdType.MESH,
        )
        copy.start()
        sent.append(copy)
        return copy

    def move(source, target):
        copy = pltpu.make_async_copy(source, target, local_sem.at[local[0]])
        local[0] += 1
        copy.start()
        return copy

    def part(ref, row, rows, column, columns):
        if columns == ref.shape[1]:
            return ref.at[pl.ds(pl.multiple_of(row, 16), rows)]
        return ref.at[pl.ds(pl.multiple_of(row, 16), rows), pl.ds(pl.multiple_of(column, 128), columns)]

    def add(left, right, target, measure=False):
        def body(i, held):
            here = pl.ds(pl.multiple_of(i * 16, 16), 16)
            value = (left[here, :].astype(jnp.float32) + right[here, :].astype(jnp.float32)).astype(jnp.bfloat16)
            target[here, :] = value
            if measure:
                value = value.astype(jnp.float32)
                for tile in range(value.shape[1] // 128):
                    piece = value[:, tile * 128:(tile + 1) * 128]
                    held = held + piece * piece
            return held

        held = lax.fori_loop(0, left.shape[0] // 16, body, jnp.zeros((16, 128), jnp.float32))
        if measure:
            squares[0, 0:16] = squares[0, 0:16] + held

    class Unit:
        pass

    states = []
    for index, (rows, columns, begun, spared) in enumerate(units):
        unit = Unit()
        unit.begun, unit.target, unit.dims = begun, targets[index], splits[index]
        unit.spared = spared
        unit.region = [(0, rows, 0, columns)]
        for bit in range(count):
            row, depth, column, width = unit.region[-1]
            if unit.dims[bit] == 0:
                depth //= 2
                row = row + place_bit[bit] * depth
            else:
                width //= 2
                column = column + place_bit[bit] * width
            unit.region.append((row, depth, column, width))
        unit.final, unit.held, unit.came = take(3)
        unit.taken = [None] * begun + take(count - begun)
        unit.loads = [move(sources[2 * index], unit.held), move(sources[2 * index + 1], unit.came)]
        states.append(unit)

    def halves(unit, ref, bit):
        depth, width = ref.shape
        if unit.dims[bit] == 0:
            depth //= 2
            pick = lambda side: part(ref, side * depth, depth, 0, width)
        else:
            width //= 2
            pick = lambda side: part(ref, 0, depth, side * width, width)
        return pick(place_bit[bit]), pick(1 - place_bit[bit])

    def proceed(unit, bit, ref):
        unit.kept, leaving = halves(unit, ref, bit)
        unit.copy = send(("ctx", bit), leaving, unit.taken[bit])

    def hand_out(unit, bit):
        region = part(unit.final, *unit.region[bit + 1])
        unit.copy = send(("ctx", bit), region, region)

    left = [number]

    def settled(unit, own, came):
        add(own, came, part(unit.final, *unit.region[count]), measure=True)
        left[0] -= 1
        hand_out(unit, count - 1)

    def advance(unit, phase):
        unit.copy.wait_recv()
        if phase < count - 1:
            add(unit.kept, unit.taken[phase], unit.taken[phase])
            proceed(unit, phase + 1, unit.taken[phase])
        elif phase == count - 1:
            settled(unit, unit.kept, unit.taken[phase])
        elif phase < 2 * count - 1 - unit.spared:
            hand_out(unit, 2 * count - 2 - phase)
        else:
            unit.store = move(part(unit.final, *unit.region[unit.spared]), unit.target)

    squared, squares_copy = [-1], [None]

    def exchange_squares():
        step = squared[0] = squared[0] + 1
        if step > 0:
            squares_copy[0].wait_recv()
            squares[step] = squares[step - 1] + from_others[step - 1]
        if step < len(partner):
            squares_copy[0] = send(list(partner)[step], squares.at[step], from_others.at[step])

    squares[0, 0:16] = jnp.zeros((16, 128), jnp.float32)
    squares[0, 16:] = small[...]
    for unit in states:
        for load in unit.loads:
            load.wait()
        if unit.begun < count:
            add(unit.held, unit.came, unit.held)
            proceed(unit, unit.begun, unit.held)
        else:
            settled(unit, unit.held, unit.came)
    for index, phase in plan(units, count):
        advance(states[index], phase)
        if left[0] == 0 and squared[0] < len(partner):
            exchange_squares()
    while squared[0] < len(partner):
        exchange_squares()
    total[...] = squares[len(partner)]
    for copy in sent:
        copy.wait_send()
    for unit in states:
        unit.store.wait()


def settle(sums, spared, vector, number):
    count, links = len(bits("ctx")), len(bits("ctx")) + len(bits("fsdp"))
    units = [(value.rows, value.columns, value.begun, less) for value, less in zip(sums, spared)]
    tall = -(-vector.shape[0] // 1024) * 8
    small = jnp.pad(vector, (0, tall * 128 - vector.shape[0])).reshape(tall, 128)
    low = jnp.bfloat16
    scratch, sends, sources = [], links, []
    for value in sums:
        own, came = value.state()
        sources += [own, came]
        scratch += [pltpu.VMEM((value.rows, value.columns), low)] + 2 * [pltpu.VMEM(own.shape, low)]
        depth, width = own.shape
        for dim in value.splits[value.begun:]:
            depth, width = (depth // 2, width) if dim == 0 else (depth, width // 2)
            scratch.append(pltpu.VMEM((depth, width), low))
        sends += 2 * count - value.begun
    scratch = [
        pltpu.SemaphoreType.DMA((3 * len(units),)),
        pltpu.SemaphoreType.DMA((sends,)),
        pltpu.SemaphoreType.DMA((sends,)),
        pltpu.VMEM((links + 1, 16 + tall, 128), jnp.float32),
        pltpu.VMEM((links, 16 + tall, 128), jnp.float32),
    ] + scratch
    shapes = []
    for value, less in zip(sums, spared):
        rows, columns = value.rows, value.columns
        for dim in value.splits[:less]:
            rows, columns = (rows // 2, columns) if dim == 0 else (rows, columns // 2)
        shapes.append(jax.ShapeDtypeStruct((rows, columns), low))
    *results, total = pl.pallas_call(
        functools.partial(
            settle_kernel, units=units, splits=[value.splits for value in sums], count=count
        ),
        out_shape=shapes + [jax.ShapeDtypeStruct((16 + tall, 128), jnp.float32)],
        in_specs=[pl.BlockSpec(memory_space=pl.ANY) for _ in sources]
        + [pl.BlockSpec(memory_space=pltpu.VMEM)],
        out_specs=[pl.BlockSpec(memory_space=pl.ANY) for _ in units]
        + [pl.BlockSpec(memory_space=pltpu.VMEM)],
        scratch_shapes=scratch,
        cost_estimate=pl.CostEstimate(
            flops=0, bytes_accessed=64 * sum(unit[0] * unit[1] * 2 for unit in units), transcendentals=0
        ),
        compiler_params=pltpu.CompilerParams(
            collective_id=number, has_side_effects=True, vmem_limit_bytes=56 * 1024 * 1024
        ),
        name="settle",
    )(*sources, small)
    for index, (value, less) in enumerate(zip(sums, spared)):
        for bit in reversed(range(less)):
            other, dim = swap(results[index], "ctx", bit), value.splits[bit]
            results[index] = jnp.where(
                bit_of("ctx", bit) == 0,
                jnp.concatenate([results[index], other], axis=dim),
                jnp.concatenate([other, results[index]], axis=dim),
            )
    return results, jnp.sum(total[:16]), total[16:].reshape(-1)[: vector.shape[0]]


def on_device(
    tokens,
    cotangent,
    lengths,
    widths,
    weight_qkv,
    moment_qkv,
    square_qkv,
    weight_out,
    moment_out,
    square_out,
    weight_up,
    moment_up,
    square_up,
    weight_down,
    moment_down,
    square_down,
    vectors,
    moment_vectors,
    square_vectors,
):
    full_qkv, full_out, full_up, full_down, full_vector = (
        lax.all_gather(weight_qkv.astype(jnp.bfloat16), "fsdp", axis=0, tiled=True),
        lax.all_gather(weight_out.astype(jnp.bfloat16), "fsdp", axis=0, tiled=True),
        lax.all_gather(weight_up.astype(jnp.bfloat16), "fsdp", axis=0, tiled=True),
        lax.all_gather(weight_down.astype(jnp.bfloat16), "fsdp", axis=0, tiled=True),
        lax.all_gather(vectors.astype(jnp.bfloat16), "fsdp", axis=0, tiled=True),
    )
    model_width = tokens.shape[2]
    hidden_units = full_up.shape[1]
    gain_one, shift_one, bias_qkv, bias_out, gain_two, shift_two, bias_up, bias_down = split_vector(
        full_vector.astype(jnp.float32), model_width, hidden_units
    )
    row_count = tokens.shape[0]
    slots_here = tokens.shape[1]
    slots_all = slots_here * lax.axis_size("ctx")
    token_count = row_count * slots_here
    ranks = lax.axis_size("ctx")
    here = lax.axis_index("ctx")
    local_heads = HEADS // ranks
    row_pos, col_pos, valid_slots, start_of, end_of = layout(lengths, widths, slots_all)
    valid_here = lax.dynamic_slice_in_dim(valid_slots, here * slots_here, slots_here, 1)
    cosine_table, sine_table = rotary_tables(by_block(row_pos, slots_here), by_block(col_pos, slots_here))
    cosine_here = lax.dynamic_index_in_dim(cosine_table, here, 0, keepdims=False)
    sine_here = lax.dynamic_index_in_dim(sine_table, here, 0, keepdims=False)
    low_high = jnp.stack([by_block(start_of, slots_here), by_block(end_of, slots_here)], axis=1)
    tile = slots_here * max(1, min(512 // slots_here, ranks))
    starts = start_of.reshape(row_count, slots_all // tile, tile)
    ends = end_of.reshape(row_count, slots_all // tile, tile)
    plain = (jnp.max(starts, axis=2) == 0) & (jnp.min(ends, axis=2) == slots_all)
    span = jnp.stack(
        [
            jnp.min(starts, axis=2) // tile,
            (jnp.max(ends, axis=2) + tile - 1) // tile,
            plain.astype(jnp.int32),
        ],
        axis=-1,
    ).astype(jnp.int32)
    flat_tokens = tokens.reshape(token_count, model_width).astype(jnp.float32)
    scaled_one, root_one = standardize(flat_tokens)
    first_normed = (scaled_one * gain_one + shift_one).astype(jnp.bfloat16)
    joined = (
        jnp.einsum("df,td->ft", full_qkv, first_normed, preferred_element_type=jnp.float32)
        + bias_qkv[:, None]
    )
    pairs = joined[: 2 * model_width].reshape(2, HEADS, 2, HEAD_DIM // 2, token_count)
    lower, upper_half = pairs[:, :, 0], pairs[:, :, 1]
    turned = jnp.stack(
        [lower * cosine_here - upper_half * sine_here, upper_half * cosine_here + lower * sine_here],
        axis=2,
    ).reshape(2 * model_width, token_count)
    heads_out = (
        jnp.concatenate([turned, joined[2 * model_width :]], axis=0)
        .astype(jnp.bfloat16)
        .reshape(3, local_heads, ranks, HEAD_DIM, token_count)
        .transpose(1, 2, 0, 3, 4)
    )
    heads_in = [exchange(heads_out[h]) for h in range(local_heads)]
    attended, lse, mixed = [], [], []
    for h in range(local_heads):
        result, stat = attend(span, heads_in[h], low_high)
        attended.append(result)
        lse.append(stat)
        mixed.append(exchange(result))
    mixed = jnp.stack(mixed, axis=0).reshape(model_width, token_count)
    hidden = flat_tokens + jnp.einsum("it,io->to", mixed, full_out, preferred_element_type=jnp.float32) + bias_out
    scaled_two, root_two = standardize(hidden)
    second_normed = (scaled_two * gain_two + shift_two).astype(jnp.bfloat16)
    upper = jnp.dot(second_normed, full_up, preferred_element_type=jnp.float32) + bias_up
    sigma = jax.nn.sigmoid(1.702 * upper)
    active = (upper * sigma).astype(jnp.bfloat16)
    result = hidden + jnp.dot(active, full_down, preferred_element_type=jnp.float32) + bias_down
    output = result.astype(jnp.bfloat16).reshape(tokens.shape)
    back_qkv, back_out, back_up, back_down = (
        lax.all_gather(weight_qkv.astype(jnp.bfloat16), "fsdp", axis=0, tiled=True),
        lax.all_gather(weight_out.astype(jnp.bfloat16), "fsdp", axis=0, tiled=True),
        lax.all_gather(weight_up.astype(jnp.bfloat16), "fsdp", axis=0, tiled=True),
        lax.all_gather(weight_down.astype(jnp.bfloat16), "fsdp", axis=0, tiled=True),
    )
    grad_result = cotangent.reshape(token_count, model_width).astype(
        jnp.float32
    ) * valid_here.reshape(token_count, 1).astype(jnp.float32)
    grad_low = grad_result.astype(jnp.bfloat16)
    d_bias_down = jnp.sum(grad_result, axis=0)
    steps = range(1, len(bits("fsdp")))
    sum_down = Reduction(owner_order(active, 1), grad_low, "ti,to->io", 1)
    grad_low = after(grad_low, sum_down.leave())
    d_active = jnp.einsum("td,fd->tf", grad_low, back_down, preferred_element_type=jnp.float32)
    d_upper = (d_active * (sigma + 1.702 * upper * sigma * (1.0 - sigma))).astype(jnp.bfloat16)
    d_bias_up = jnp.sum(d_upper, axis=0, dtype=jnp.float32)
    d_upper = after(d_upper, *[sum_down.leave(d_upper) for _ in steps])
    sum_up = Reduction(owner_order(second_normed, 1), d_upper, "ti,to->io", 1)
    d_upper = after(d_upper, sum_up.leave())
    d_second = jnp.einsum("tf,df->td", d_upper, back_up, preferred_element_type=jnp.float32)
    d_second = after(d_second, *[sum_up.leave(d_second) for _ in steps])
    d_gain_two = jnp.sum(d_second * scaled_two, axis=0)
    d_shift_two = jnp.sum(d_second, axis=0)
    d_hidden = grad_result + norm_back(d_second, gain_two, scaled_two, root_two)
    d_branch = d_hidden.astype(jnp.bfloat16)
    d_bias_out = jnp.sum(d_branch, axis=0, dtype=jnp.float32)
    sum_out = Reduction(owner_order(mixed, 0), d_branch, "it,to->io", 0)
    d_branch = after(d_branch, sum_out.leave())
    d_mixed = (
        jnp.einsum("to,io->it", d_branch, back_out, preferred_element_type=jnp.float32)
        .astype(jnp.bfloat16)
        .reshape(local_heads, ranks, HEAD_DIM, token_count)
    )
    split = all(
        splits_of(value.shape[0], value.shape[1]) for value in (weight_qkv, weight_out, weight_up, weight_down)
    )
    d_attended = [exchange(d_mixed[h]) for h in range(local_heads)]
    busy = [sum_down.own(d_mixed), sum_up.own(d_mixed)] + [sum_out.leave(d_mixed) for _ in steps]
    d_attended[0] = after(d_attended[0], *busy)
    normed_owners = owner_order(first_normed, 1)
    d_heads, sum_qkv = [], []
    for h in range(local_heads):
        d_heads.append(
            attend_back(
                span, heads_in[h], low_high, attended[h], d_attended[h], lse[h], cosine_table, sine_table
            )
        )
        if h == 0 and split:
            sent = sum_down.leave_ctx(d_heads[0])
            if local_heads > 1:
                d_attended[1] = after(d_attended[1], sent)
    for h in range(local_heads):
        came = exchange(d_heads[h])
        if h > 0:
            sent = [sum_qkv[-1].leave()]
            if split:
                sent.append(sum_down.leave_ctx(*sent))
                sent.append(sum_up.leave_ctx(*sent))
            sent += [sum_qkv[-1].leave(*sent) for _ in steps]
            came = after(came, *sent)
        d_heads[h] = came.transpose(1, 0, 2, 3)
        right = d_heads[h].reshape(3 * ranks * HEAD_DIM, token_count)
        sum_qkv.append(Reduction(normed_owners, right, "ti,ot->io", 1))
    last = sum_qkv[-1].leave()
    d_joined = jnp.stack(d_heads, axis=1).reshape(3 * model_width, token_count)
    d_joined = after(d_joined, last)
    d_bias_qkv = jnp.sum(d_joined, axis=1, dtype=jnp.float32)
    d_first = jnp.einsum("jt,dj->td", d_joined, back_qkv, preferred_element_type=jnp.float32)
    d_first = after(d_first, *[sum_qkv[-1].leave(d_first) for _ in steps])
    d_gain_one = jnp.sum(d_first * scaled_one, axis=0)
    d_shift_one = jnp.sum(d_first, axis=0)
    input_grad = (d_hidden + norm_back(d_first, gain_one, scaled_one, root_one)).reshape(
        tokens.shape
    )
    everywhere = ("fsdp", "ctx")
    d_vectors = jnp.concatenate(
        [
            d_gain_one,
            d_shift_one,
            d_bias_qkv,
            d_bias_out,
            d_gain_two,
            d_shift_two,
            d_bias_up,
            d_bias_down,
        ]
    )
    for value in sum_qkv + [sum_out]:
        value.own()
    sum_qkv = Joined(sum_qkv, 3)
    if split:
        (grad_down, grad_up, grad_qkv, grad_outw), total_squares, total_vectors = settle(
            [sum_down, sum_up, sum_qkv, sum_out], [0, 0, 1, 1], d_vectors, 0
        )
    else:
        grad_down, grad_up, grad_qkv, grad_outw = [
            lax.psum(add_up(value.parts).astype(jnp.bfloat16), "ctx")
            for value in (sum_down, sum_up, sum_qkv, sum_out)
        ]
        total_squares = lax.psum(
            functools.reduce(
                jnp.add,
                [
                    jnp.sum(jnp.square(grad.astype(jnp.float32)))
                    for grad in (grad_down, grad_up, grad_outw, grad_qkv)
                ],
            ),
            "fsdp",
        )
        total_vectors = lax.psum(d_vectors, everywhere)
    total_squares = total_squares + jnp.sum(jnp.square(total_vectors))
    grad_vectors = lax.dynamic_slice_in_dim(
        total_vectors, lax.axis_index("fsdp") * vectors.shape[0], vectors.shape[0], 0
    )
    grad_down, grad_up, grad_outw, grad_qkv = [
        grad.astype(jnp.float32) for grad in (grad_down, grad_up, grad_outw, grad_qkv)
    ]
    grad_norm = jnp.sqrt(total_squares)
    factor = jnp.minimum(1.0, clip_level / grad_norm)
    new_qkv = adam_update(
        weight_qkv, moment_qkv, square_qkv, grad_qkv, factor, rate_matrix, decay_matrix
    )
    new_out = adam_update(
        weight_out, moment_out, square_out, grad_outw, factor, rate_matrix, decay_matrix
    )
    new_up = adam_update(
        weight_up, moment_up, square_up, grad_up, factor, rate_matrix, decay_matrix
    )
    new_down = adam_update(
        weight_down, moment_down, square_down, grad_down, factor, rate_matrix, decay_matrix
    )
    new_vec = adam_update(
        vectors, moment_vectors, square_vectors, grad_vectors, factor, rate_vector, 0.0
    )
    return (
        output,
        input_grad,
        grad_norm,
        new_qkv[0],
        new_qkv[1],
        new_qkv[2],
        new_out[0],
        new_out[1],
        new_out[2],
        new_up[0],
        new_up[1],
        new_up[2],
        new_down[0],
        new_down[1],
        new_down[2],
        new_vec[0],
        new_vec[1],
        new_vec[2],
    )


def solution(mesh):
    placed = (
        P("fsdp", "ctx", None),
        P("fsdp", "ctx", None),
        P("fsdp", None),
        P("fsdp", None),
        P("fsdp", None),
        P("fsdp", None),
        P("fsdp", None),
        P("fsdp", None),
        P("fsdp", None),
        P("fsdp", None),
        P("fsdp", None),
        P("fsdp", None),
        P("fsdp", None),
        P("fsdp", None),
        P("fsdp", None),
        P("fsdp", None),
        P("fsdp"),
        P("fsdp"),
        P("fsdp"),
    )
    return jax.shard_map(
        on_device,
        mesh=mesh,
        in_specs=placed,
        out_specs=(
            P("fsdp", "ctx", None),
            P("fsdp", "ctx", None),
            P(),
            P("fsdp", None),
            P("fsdp", None),
            P("fsdp", None),
            P("fsdp", None),
            P("fsdp", None),
            P("fsdp", None),
            P("fsdp", None),
            P("fsdp", None),
            P("fsdp", None),
            P("fsdp", None),
            P("fsdp", None),
            P("fsdp", None),
            P("fsdp"),
            P("fsdp"),
            P("fsdp"),
        ),
        check_vma=False,
    )
```

```python
import functools

import jax
import jax.numpy as jnp
from jax import lax
from jax.experimental import pallas as pl
from jax.experimental.pallas import tpu as pltpu
from jax.sharding import PartitionSpec as P

HEADS = 16
HEAD_DIM = 80
STEP = 5


eps_norm = 1e-06
beta_one = 0.9
beta_two = 0.999
adam_eps = 1e-08
decay_matrix = 0.05
rate_matrix = 0.04
rate_vector = 0.3
clip_level = 1.0


LOG2E = 1.4426950408889634


EVERYWHERE = ("fsdp", "ctx")


def device(pair, core, top, low):
    half = lax.axis_size("ctx") // 2
    return ((pair * 2 + core) * 2 + top) * half + low


def trade(value, kept):
    pairs = []
    for pair in range(lax.axis_size("fsdp") // 2):
        for low in range(lax.axis_size("ctx") // 2):
            one, other = device(pair, 1, 0, low), device(pair, 0, 1, low)
            pairs += [(one, other), (other, one)]
    return jnp.where(kept, value, lax.ppermute(value, EVERYWHERE, pairs))


def exchange(source):
    groups = [
        [device(pair, core, top, low) for core in range(2) for low in range(lax.axis_size("ctx") // 2)]
        for pair in range(lax.axis_size("fsdp") // 2)
        for top in range(2)
    ]
    return lax.all_to_all(source, EVERYWHERE, 0, 0, axis_index_groups=groups)


def after(value, *others):
    return lax.optimization_barrier((value,) + others)[0]


def attend_kernel(span, qkv, low_high, out, stat, keys, values, *, size, tile, extent, step_size):
    row, place = pl.program_id(0), pl.program_id(1)
    blocks = extent // size
    group = tile // size
    scale = HEAD_DIM ** (-0.5) * LOG2E

    @pl.when(place == 0)
    def _():
        for b in range(blocks):
            keys[b * size:(b + 1) * size, :] = qkv[b, 1].T
            values[:, b * size:(b + 1) * size] = qkv[b, 2]

    first, last, plain = span[row, place, 0], span[row, place, 1], span[row, place, 2]
    query = jnp.concatenate([qkv[place * group + i, 0] for i in range(group)], axis=1)

    def finish(peak, total, mixed):
        mixed = (mixed / total).astype(jnp.bfloat16)
        lse = peak + jnp.log2(total)
        for i in range(group):
            out[i] = mixed[:, i * size:(i + 1) * size]
            stat[i] = lse[:, i * size:(i + 1) * size]

    def step(start, carry, keep=None):
        peak, total, mixed = carry
        s = jnp.dot(keys[pl.ds(start, step_size), :], query, preferred_element_type=jnp.float32) * scale
        if keep is not None:
            s = jnp.where(keep, s, -1e30)
        top = jnp.maximum(peak, jnp.max(s, axis=0, keepdims=True))
        fade = jnp.exp2(peak - top)
        raised = jnp.exp2(s - top)
        total = total * fade + jnp.sum(raised, axis=0, keepdims=True)
        mixed = mixed * fade + jnp.dot(values[:, pl.ds(start, step_size)], raised.astype(jnp.bfloat16),
                                       preferred_element_type=jnp.float32)
        return top, total, mixed

    begin = (
        jnp.full((1, tile), -1e30, jnp.float32),
        jnp.zeros((1, tile), jnp.float32),
        jnp.zeros((HEAD_DIM, tile), jnp.float32),
    )

    @pl.when(plain == 1)
    def _():
        carry = begin
        for b in range(extent // step_size):
            carry = step(b * step_size, carry)
        finish(*carry)

    @pl.when(plain == 0)
    def _():
        low = jnp.concatenate([low_high[i, 0:1, :] for i in range(group)], axis=1)
        high = jnp.concatenate([low_high[i, 1:2, :] for i in range(group)], axis=1)

        def masked(b, carry):
            start = pl.multiple_of(b * step_size, step_size)
            places = lax.broadcasted_iota(jnp.int32, (step_size, tile), 0) + start
            return step(start, carry, (places >= low) & (places < high))

        finish(*lax.fori_loop(first, last, masked, begin))


def attend(span, qkv, low_high):
    blocks, _, width, lanes = qkv.shape
    rows = span.shape[0]
    size = lanes // rows
    group = blocks // span.shape[1]
    tile = group * size
    grid_spec = pltpu.PrefetchScalarGridSpec(
        num_scalar_prefetch=1,
        grid=(rows, blocks // group),
        in_specs=[
            pl.BlockSpec((blocks, 3, width, size), lambda r, b, s: (0, 0, 0, r)),
            pl.BlockSpec((group, 2, size), lambda r, b, s: (b, 0, r)),
        ],
        out_specs=[
            pl.BlockSpec((group, width, size), lambda r, b, s: (b, 0, r)),
            pl.BlockSpec((group, 1, size), lambda r, b, s: (b, 0, r)),
        ],
        scratch_shapes=[pltpu.VMEM((blocks * size, HEAD_DIM), jnp.bfloat16), pltpu.VMEM((HEAD_DIM, blocks * size), jnp.bfloat16)],
    )
    return pl.pallas_call(
        functools.partial(attend_kernel, size=size, tile=tile, extent=blocks * size, step_size=tile),
        grid_spec=grid_spec,
        out_shape=[
            jax.ShapeDtypeStruct((blocks, width, lanes), jnp.bfloat16),
            jax.ShapeDtypeStruct((blocks, 1, lanes), jnp.float32),
        ],
        compiler_params=pltpu.CompilerParams(vmem_limit_bytes=48 * 1024 * 1024),
        name="attend",
    )(span, qkv, low_high)


def attend_back_kernel(span, qkv, low_high, mixed, d_mixed, stat, cosine, sine, out, keys, values, keys_t, d_keys, d_values,
                       *, size, tile, extent, step_size):
    row, place = pl.program_id(0), pl.program_id(1)
    blocks = extent // size
    group = tile // size
    scale = HEAD_DIM ** (-0.5)
    half = HEAD_DIM // 2

    @pl.when(place == 0)
    def _():
        d_keys[...] = jnp.zeros_like(d_keys)
        d_values[...] = jnp.zeros_like(d_values)
        for b in range(blocks):
            keys[b * size:(b + 1) * size, :] = qkv[b, 1].T
            values[b * size:(b + 1) * size, :] = qkv[b, 2].T
            keys_t[:, b * size:(b + 1) * size] = qkv[b, 1]

    def turn_back(v, cos, sin):
        upper, lower = v[half:], v[:half]
        return jnp.concatenate([lower * cos + upper * sin, upper * cos - lower * sin], axis=0)

    side = lambda parts: jnp.concatenate(parts, axis=1)
    first, last, plain = span[row, place, 0], span[row, place, 1], span[row, place, 2]
    query = side([qkv[place * group + i, 0] for i in range(group)])
    grad = side([d_mixed[i] for i in range(group)])
    query_n, grad_n = query.T, grad.T
    delta = jnp.sum(grad.astype(jnp.float32) * side([mixed[i] for i in range(group)]).astype(jnp.float32), axis=0, keepdims=True)
    lse = side([stat[i] for i in range(group)])

    def step(start, d_query, keep=None):
        here = pl.ds(start, step_size)
        s = jnp.dot(keys[here, :], query, preferred_element_type=jnp.float32)
        d_probs = jnp.dot(values[here, :], grad, preferred_element_type=jnp.float32)
        exact = jnp.exp2(s * (scale * LOG2E) - lse)
        if keep is not None:
            exact = jnp.where(keep, exact, 0.0)
        d_scores = (exact * (d_probs - delta)).astype(jnp.bfloat16)
        d_values[here, :] += jnp.dot(exact.astype(jnp.bfloat16), grad_n, preferred_element_type=jnp.float32)
        d_keys[here, :] += jnp.dot(d_scores, query_n, preferred_element_type=jnp.float32)
        return d_query + jnp.dot(keys_t[:, here], d_scores, preferred_element_type=jnp.float32)

    def finish(d_query):
        for i in range(group):
            b = place * group + i
            out[b, 0] = turn_back(d_query[:, i * size:(i + 1) * size] * scale, cosine[b], sine[b]).astype(jnp.bfloat16)

    begin = jnp.zeros((HEAD_DIM, tile), jnp.float32)

    @pl.when(plain == 1)
    def _():
        d_query = begin
        for b in range(extent // step_size):
            d_query = step(b * step_size, d_query)
        finish(d_query)

    @pl.when(plain == 0)
    def _():
        low = side([low_high[i, 0:1, :] for i in range(group)])
        high = side([low_high[i, 1:2, :] for i in range(group)])

        def masked(b, d_query):
            start = pl.multiple_of(b * step_size, step_size)
            places = lax.broadcasted_iota(jnp.int32, (step_size, tile), 0) + start
            return step(start, d_query, (places >= low) & (places < high))

        finish(lax.fori_loop(first, last, masked, begin))

    @pl.when(place == blocks // group - 1)
    def _():
        for b in range(blocks):
            here = slice(b * size, (b + 1) * size)
            out[b, 1] = turn_back(d_keys[here, :].T * scale, cosine[b], sine[b]).astype(jnp.bfloat16)
            out[b, 2] = d_values[here, :].T.astype(jnp.bfloat16)


def attend_back(span, qkv, low_high, mixed, d_mixed, stat, cosine, sine):
    blocks, _, width, lanes = qkv.shape
    rows = span.shape[0]
    size = lanes // rows
    group = blocks // span.shape[1]
    tile = group * size
    per = lambda r, b, s: (b, 0, r)
    whole = lambda r, b, s: (0, 0, r)
    grid_spec = pltpu.PrefetchScalarGridSpec(
        num_scalar_prefetch=1,
        grid=(rows, blocks // group),
        in_specs=[
            pl.BlockSpec((blocks, 3, width, size), lambda r, b, s: (0, 0, 0, r)),
            pl.BlockSpec((group, 2, size), per),
            pl.BlockSpec((group, width, size), per),
            pl.BlockSpec((group, width, size), per),
            pl.BlockSpec((group, 1, size), per),
            pl.BlockSpec((blocks, HEAD_DIM // 2, size), whole),
            pl.BlockSpec((blocks, HEAD_DIM // 2, size), whole),
        ],
        out_specs=pl.BlockSpec((blocks, 3, width, size), lambda r, b, s: (0, 0, 0, r)),
        scratch_shapes=[
            pltpu.VMEM((blocks * size, HEAD_DIM), jnp.bfloat16),
            pltpu.VMEM((blocks * size, HEAD_DIM), jnp.bfloat16),
            pltpu.VMEM((HEAD_DIM, blocks * size), jnp.bfloat16),
            pltpu.VMEM((blocks * size, HEAD_DIM), jnp.float32),
            pltpu.VMEM((blocks * size, HEAD_DIM), jnp.float32),
        ],
    )
    return pl.pallas_call(
        functools.partial(attend_back_kernel, size=size, tile=tile, extent=blocks * size, step_size=tile),
        grid_spec=grid_spec,
        out_shape=jax.ShapeDtypeStruct(qkv.shape, jnp.bfloat16),
        compiler_params=pltpu.CompilerParams(vmem_limit_bytes=56 * 1024 * 1024),
        name="attend_back",
    )(span, qkv, low_high, mixed, d_mixed, stat, cosine, sine)


def layout(lengths, widths, extent):
    piece_ends = jnp.cumsum(lengths, axis=1)
    piece_starts = piece_ends - lengths
    places = jnp.arange(extent, dtype=jnp.int32)[None, :, None]
    inside = (places >= piece_starts[:, None, :]) & (places < piece_ends[:, None, :])
    pick = lambda table: jnp.sum(jnp.where(inside, table[:, None, :], 0), axis=2)
    filled = piece_ends[:, -1:]
    valid = places[..., 0] < filled
    start_of = jnp.where(valid, pick(piece_starts), filled)
    end_of = jnp.where(valid, pick(piece_ends), extent)
    width_of = jnp.where(valid, pick(widths), 1)
    within = places[..., 0] - start_of
    return within // width_of, within % width_of, valid, start_of, end_of


def by_block(table, size):
    rows, extent = table.shape
    return table.reshape(rows, extent // size, size).transpose(1, 0, 2).reshape(extent // size, rows * size)


def rotary_tables(row_pos, col_pos):
    quarter = HEAD_DIM // 4
    inverse = 10000.0 ** (-(2.0 * jnp.arange(quarter, dtype=jnp.float32)) / (HEAD_DIM // 2))
    angles = jnp.concatenate(
        [
            row_pos.astype(jnp.float32)[:, None, :] * inverse[None, :, None],
            col_pos.astype(jnp.float32)[:, None, :] * inverse[None, :, None],
        ],
        axis=1,
    )
    return (jnp.cos(angles), jnp.sin(angles))


def split_vector(vector, width, hidden_units):
    return (
        vector[:width],
        vector[width : 2 * width],
        vector[2 * width : 5 * width],
        vector[5 * width : 6 * width],
        vector[6 * width : 7 * width],
        vector[7 * width : 8 * width],
        vector[8 * width : 8 * width + hidden_units],
        vector[8 * width + hidden_units :],
    )


def standardize(inputs):
    center = inputs - jnp.mean(inputs, axis=-1, keepdims=True)
    root_inverse = lax.rsqrt(jnp.mean(center * center, axis=-1, keepdims=True) + eps_norm)
    return (center * root_inverse, root_inverse)


def norm_back(d_norm, gain_vector, scaled, root_inverse):
    effect = d_norm * gain_vector
    inner = jnp.mean(effect, axis=-1, keepdims=True)
    along = jnp.mean(effect * scaled, axis=-1, keepdims=True)
    return root_inverse * (effect - inner - scaled * along)


def adam_update(weight, moment, square, grad, factor, rate, decay):
    clipped = grad * factor
    moment = beta_one * moment + (1.0 - beta_one) * clipped
    square = beta_two * square + (1.0 - beta_two) * clipped * clipped
    fixed_moment = moment / (1.0 - beta_one**STEP)
    fixed_square = square / (1.0 - beta_two**STEP)
    weight = weight - rate * (fixed_moment / (jnp.sqrt(fixed_square) + adam_eps) + decay * weight)
    return (weight, moment, square)


def swap(value, axis, bit):
    count = lax.axis_size(axis)
    return lax.ppermute(value, axis, [(i, i ^ (1 << bit)) for i in range(count)])


def bit_of(axis, bit):
    return lax.rem(lax.axis_index(axis) // (1 << bit), 2)


def bits(axis):
    return range(lax.axis_size(axis).bit_length() - 1)


def owner_order(value, dim):
    count = lax.axis_size("fsdp")
    depth = value.shape[dim] // count
    core = bit_of("fsdp", 0)
    return jnp.concatenate(
        [
            lax.dynamic_slice_in_dim(value, (2 * pair + side) * depth, depth, dim)
            for side in (1 - core, core)
            for pair in range(count // 2)
        ],
        axis=dim,
    )


def add_up(parts):
    return functools.reduce(jnp.add, [part.astype(jnp.float32) for part in parts])


class Reduction:
    def __init__(self, left, right, form, dim):
        self.left, self.right, self.form, self.dim = left, right, form, dim
        self.total = left.shape[dim]
        self.rows = self.total // lax.axis_size("fsdp")
        self.columns = right.shape[0 if form[3] == "o" else 1]
        self.splits = splits_of(self.rows, self.columns)
        self.begun = 0

    def product(self, start, stop, *others):
        left = after(self.left, *others) if others else self.left
        return jnp.einsum(
            self.form,
            lax.slice_in_dim(left, start, stop, axis=self.dim),
            self.right,
            preferred_element_type=jnp.float32,
        )

    def leave(self):
        sent = self.product(0, self.total // 2).astype(jnp.bfloat16)
        self.came = swap(sent, "fsdp", 0)
        return sent

    def cross(self, *others):
        came = after(self.came, *others) if others else self.came
        kept = add_up([self.product(self.total // 2, self.total, *others), came]).astype(jnp.bfloat16)
        pairs, places = lax.axis_size("fsdp") // 2, lax.axis_size("ctx")
        wide = self.splits is not None and self.splits[0] == 0
        step = 2 if wide else 1
        groups = [
            [(2 * pair + core) * places + place + bit for pair in range(pairs) for bit in range(step)]
            for core in range(2)
            for place in range(0, places, step)
        ]
        self.parts = [
            lax.psum_scatter(kept, EVERYWHERE, scatter_dimension=0, tiled=True, axis_index_groups=groups)
        ]
        self.begun = step - 1
        return kept

    def cross_pair(self, *others):
        if lax.axis_size("fsdp") != 4:
            return self.cross(*others)
        came = after(self.came, *others) if others else self.came
        mine = bit_of("fsdp", 1) * self.rows
        theirs = self.rows - mine
        pick = lambda start: add_up(
            [
                jnp.einsum(
                    self.form,
                    lax.dynamic_slice_in_dim(self.left, self.total // 2 + start, self.rows, self.dim),
                    self.right,
                    preferred_element_type=jnp.float32,
                ),
                lax.dynamic_slice_in_dim(came, start, self.rows, 0),
            ]
        ).astype(jnp.bfloat16)
        sent = pick(theirs)
        self.parts = [pick(mine), swap(sent, "fsdp", 1)]
        return sent

    def leave_ctx(self, *others):
        if others:
            self.parts[-1] = after(self.parts[-1], *others)
        dim = self.splits[self.begun]
        half = self.parts[0].shape[dim] // 2
        mine = bit_of("ctx", self.begun)
        pick = lambda side: [lax.dynamic_slice_in_dim(part, side * half, half, dim) for part in self.parts]
        sent = add_up(pick(1 - mine)).astype(jnp.bfloat16)
        own = add_up(pick(mine)).astype(jnp.bfloat16)
        self.parts = [own, swap(sent, "ctx", self.begun)]
        self.begun += 1
        return sent

    def state(self):
        return self.parts


class Joined:
    def __init__(self, sums, blocks):
        width = sums[0].columns // blocks
        self.parts = [
            jnp.concatenate(
                [value.parts[i][:, b * width : (b + 1) * width] for b in range(blocks) for value in sums], axis=1
            )
            for i in range(len(sums[0].parts))
        ]
        self.rows, self.columns = sums[0].rows, sums[0].columns * len(sums)
        self.splits = splits_of(self.rows, self.columns)
        self.begun = sums[0].begun

    def state(self):
        return self.parts


def splits_of(rows, columns):
    dims = []
    for _ in bits("ctx"):
        if rows % 32 == 0:
            rows //= 2
            dims.append(0)
        elif columns % 256 == 0:
            columns //= 2
            dims.append(1)
        else:
            return None
    return dims


def plan(units, count):
    links, done, ready = {}, [], []
    for unit, (rows, columns, begun, spared) in enumerate(units):
        phases = [
            (bit, rows * columns / 2 ** (bit + 1) * 2 ** max(bit - 1, 0) + 20000) for bit in range(count)
        ]
        ready.append((0.0, unit, begun, phases + phases[::-1][: count - spared]))
    while ready:
        ready.sort(key=lambda item: (max(item[0], links.get(item[3][item[2]][0], 0.0)), item[1]))
        time, unit, phase, phases = ready.pop(0)
        link, length = phases[phase]
        end = max(time, links.get(link, 0.0)) + length
        links[link] = end
        done.append((end, unit, phase))
        if phase + 1 < len(phases):
            ready.append((end, unit, phase + 1, phases))
    return [(unit, phase) for _, unit, phase in sorted(done)]


def settle_kernel(*refs, units, splits, given, count):
    number = len(units)
    arrays = sum(given)
    sources, small, targets, total = (
        list(refs[:arrays]), refs[arrays], refs[arrays + 1:arrays + 1 + number], refs[arrays + 1 + number]
    )
    scratch = list(refs[arrays + 2 + number:])
    take = lambda wanted: [scratch.pop(0) for _ in range(wanted)]
    group, place = lax.axis_index("fsdp"), lax.axis_index("ctx")
    group_bit = [lax.rem(group // 2**b, 2) for b in bits("fsdp")]
    place_bit = [lax.rem(place // 2**b, 2) for b in range(count)]
    partner = {("ctx", b): (group, place + (1 - 2 * place_bit[b]) * 2**b) for b in range(count)}
    partner.update({("fsdp", b): (group + (1 - 2 * bit) * 2**b, place) for b, bit in enumerate(group_bit)})

    barrier = pltpu.get_barrier_semaphore()
    for other in partner.values():
        pl.semaphore_signal(barrier, inc=1, device_id=other, device_id_type=pl.DeviceIdType.MESH)
    pl.semaphore_wait(barrier, len(partner))

    local_sem, send_sem, recv_sem, squares, from_others = take(5)
    sent, local = [], [0]

    def send(link, source, target):
        copy = pltpu.make_async_remote_copy(
            src_ref=source,
            dst_ref=target,
            send_sem=send_sem.at[len(sent)],
            recv_sem=recv_sem.at[len(sent)],
            device_id=partner[link],
            device_id_type=pl.DeviceIdType.MESH,
        )
        copy.start()
        sent.append(copy)
        return copy

    def move(source, target):
        copy = pltpu.make_async_copy(source, target, local_sem.at[local[0]])
        local[0] += 1
        copy.start()
        return copy

    def part(ref, row, rows, column, columns):
        if columns == ref.shape[1]:
            return ref.at[pl.ds(pl.multiple_of(row, 16), rows)]
        return ref.at[pl.ds(pl.multiple_of(row, 16), rows), pl.ds(pl.multiple_of(column, 128), columns)]

    def add(left, right, target, measure=False):
        def body(i, held):
            here = pl.ds(pl.multiple_of(i * 16, 16), 16)
            value = left[here, :]
            if right is not None:
                value = (value.astype(jnp.float32) + right[here, :].astype(jnp.float32)).astype(jnp.bfloat16)
            target[here, :] = value
            if measure:
                value = value.astype(jnp.float32)
                for tile in range(value.shape[1] // 128):
                    piece = value[:, tile * 128:(tile + 1) * 128]
                    held = held + piece * piece
            return held

        held = lax.fori_loop(0, left.shape[0] // 16, body, jnp.zeros((16, 128), jnp.float32))
        if measure:
            squares[0, 0:16] = squares[0, 0:16] + held

    class Unit:
        pass

    states = []
    for index, (rows, columns, begun, spared) in enumerate(units):
        unit = Unit()
        unit.begun, unit.target, unit.dims = begun, targets[index], splits[index]
        unit.spared = spared
        unit.region = [(0, rows, 0, columns)]
        for bit in range(count):
            row, depth, column, width = unit.region[-1]
            if unit.dims[bit] == 0:
                depth //= 2
                row = row + place_bit[bit] * depth
            else:
                width //= 2
                column = column + place_bit[bit] * width
            unit.region.append((row, depth, column, width))
        unit.final, unit.held = take(2)
        unit.came = take(1)[0] if given[index] == 2 else None
        unit.taken = [None] * begun + take(count - begun)
        unit.loads = [move(sources.pop(0), unit.held)]
        if unit.came is not None:
            unit.loads.append(move(sources.pop(0), unit.came))
        states.append(unit)

    def halves(unit, ref, bit):
        depth, width = ref.shape
        if unit.dims[bit] == 0:
            depth //= 2
            pick = lambda side: part(ref, side * depth, depth, 0, width)
        else:
            width //= 2
            pick = lambda side: part(ref, 0, depth, side * width, width)
        return pick(place_bit[bit]), pick(1 - place_bit[bit])

    def proceed(unit, bit, ref):
        unit.kept, leaving = halves(unit, ref, bit)
        unit.copy = send(("ctx", bit), leaving, unit.taken[bit])

    def hand_out(unit, bit):
        region = part(unit.final, *unit.region[bit + 1])
        unit.copy = send(("ctx", bit), region, region)

    left = [number]

    def settled(unit, own, came):
        add(own, came, part(unit.final, *unit.region[count]), measure=True)
        left[0] -= 1
        hand_out(unit, count - 1)

    def advance(unit, phase):
        unit.copy.wait_recv()
        if phase < count - 1:
            add(unit.kept, unit.taken[phase], unit.taken[phase])
            proceed(unit, phase + 1, unit.taken[phase])
        elif phase == count - 1:
            settled(unit, unit.kept, unit.taken[phase])
        elif phase < 2 * count - 1 - unit.spared:
            hand_out(unit, 2 * count - 2 - phase)
        else:
            unit.store = move(part(unit.final, *unit.region[unit.spared]), unit.target)

    squared, squares_copy = [-1], [None]

    def exchange_squares():
        step = squared[0] = squared[0] + 1
        if step > 0:
            squares_copy[0].wait_recv()
            squares[step] = squares[step - 1] + from_others[step - 1]
        if step < len(partner):
            squares_copy[0] = send(list(partner)[step], squares.at[step], from_others.at[step])

    squares[0, 0:16] = jnp.zeros((16, 128), jnp.float32)
    squares[0, 16:] = small[...]
    for unit in states:
        for load in unit.loads:
            load.wait()
        if unit.begun < count:
            if unit.came is not None:
                add(unit.held, unit.came, unit.held)
            proceed(unit, unit.begun, unit.held)
        else:
            settled(unit, unit.held, unit.came)
    for index, phase in plan(units, count):
        advance(states[index], phase)
        if left[0] == 0 and squared[0] < len(partner):
            exchange_squares()
    while squared[0] < len(partner):
        exchange_squares()
    total[...] = squares[len(partner)]
    for copy in sent:
        copy.wait_send()
    for unit in states:
        unit.store.wait()


def settle(sums, spared, vector, number):
    count, links = len(bits("ctx")), len(bits("ctx")) + len(bits("fsdp"))
    units = [(value.rows, value.columns, value.begun, less) for value, less in zip(sums, spared)]
    tall = -(-vector.shape[0] // 1024) * 8
    small = jnp.pad(vector, (0, tall * 128 - vector.shape[0])).reshape(tall, 128)
    low = jnp.bfloat16
    scratch, sends, sources = [], links, []
    for value in sums:
        state = value.state()
        sources += state
        scratch.append(pltpu.VMEM((value.rows, value.columns), low))
        scratch += len(state) * [pltpu.VMEM(state[0].shape, low)]
        depth, width = state[0].shape
        for dim in value.splits[value.begun:]:
            depth, width = (depth // 2, width) if dim == 0 else (depth, width // 2)
            scratch.append(pltpu.VMEM((depth, width), low))
        sends += 2 * count - value.begun
    scratch = [
        pltpu.SemaphoreType.DMA((3 * len(units),)),
        pltpu.SemaphoreType.DMA((sends,)),
        pltpu.SemaphoreType.DMA((sends,)),
        pltpu.VMEM((links + 1, 16 + tall, 128), jnp.float32),
        pltpu.VMEM((links, 16 + tall, 128), jnp.float32),
    ] + scratch
    shapes = []
    for value, less in zip(sums, spared):
        rows, columns = value.rows, value.columns
        for dim in value.splits[:less]:
            rows, columns = (rows // 2, columns) if dim == 0 else (rows, columns // 2)
        shapes.append(jax.ShapeDtypeStruct((rows, columns), low))
    *results, total = pl.pallas_call(
        functools.partial(
            settle_kernel,
            units=units,
            splits=[value.splits for value in sums],
            given=[len(value.state()) for value in sums],
            count=count,
        ),
        out_shape=shapes + [jax.ShapeDtypeStruct((16 + tall, 128), jnp.float32)],
        in_specs=[pl.BlockSpec(memory_space=pl.ANY) for _ in sources]
        + [pl.BlockSpec(memory_space=pltpu.VMEM)],
        out_specs=[pl.BlockSpec(memory_space=pl.ANY) for _ in units]
        + [pl.BlockSpec(memory_space=pltpu.VMEM)],
        scratch_shapes=scratch,
        cost_estimate=pl.CostEstimate(
            flops=0, bytes_accessed=64 * sum(unit[0] * unit[1] * 2 for unit in units), transcendentals=0
        ),
        compiler_params=pltpu.CompilerParams(
            collective_id=number, has_side_effects=True, vmem_limit_bytes=56 * 1024 * 1024
        ),
        name="settle",
    )(*sources, small)
    for index, (value, less) in enumerate(zip(sums, spared)):
        for bit in reversed(range(less)):
            other, dim = swap(results[index], "ctx", bit), value.splits[bit]
            results[index] = jnp.where(
                bit_of("ctx", bit) == 0,
                jnp.concatenate([results[index], other], axis=dim),
                jnp.concatenate([other, results[index]], axis=dim),
            )
    return results, jnp.sum(total[:16]), total[16:].reshape(-1)[: vector.shape[0]]


def gather_kernel(*refs, number, widths, half_place):
    masters, tokens = refs[:number], refs[number]
    fulls, traded, own = refs[number + 1:2 * number + 1], refs[2 * number + 1], refs[2 * number + 2:3 * number + 2]
    local_sem, send_sem, recv_sem, trade_sem = refs[3 * number + 2:]
    group, place = lax.axis_index("fsdp"), lax.axis_index("ctx")
    core_bit, pair_bit, side = lax.rem(group, 2), lax.rem(group // 2, 2), lax.rem(place, 2)
    core, pair = group + 1 - 2 * core_bit, group + 2 - 4 * pair_bit
    partner = {"core": (core, place), "pair": (pair, place), "side": (group, place + 1 - 2 * side)}
    top = place // half_place
    trader = (core, place + half_place - 2 * half_place * top)
    trades = core_bit != top

    barrier = pltpu.get_barrier_semaphore()
    for other in partner.values():
        pl.semaphore_signal(barrier, inc=1, device_id=other, device_id_type=pl.DeviceIdType.MESH)

    def trading():
        return pltpu.make_async_remote_copy(
            src_ref=tokens,
            dst_ref=traded,
            send_sem=trade_sem.at[0],
            recv_sem=trade_sem.at[1],
            device_id=trader,
            device_id_type=pl.DeviceIdType.MESH,
        )

    def keeping():
        return pltpu.make_async_copy(tokens, traded, trade_sem.at[2])

    @pl.when(trades)
    def _():
        pl.semaphore_signal(barrier, inc=1, device_id=trader, device_id_type=pl.DeviceIdType.MESH)
        pl.semaphore_wait(barrier, len(partner) + 1)
        trading().start()

    @pl.when(jnp.logical_not(trades))
    def _():
        pl.semaphore_wait(barrier, len(partner))
        keeping().start()

    sent = []

    def send(to, source, target):
        copy = pltpu.make_async_remote_copy(
            src_ref=source,
            dst_ref=target,
            send_sem=send_sem.at[len(sent)],
            recv_sem=recv_sem.at[len(sent)],
            device_id=partner[to],
            device_id_type=pl.DeviceIdType.MESH,
        )
        copy.start()
        sent.append(copy)
        return copy

    depth = own[0].shape[0]
    half = depth // 2
    rows = lambda start, count: pl.ds(pl.multiple_of(start, 16), count)

    def cast(index, start):
        def body(i, carry):
            here = rows(start + i * 16, 16)
            own[index][here, :] = masters[index][here, :].astype(jnp.bfloat16)
            return carry

        lax.fori_loop(0, half // 16, body, 0)

    pieces = [
        (index, slice(start, start + width))
        for index, width in enumerate(widths)
        for start in range(0, own[index].shape[1], width)
    ]
    mine, others = side * half, (1 - side) * half
    crossing = []
    for index in range(number):
        cast(index, mine)
        for piece, columns in pieces:
            if piece == index:
                crossing.append(
                    send(
                        "pair",
                        own[index].at[rows(mine, half), columns],
                        fulls[index].at[rows(group * depth + mine, half), columns],
                    )
                )
    local = []
    for index in range(number):
        cast(index, others)
        place_own = fulls[index].at[rows(group * depth, depth)]
        send("core", own[index], place_own)
        local.append(pltpu.make_async_copy(own[index], place_own, local_sem.at[index]))
        local[-1].start()
    passing = []
    for (index, columns), copy in zip(pieces, crossing):
        copy.wait_recv()
        here = fulls[index].at[rows(pair * depth + mine, half), columns]
        passing.append(send("side", here, here))
        send("core", here, here)
    last = []
    for (index, columns), copy in zip(pieces, passing):
        copy.wait_recv()
        here = fulls[index].at[rows(pair * depth + others, half), columns]
        last.append(send("core", here, here))
    for copy in sent:
        if all(copy is not other for other in crossing + passing):
            copy.wait_recv()

    @pl.when(trades)
    def _():
        trading().wait()

    @pl.when(jnp.logical_not(trades))
    def _():
        keeping().wait()

    for copy in sent:
        copy.wait_send()
    for copy in local:
        copy.wait()


def gather(masters, tokens, number):
    widths = [next(w for w in (1280, master.shape[1]) if master.shape[1] % w == 0) for master in masters]
    count = len(masters)
    pieces = sum(master.shape[1] // width for master, width in zip(masters, widths))
    low, sends = jnp.bfloat16, 3 * pieces + pieces + count
    return pl.pallas_call(
        functools.partial(
            gather_kernel, number=count, widths=widths, half_place=lax.axis_size("ctx") // 2
        ),
        out_shape=[
            jax.ShapeDtypeStruct((value.shape[0] * lax.axis_size("fsdp"), value.shape[1]), low) for value in masters
        ]
        + [jax.ShapeDtypeStruct(tokens.shape, tokens.dtype)],
        in_specs=[pl.BlockSpec(memory_space=pltpu.VMEM) for _ in masters]
        + [pl.BlockSpec(memory_space=pl.ANY)],
        out_specs=[pl.BlockSpec(memory_space=pl.ANY) for _ in masters]
        + [pl.BlockSpec(memory_space=pl.ANY)],
        scratch_shapes=[pltpu.VMEM(value.shape, low) for value in masters]
        + [
            pltpu.SemaphoreType.DMA((count,)),
            pltpu.SemaphoreType.DMA((sends,)),
            pltpu.SemaphoreType.DMA((sends,)),
            pltpu.SemaphoreType.DMA((3,)),
        ],
        cost_estimate=pl.CostEstimate(
            flops=0, bytes_accessed=16 * sum(value.size * 4 for value in masters), transcendentals=0
        ),
        compiler_params=pltpu.CompilerParams(
            collective_id=number, has_side_effects=True, vmem_limit_bytes=56 * 1024 * 1024
        ),
        name="gather",
    )(*masters, tokens)


def gather_plain(master, *others):
    low = master.astype(jnp.bfloat16)
    return lax.all_gather(after(low, *others) if others else low, "fsdp", axis=0, tiled=True)


def gather_vector(vector):
    me, count = lax.axis_index("fsdp"), lax.axis_size("fsdp")
    low = vector.astype(jnp.bfloat16)
    by_distance = jnp.stack(
        [low]
        + [lax.ppermute(low, "fsdp", [(i, i ^ step) for i in range(count)]) for step in range(1, count)]
    )
    return jnp.concatenate(
        [lax.dynamic_index_in_dim(by_distance, me ^ shard, 0, keepdims=False) for shard in range(count)]
    )


def on_device(
    tokens,
    cotangent,
    lengths,
    widths,
    weight_qkv,
    moment_qkv,
    square_qkv,
    weight_out,
    moment_out,
    square_out,
    weight_up,
    moment_up,
    square_up,
    weight_down,
    moment_down,
    square_down,
    vectors,
    moment_vectors,
    square_vectors,
):
    ranks = lax.axis_size("ctx")
    core, top = bit_of("fsdp", 0), lax.axis_index("ctx") // (ranks // 2)
    here = core * (ranks // 2) + lax.rem(lax.axis_index("ctx"), ranks // 2)
    kept = core == top
    lengths, widths = [jnp.where(kept, value, swap(value, "fsdp", 0)) for value in (lengths, widths)]
    full_vector = gather_vector(vectors)
    if lax.axis_size("fsdp") == 4 and weight_qkv.shape[0] % 32 == 0 and weight_out.shape[0] % 32 == 0:
        full_qkv, full_out, own_tokens = gather([weight_qkv, weight_out], tokens.reshape(-1, tokens.shape[2]), 1)
    else:
        own_tokens = trade(tokens, kept)
        full_qkv, full_out = gather_plain(weight_qkv), gather_plain(weight_out)
    full_up = gather_plain(weight_up, full_out)
    full_down = gather_plain(weight_down, full_out)
    model_width = tokens.shape[2]
    hidden_units = full_up.shape[1]
    gain_one, shift_one, bias_qkv, bias_out, gain_two, shift_two, bias_up, bias_down = split_vector(
        full_vector.astype(jnp.float32), model_width, hidden_units
    )
    row_count = tokens.shape[0]
    slots_here = tokens.shape[1]
    slots_all = slots_here * lax.axis_size("ctx")
    token_count = row_count * slots_here
    local_heads = HEADS // ranks
    row_pos, col_pos, valid_slots, start_of, end_of = layout(lengths, widths, slots_all)
    valid_here = lax.dynamic_slice_in_dim(valid_slots, here * slots_here, slots_here, 1)
    cosine_table, sine_table = rotary_tables(by_block(row_pos, slots_here), by_block(col_pos, slots_here))
    cosine_here = lax.dynamic_index_in_dim(cosine_table, here, 0, keepdims=False)
    sine_here = lax.dynamic_index_in_dim(sine_table, here, 0, keepdims=False)
    low_high = jnp.stack([by_block(start_of, slots_here), by_block(end_of, slots_here)], axis=1)
    tile = slots_here * max(1, min(512 // slots_here, ranks))
    starts = start_of.reshape(row_count, slots_all // tile, tile)
    ends = end_of.reshape(row_count, slots_all // tile, tile)
    plain = (jnp.max(starts, axis=2) == 0) & (jnp.min(ends, axis=2) == slots_all)
    span = jnp.stack(
        [
            jnp.min(starts, axis=2) // tile,
            (jnp.max(ends, axis=2) + tile - 1) // tile,
            plain.astype(jnp.int32),
        ],
        axis=-1,
    ).astype(jnp.int32)
    flat_tokens = own_tokens.reshape(token_count, model_width).astype(jnp.float32)
    scaled_one, root_one = standardize(flat_tokens)
    first_normed = (scaled_one * gain_one + shift_one).astype(jnp.bfloat16)
    joined = (
        jnp.einsum("df,td->ft", full_qkv, first_normed, preferred_element_type=jnp.float32)
        + bias_qkv[:, None]
    )
    pairs = joined[: 2 * model_width].reshape(2, HEADS, 2, HEAD_DIM // 2, token_count)
    lower, upper_half = pairs[:, :, 0], pairs[:, :, 1]
    turned = jnp.stack(
        [lower * cosine_here - upper_half * sine_here, upper_half * cosine_here + lower * sine_here],
        axis=2,
    ).reshape(2 * model_width, token_count)
    heads_out = (
        jnp.concatenate([turned, joined[2 * model_width :]], axis=0)
        .astype(jnp.bfloat16)
        .reshape(3, local_heads, ranks, HEAD_DIM, token_count)
        .transpose(1, 2, 0, 3, 4)
    )
    heads_in = [exchange(heads_out[h]) for h in range(local_heads)]
    attended, lse, mixed = [], [], []
    for h in range(local_heads):
        result, stat = attend(span, heads_in[h], low_high)
        attended.append(result)
        lse.append(stat)
        mixed.append(exchange(result))
    own_cotangent = trade(after(cotangent, attended[0]), kept)
    mixed = jnp.stack(mixed, axis=0).reshape(model_width, token_count)
    hidden = flat_tokens + jnp.einsum("it,io->to", mixed, full_out, preferred_element_type=jnp.float32) + bias_out
    scaled_two, root_two = standardize(hidden)
    second_normed = (scaled_two * gain_two + shift_two).astype(jnp.bfloat16)
    upper = jnp.dot(second_normed, full_up, preferred_element_type=jnp.float32) + bias_up
    sigma = jax.nn.sigmoid(1.702 * upper)
    active = (upper * sigma).astype(jnp.bfloat16)
    result = hidden + jnp.dot(active, full_down, preferred_element_type=jnp.float32) + bias_down
    output = trade(result.astype(jnp.bfloat16).reshape(tokens.shape), kept)
    grad_result = own_cotangent.reshape(token_count, model_width).astype(
        jnp.float32
    ) * valid_here.reshape(token_count, 1).astype(jnp.float32)
    grad_low = grad_result.astype(jnp.bfloat16)
    d_bias_down = jnp.sum(grad_result, axis=0)
    sum_down = Reduction(owner_order(active, 1), grad_low, "ti,to->io", 1)
    grad_low = after(grad_low, sum_down.leave())
    d_active = jnp.einsum("td,fd->tf", grad_low, full_down, preferred_element_type=jnp.float32)
    d_upper = (d_active * (sigma + 1.702 * upper * sigma * (1.0 - sigma))).astype(jnp.bfloat16)
    d_bias_up = jnp.sum(d_upper, axis=0, dtype=jnp.float32)
    d_upper = after(d_upper, sum_down.cross(d_upper))
    sum_up = Reduction(owner_order(second_normed, 1), d_upper, "ti,to->io", 1)
    d_upper = after(d_upper, sum_up.leave())
    d_second = jnp.einsum("tf,df->td", d_upper, full_up, preferred_element_type=jnp.float32)
    d_second = after(d_second, sum_up.cross(d_second))
    d_gain_two = jnp.sum(d_second * scaled_two, axis=0)
    d_shift_two = jnp.sum(d_second, axis=0)
    d_hidden = grad_result + norm_back(d_second, gain_two, scaled_two, root_two)
    d_branch = d_hidden.astype(jnp.bfloat16)
    d_bias_out = jnp.sum(d_branch, axis=0, dtype=jnp.float32)
    sum_out = Reduction(owner_order(mixed, 0), d_branch, "it,to->io", 0)
    d_branch = after(d_branch, sum_out.leave())
    d_mixed = (
        jnp.einsum("to,io->it", d_branch, full_out, preferred_element_type=jnp.float32)
        .astype(jnp.bfloat16)
        .reshape(local_heads, ranks, HEAD_DIM, token_count)
    )
    split = all(
        splits_of(value.shape[0], value.shape[1]) for value in (weight_qkv, weight_out, weight_up, weight_down)
    )
    d_attended = [exchange(d_mixed[h]) for h in range(local_heads)]
    d_attended[0] = after(d_attended[0], sum_out.cross(d_mixed))
    normed_owners = owner_order(first_normed, 1)
    d_heads, sum_qkv = [], []
    for h in range(local_heads):
        d_heads.append(
            attend_back(
                span, heads_in[h], low_high, attended[h], d_attended[h], lse[h], cosine_table, sine_table
            )
        )
        if h == 0 and split:
            sent = sum_down.leave_ctx(d_heads[0])
            if local_heads > 1:
                d_attended[1] = after(d_attended[1], sent)
    for h in range(local_heads):
        came = exchange(d_heads[h])
        if h > 0:
            sent = [sum_qkv[-1].leave()]
            if split:
                sent.append(sum_down.leave_ctx(*sent))
                sent.append(sum_up.leave_ctx(*sent))
            came = after(came, *sent, sum_qkv[-1].cross_pair(*sent))
        d_heads[h] = came.transpose(1, 0, 2, 3)
        right = d_heads[h].reshape(3 * ranks * HEAD_DIM, token_count)
        sum_qkv.append(Reduction(normed_owners, right, "ti,ot->io", 1))
    last = sum_qkv[-1].leave()
    d_joined = jnp.stack(d_heads, axis=1).reshape(3 * model_width, token_count)
    d_joined = after(d_joined, last)
    d_bias_qkv = jnp.sum(d_joined, axis=1, dtype=jnp.float32)
    d_first = jnp.einsum("jt,dj->td", d_joined, full_qkv, preferred_element_type=jnp.float32)
    d_first = after(d_first, sum_qkv[-1].cross_pair(d_first))
    d_gain_one = jnp.sum(d_first * scaled_one, axis=0)
    d_shift_one = jnp.sum(d_first, axis=0)
    input_grad = (d_hidden + norm_back(d_first, gain_one, scaled_one, root_one)).reshape(
        tokens.shape
    )
    input_grad = jnp.where(kept, input_grad, trade(input_grad.astype(jnp.bfloat16), kept).astype(jnp.float32))
    d_vectors = jnp.concatenate(
        [
            d_gain_one,
            d_shift_one,
            d_bias_qkv,
            d_bias_out,
            d_gain_two,
            d_shift_two,
            d_bias_up,
            d_bias_down,
        ]
    )
    sum_qkv = Joined(sum_qkv, 3)
    if split:
        (grad_down, grad_up, grad_qkv, grad_outw), total_squares, total_vectors = settle(
            [sum_down, sum_up, sum_qkv, sum_out], [0, 0, 1, 1], d_vectors, 0
        )
    else:
        grad_down, grad_up, grad_qkv, grad_outw = [
            lax.psum(add_up(value.parts).astype(jnp.bfloat16), "ctx")
            for value in (sum_down, sum_up, sum_qkv, sum_out)
        ]
        total_squares = lax.psum(
            functools.reduce(
                jnp.add,
                [
                    jnp.sum(jnp.square(grad.astype(jnp.float32)))
                    for grad in (grad_down, grad_up, grad_outw, grad_qkv)
                ],
            ),
            "fsdp",
        )
        total_vectors = lax.psum(d_vectors, EVERYWHERE)
    total_squares = total_squares + jnp.sum(jnp.square(total_vectors))
    grad_vectors = lax.dynamic_slice_in_dim(
        total_vectors, lax.axis_index("fsdp") * vectors.shape[0], vectors.shape[0], 0
    )
    grad_down, grad_up, grad_outw, grad_qkv = [
        grad.astype(jnp.float32) for grad in (grad_down, grad_up, grad_outw, grad_qkv)
    ]
    grad_norm = jnp.sqrt(total_squares)
    factor = jnp.minimum(1.0, clip_level / grad_norm)
    new_qkv = adam_update(
        weight_qkv, moment_qkv, square_qkv, grad_qkv, factor, rate_matrix, decay_matrix
    )
    new_out = adam_update(
        weight_out, moment_out, square_out, grad_outw, factor, rate_matrix, decay_matrix
    )
    new_up = adam_update(
        weight_up, moment_up, square_up, grad_up, factor, rate_matrix, decay_matrix
    )
    new_down = adam_update(
        weight_down, moment_down, square_down, grad_down, factor, rate_matrix, decay_matrix
    )
    new_vec = adam_update(
        vectors, moment_vectors, square_vectors, grad_vectors, factor, rate_vector, 0.0
    )
    return (
        output,
        input_grad,
        grad_norm,
        new_qkv[0],
        new_qkv[1],
        new_qkv[2],
        new_out[0],
        new_out[1],
        new_out[2],
        new_up[0],
        new_up[1],
        new_up[2],
        new_down[0],
        new_down[1],
        new_down[2],
        new_vec[0],
        new_vec[1],
        new_vec[2],
    )


def solution(mesh):
    placed = (
        P("fsdp", "ctx", None),
        P("fsdp", "ctx", None),
        P("fsdp", None),
        P("fsdp", None),
        P("fsdp", None),
        P("fsdp", None),
        P("fsdp", None),
        P("fsdp", None),
        P("fsdp", None),
        P("fsdp", None),
        P("fsdp", None),
        P("fsdp", None),
        P("fsdp", None),
        P("fsdp", None),
        P("fsdp", None),
        P("fsdp", None),
        P("fsdp"),
        P("fsdp"),
        P("fsdp"),
    )
    return jax.shard_map(
        on_device,
        mesh=mesh,
        in_specs=placed,
        out_specs=(
            P("fsdp", "ctx", None),
            P("fsdp", "ctx", None),
            P(),
            P("fsdp", None),
            P("fsdp", None),
            P("fsdp", None),
            P("fsdp", None),
            P("fsdp", None),
            P("fsdp", None),
            P("fsdp", None),
            P("fsdp", None),
            P("fsdp", None),
            P("fsdp", None),
            P("fsdp", None),
            P("fsdp", None),
            P("fsdp"),
            P("fsdp"),
            P("fsdp"),
        ),
        check_vma=False,
    )
```

```python
import functools

import jax
import jax.numpy as jnp
from jax import lax
from jax.experimental import pallas as pl
from jax.experimental.pallas import tpu as pltpu
from jax.sharding import PartitionSpec as P

HEADS = 16
HEAD_DIM = 80
STEP = 5


eps_norm = 1e-06
beta_one = 0.9
beta_two = 0.999
adam_eps = 1e-08
decay_matrix = 0.05
rate_matrix = 0.04
rate_vector = 0.3
clip_level = 1.0


LOG2E = 1.4426950408889634


EVERYWHERE = ("fsdp", "ctx")


def device(pair, core, top, low):
    half = lax.axis_size("ctx") // 2
    return ((pair * 2 + core) * 2 + top) * half + low


def trade(value):
    pairs = []
    for pair in range(lax.axis_size("fsdp") // 2):
        for low in range(lax.axis_size("ctx") // 2):
            one, other = device(pair, 1, 0, low), device(pair, 0, 1, low)
            pairs += [(one, other), (other, one)]
    return lax.ppermute(value, EVERYWHERE, pairs)


def exchange(source):
    groups = [
        [device(pair, core, top, low) for core in range(2) for low in range(lax.axis_size("ctx") // 2)]
        for pair in range(lax.axis_size("fsdp") // 2)
        for top in range(2)
    ]
    return lax.all_to_all(source, EVERYWHERE, 0, 0, axis_index_groups=groups)


def after(value, *others):
    return lax.optimization_barrier((value,) + others)[0]


def attend_kernel(span, qkv, low_high, out, stat, keys, values, *, size, tile, extent, step_size):
    row, place = pl.program_id(0), pl.program_id(1)
    blocks = extent // size
    group = tile // size
    scale = HEAD_DIM ** (-0.5) * LOG2E

    @pl.when(place == 0)
    def _():
        for b in range(blocks):
            keys[b * size:(b + 1) * size, :] = qkv[b, 1].T
            values[:, b * size:(b + 1) * size] = qkv[b, 2]

    first, last, plain = span[row, place, 0], span[row, place, 1], span[row, place, 2]
    query = jnp.concatenate([qkv[place * group + i, 0] for i in range(group)], axis=1)

    def finish(peak, total, mixed):
        mixed = (mixed / total).astype(jnp.bfloat16)
        lse = peak + jnp.log2(total)
        for i in range(group):
            out[i] = mixed[:, i * size:(i + 1) * size]
            stat[i] = lse[:, i * size:(i + 1) * size]

    def step(start, carry, keep=None):
        peak, total, mixed = carry
        s = jnp.dot(keys[pl.ds(start, step_size), :], query, preferred_element_type=jnp.float32) * scale
        if keep is not None:
            s = jnp.where(keep, s, -1e30)
        top = jnp.maximum(peak, jnp.max(s, axis=0, keepdims=True))
        fade = jnp.exp2(peak - top)
        raised = jnp.exp2(s - top)
        total = total * fade + jnp.sum(raised, axis=0, keepdims=True)
        mixed = mixed * fade + jnp.dot(values[:, pl.ds(start, step_size)], raised.astype(jnp.bfloat16),
                                       preferred_element_type=jnp.float32)
        return top, total, mixed

    begin = (
        jnp.full((1, tile), -1e30, jnp.float32),
        jnp.zeros((1, tile), jnp.float32),
        jnp.zeros((HEAD_DIM, tile), jnp.float32),
    )

    @pl.when(plain == 1)
    def _():
        carry = begin
        for b in range(extent // step_size):
            carry = step(b * step_size, carry)
        finish(*carry)

    @pl.when(plain == 0)
    def _():
        low = jnp.concatenate([low_high[i, 0:1, :] for i in range(group)], axis=1)
        high = jnp.concatenate([low_high[i, 1:2, :] for i in range(group)], axis=1)

        def masked(b, carry):
            start = pl.multiple_of(b * step_size, step_size)
            places = lax.broadcasted_iota(jnp.int32, (step_size, tile), 0) + start
            return step(start, carry, (places >= low) & (places < high))

        finish(*lax.fori_loop(first, last, masked, begin))


def attend(span, qkv, low_high):
    blocks, _, width, lanes = qkv.shape
    rows = span.shape[0]
    size = lanes // rows
    group = blocks // span.shape[1]
    tile = group * size
    grid_spec = pltpu.PrefetchScalarGridSpec(
        num_scalar_prefetch=1,
        grid=(rows, blocks // group),
        in_specs=[
            pl.BlockSpec((blocks, 3, width, size), lambda r, b, s: (0, 0, 0, r)),
            pl.BlockSpec((group, 2, size), lambda r, b, s: (b, 0, r)),
        ],
        out_specs=[
            pl.BlockSpec((group, width, size), lambda r, b, s: (b, 0, r)),
            pl.BlockSpec((group, 1, size), lambda r, b, s: (b, 0, r)),
        ],
        scratch_shapes=[pltpu.VMEM((blocks * size, HEAD_DIM), jnp.bfloat16), pltpu.VMEM((HEAD_DIM, blocks * size), jnp.bfloat16)],
    )
    return pl.pallas_call(
        functools.partial(attend_kernel, size=size, tile=tile, extent=blocks * size, step_size=tile),
        grid_spec=grid_spec,
        out_shape=[
            jax.ShapeDtypeStruct((blocks, width, lanes), jnp.bfloat16),
            jax.ShapeDtypeStruct((blocks, 1, lanes), jnp.float32),
        ],
        cost_estimate=pl.CostEstimate(
            flops=4 * rows * (blocks * size) ** 2 * 256,
            bytes_accessed=5 * blocks * width * lanes * 2,
            transcendentals=rows * (blocks * size) ** 2,
        ),
        compiler_params=pltpu.CompilerParams(vmem_limit_bytes=48 * 1024 * 1024),
        name="attend",
    )(span, qkv, low_high)


def attend_back_kernel(span, qkv, low_high, mixed, d_mixed, stat, cosine, sine, out, keys, values, keys_t, d_keys, d_values,
                       *, size, tile, extent, step_size):
    row, place = pl.program_id(0), pl.program_id(1)
    blocks = extent // size
    group = tile // size
    scale = HEAD_DIM ** (-0.5)
    half = HEAD_DIM // 2

    @pl.when(place == 0)
    def _():
        d_keys[...] = jnp.zeros_like(d_keys)
        d_values[...] = jnp.zeros_like(d_values)
        for b in range(blocks):
            keys[b * size:(b + 1) * size, :] = qkv[b, 1].T
            values[b * size:(b + 1) * size, :] = qkv[b, 2].T
            keys_t[:, b * size:(b + 1) * size] = qkv[b, 1]

    def turn_back(v, cos, sin):
        upper, lower = v[half:], v[:half]
        return jnp.concatenate([lower * cos + upper * sin, upper * cos - lower * sin], axis=0)

    side = lambda parts: jnp.concatenate(parts, axis=1)
    first, last, plain = span[row, place, 0], span[row, place, 1], span[row, place, 2]
    query = side([qkv[place * group + i, 0] for i in range(group)])
    grad = side([d_mixed[i] for i in range(group)])
    query_n, grad_n = query.T, grad.T
    delta = jnp.sum(grad.astype(jnp.float32) * side([mixed[i] for i in range(group)]).astype(jnp.float32), axis=0, keepdims=True)
    lse = side([stat[i] for i in range(group)])

    def step(start, d_query, keep=None):
        here = pl.ds(start, step_size)
        s = jnp.dot(keys[here, :], query, preferred_element_type=jnp.float32)
        d_probs = jnp.dot(values[here, :], grad, preferred_element_type=jnp.float32)
        exact = jnp.exp2(s * (scale * LOG2E) - lse)
        if keep is not None:
            exact = jnp.where(keep, exact, 0.0)
        d_scores = (exact * (d_probs - delta)).astype(jnp.bfloat16)
        d_values[here, :] += jnp.dot(exact.astype(jnp.bfloat16), grad_n, preferred_element_type=jnp.float32)
        d_keys[here, :] += jnp.dot(d_scores, query_n, preferred_element_type=jnp.float32)
        return d_query + jnp.dot(keys_t[:, here], d_scores, preferred_element_type=jnp.float32)

    def finish(d_query):
        for i in range(group):
            b = place * group + i
            out[b, 0] = turn_back(d_query[:, i * size:(i + 1) * size] * scale, cosine[b], sine[b]).astype(jnp.bfloat16)

    begin = jnp.zeros((HEAD_DIM, tile), jnp.float32)

    @pl.when(plain == 1)
    def _():
        d_query = begin
        for b in range(extent // step_size):
            d_query = step(b * step_size, d_query)
        finish(d_query)

    @pl.when(plain == 0)
    def _():
        low = side([low_high[i, 0:1, :] for i in range(group)])
        high = side([low_high[i, 1:2, :] for i in range(group)])

        def masked(b, d_query):
            start = pl.multiple_of(b * step_size, step_size)
            places = lax.broadcasted_iota(jnp.int32, (step_size, tile), 0) + start
            return step(start, d_query, (places >= low) & (places < high))

        finish(lax.fori_loop(first, last, masked, begin))

    @pl.when(place == blocks // group - 1)
    def _():
        for b in range(blocks):
            here = slice(b * size, (b + 1) * size)
            out[b, 1] = turn_back(d_keys[here, :].T * scale, cosine[b], sine[b]).astype(jnp.bfloat16)
            out[b, 2] = d_values[here, :].T.astype(jnp.bfloat16)


def attend_back(span, qkv, low_high, mixed, d_mixed, stat, cosine, sine):
    blocks, _, width, lanes = qkv.shape
    rows = span.shape[0]
    size = lanes // rows
    group = blocks // span.shape[1]
    tile = group * size
    per = lambda r, b, s: (b, 0, r)
    whole = lambda r, b, s: (0, 0, r)
    grid_spec = pltpu.PrefetchScalarGridSpec(
        num_scalar_prefetch=1,
        grid=(rows, blocks // group),
        in_specs=[
            pl.BlockSpec((blocks, 3, width, size), lambda r, b, s: (0, 0, 0, r)),
            pl.BlockSpec((group, 2, size), per),
            pl.BlockSpec((group, width, size), per),
            pl.BlockSpec((group, width, size), per),
            pl.BlockSpec((group, 1, size), per),
            pl.BlockSpec((blocks, HEAD_DIM // 2, size), whole),
            pl.BlockSpec((blocks, HEAD_DIM // 2, size), whole),
        ],
        out_specs=pl.BlockSpec((blocks, 3, width, size), lambda r, b, s: (0, 0, 0, r)),
        scratch_shapes=[
            pltpu.VMEM((blocks * size, HEAD_DIM), jnp.bfloat16),
            pltpu.VMEM((blocks * size, HEAD_DIM), jnp.bfloat16),
            pltpu.VMEM((HEAD_DIM, blocks * size), jnp.bfloat16),
            pltpu.VMEM((blocks * size, HEAD_DIM), jnp.float32),
            pltpu.VMEM((blocks * size, HEAD_DIM), jnp.float32),
        ],
    )
    return pl.pallas_call(
        functools.partial(attend_back_kernel, size=size, tile=tile, extent=blocks * size, step_size=tile),
        grid_spec=grid_spec,
        out_shape=jax.ShapeDtypeStruct(qkv.shape, jnp.bfloat16),
        cost_estimate=pl.CostEstimate(
            flops=10 * rows * (blocks * size) ** 2 * 256,
            bytes_accessed=10 * blocks * width * lanes * 2,
            transcendentals=rows * (blocks * size) ** 2,
        ),
        compiler_params=pltpu.CompilerParams(vmem_limit_bytes=56 * 1024 * 1024),
        name="attend_back",
    )(span, qkv, low_high, mixed, d_mixed, stat, cosine, sine)


def layout(lengths, widths, extent):
    piece_ends = jnp.cumsum(lengths, axis=1)
    piece_starts = piece_ends - lengths
    places = jnp.arange(extent, dtype=jnp.int32)[None, :, None]
    inside = (places >= piece_starts[:, None, :]) & (places < piece_ends[:, None, :])
    pick = lambda table: jnp.sum(jnp.where(inside, table[:, None, :], 0), axis=2)
    filled = piece_ends[:, -1:]
    valid = places[..., 0] < filled
    start_of = jnp.where(valid, pick(piece_starts), filled)
    end_of = jnp.where(valid, pick(piece_ends), extent)
    width_of = jnp.where(valid, pick(widths), 1)
    within = places[..., 0] - start_of
    return within // width_of, within % width_of, valid, start_of, end_of


def by_block(table, size):
    rows, extent = table.shape
    return table.reshape(rows, extent // size, size).transpose(1, 0, 2).reshape(extent // size, rows * size)


def rotary_tables(row_pos, col_pos):
    quarter = HEAD_DIM // 4
    inverse = 10000.0 ** (-(2.0 * jnp.arange(quarter, dtype=jnp.float32)) / (HEAD_DIM // 2))
    angles = jnp.concatenate(
        [
            row_pos.astype(jnp.float32)[:, None, :] * inverse[None, :, None],
            col_pos.astype(jnp.float32)[:, None, :] * inverse[None, :, None],
        ],
        axis=1,
    )
    return (jnp.cos(angles), jnp.sin(angles))


def split_vector(vector, width, hidden_units):
    return (
        vector[:width],
        vector[width : 2 * width],
        vector[2 * width : 5 * width],
        vector[5 * width : 6 * width],
        vector[6 * width : 7 * width],
        vector[7 * width : 8 * width],
        vector[8 * width : 8 * width + hidden_units],
        vector[8 * width + hidden_units :],
    )


def standardize(inputs):
    center = inputs - jnp.mean(inputs, axis=-1, keepdims=True)
    root_inverse = lax.rsqrt(jnp.mean(center * center, axis=-1, keepdims=True) + eps_norm)
    return (center * root_inverse, root_inverse)


def norm_back(d_norm, gain_vector, scaled, root_inverse):
    effect = d_norm * gain_vector
    inner = jnp.mean(effect, axis=-1, keepdims=True)
    along = jnp.mean(effect * scaled, axis=-1, keepdims=True)
    return root_inverse * (effect - inner - scaled * along)


def adam_update(weight, moment, square, grad, factor, rate, decay):
    clipped = grad * factor
    moment = beta_one * moment + (1.0 - beta_one) * clipped
    square = beta_two * square + (1.0 - beta_two) * clipped * clipped
    fixed_moment = moment / (1.0 - beta_one**STEP)
    fixed_square = square / (1.0 - beta_two**STEP)
    weight = weight - rate * (fixed_moment / (jnp.sqrt(fixed_square) + adam_eps) + decay * weight)
    return (weight, moment, square)


def swap(value, axis, bit):
    count = lax.axis_size(axis)
    return lax.ppermute(value, axis, [(i, i ^ (1 << bit)) for i in range(count)])


def bit_of(axis, bit):
    return lax.rem(lax.axis_index(axis) // (1 << bit), 2)


def bits(axis):
    return range(lax.axis_size(axis).bit_length() - 1)


def owner_order(value, dim):
    count = lax.axis_size("fsdp")
    depth = value.shape[dim] // count
    core = bit_of("fsdp", 0)
    return jnp.concatenate(
        [
            lax.dynamic_slice_in_dim(value, (2 * pair + side) * depth, depth, dim)
            for side in (1 - core, core)
            for pair in range(count // 2)
        ],
        axis=dim,
    )


def add_up(parts):
    return functools.reduce(jnp.add, [part.astype(jnp.float32) for part in parts])


class Reduction:
    def __init__(self, left, right, form, dim):
        self.left, self.right, self.form, self.dim = left, right, form, dim
        self.total = left.shape[dim]
        self.rows = self.total // lax.axis_size("fsdp")
        self.columns = right.shape[0 if form[3] == "o" else 1]
        self.splits = splits_of(self.rows, self.columns)
        self.begun = 0

    def product(self, start, stop, *others):
        left = after(self.left, *others) if others else self.left
        return jnp.einsum(
            self.form,
            lax.slice_in_dim(left, start, stop, axis=self.dim),
            self.right,
            preferred_element_type=jnp.float32,
        )

    def leave(self):
        sent = self.product(0, self.total // 2).astype(jnp.bfloat16)
        self.came = swap(sent, "fsdp", 0)
        return sent

    def cross(self, *others):
        came = after(self.came, *others) if others else self.came
        kept = add_up([self.product(self.total // 2, self.total, *others), came]).astype(jnp.bfloat16)
        pairs, places = lax.axis_size("fsdp") // 2, lax.axis_size("ctx")
        wide = self.splits is not None and self.splits[0] == 0
        step = 2 if wide else 1
        groups = [
            [(2 * pair + core) * places + place + bit for pair in range(pairs) for bit in range(step)]
            for core in range(2)
            for place in range(0, places, step)
        ]
        self.parts = [
            lax.psum_scatter(kept, EVERYWHERE, scatter_dimension=0, tiled=True, axis_index_groups=groups)
        ]
        self.begun = step - 1
        return kept

    def cross_later(self, *others):
        if lax.axis_size("fsdp") != 4 or self.splits is None:
            return self.cross(*others)
        came = after(self.came, *others) if others else self.came
        kept = add_up([self.product(self.total // 2, self.total), came]).astype(jnp.bfloat16)
        mine = bit_of("fsdp", 1) * self.rows
        self.parts = [lax.dynamic_slice_in_dim(kept, mine, self.rows, 0)]
        self.crossing = lax.dynamic_slice_in_dim(kept, self.rows - mine, self.rows, 0)
        self.starts = [0]
        return kept

    def cross_pair(self, *others, send=True):
        if lax.axis_size("fsdp") != 4:
            return self.cross(*others)
        came = after(self.came, *others) if others else self.came
        mine = bit_of("fsdp", 1) * self.rows
        theirs = self.rows - mine
        pick = lambda start: add_up(
            [
                jnp.einsum(
                    self.form,
                    lax.dynamic_slice_in_dim(self.left, self.total // 2 + start, self.rows, self.dim),
                    self.right,
                    preferred_element_type=jnp.float32,
                ),
                lax.dynamic_slice_in_dim(came, start, self.rows, 0),
            ]
        ).astype(jnp.bfloat16)
        sent = pick(theirs)
        self.parts = [pick(mine), swap(sent, "fsdp", 1) if send else sent]
        return sent

    def leave_ctx(self, *others):
        if others:
            self.parts[-1] = after(self.parts[-1], *others)
        dim = self.splits[self.begun]
        half = self.parts[0].shape[dim] // 2
        mine = bit_of("ctx", self.begun)
        pick = lambda side: [lax.dynamic_slice_in_dim(part, side * half, half, dim) for part in self.parts]
        sent = add_up(pick(1 - mine)).astype(jnp.bfloat16)
        own = add_up(pick(mine)).astype(jnp.bfloat16)
        self.parts = [own, swap(sent, "ctx", self.begun)]
        self.begun += 1
        return sent

    def state(self):
        return self.parts


class Joined:
    def __init__(self, sums, blocks, crosses=True):
        width = sums[0].columns // blocks
        self.rows, self.columns = sums[0].rows, sums[0].columns * len(sums)
        self.splits = splits_of(self.rows, self.columns)
        self.begun = sums[0].begun
        whole = [add_up(value.parts).astype(jnp.bfloat16) for value in sums]
        if crosses:
            whole[-1] = sums[-1].parts[0]
        self.parts = [
            jnp.concatenate(
                [value[:, b * width : (b + 1) * width] for b in range(blocks) for value in whole], axis=1
            )
        ]
        self.crossing = sums[-1].parts[1] if crosses and len(sums[-1].parts) > 1 else None
        self.starts = [(b * len(sums) + len(sums) - 1) * width for b in range(blocks)]

    def state(self):
        return self.parts


def splits_of(rows, columns):
    dims = []
    for _ in bits("ctx"):
        if rows % 32 == 0:
            rows //= 2
            dims.append(0)
        elif columns % 256 == 0:
            columns //= 2
            dims.append(1)
        else:
            return None
    return dims


def plan(units, count):
    links, done, ready = {}, [], []
    for unit, (rows, columns, begun, spared, crossing) in enumerate(units):
        phases = [
            (bit, rows * columns / 2 ** (bit + 1) * 2 ** max(bit - 1, 0) + 20000) for bit in range(count)
        ]
        phases = phases + phases[::-1][: count - spared] + [("x", crossing)]
        ready.append((0.0, unit, begun - 1 if crossing else begun, phases))
    while ready:
        ready.sort(key=lambda item: (max(item[0], links.get(item[3][item[2]][0], 0.0)), item[1]))
        time, unit, phase, phases = ready.pop(0)
        link, length = phases[phase]
        end = max(time, links.get(link, 0.0)) + length
        links[link] = end
        done.append((end, unit, phase))
        if phase + 2 < len(phases):
            ready.append((end, unit, phase + 1, phases))
    return [(unit, phase) for _, unit, phase in sorted(done)]


def settle_kernel(*refs, units, splits, starts, given, count):
    number = len(units)
    arrays = sum(given)
    sources, small, targets, total = (
        list(refs[:arrays]), refs[arrays], refs[arrays + 1:arrays + 1 + number], refs[arrays + 1 + number]
    )
    scratch = list(refs[arrays + 2 + number:])
    take = lambda wanted: [scratch.pop(0) for _ in range(wanted)]
    group, place = lax.axis_index("fsdp"), lax.axis_index("ctx")
    group_bit = [lax.rem(group // 2**b, 2) for b in bits("fsdp")]
    place_bit = [lax.rem(place // 2**b, 2) for b in range(count)]
    partner = {("ctx", b): (group, place + (1 - 2 * place_bit[b]) * 2**b) for b in range(count)}
    partner.update({("fsdp", b): (group + (1 - 2 * bit) * 2**b, place) for b, bit in enumerate(group_bit)})

    barrier = pltpu.get_barrier_semaphore()
    for other in partner.values():
        pl.semaphore_signal(barrier, inc=1, device_id=other, device_id_type=pl.DeviceIdType.MESH)
    pl.semaphore_wait(barrier, len(partner))

    local_sem, send_sem, recv_sem, squares, from_others = take(5)
    sent, local = [], [0]

    def send(link, source, target):
        copy = pltpu.make_async_remote_copy(
            src_ref=source,
            dst_ref=target,
            send_sem=send_sem.at[len(sent)],
            recv_sem=recv_sem.at[len(sent)],
            device_id=partner[link],
            device_id_type=pl.DeviceIdType.MESH,
        )
        copy.start()
        sent.append(copy)
        return copy

    def move(source, target):
        copy = pltpu.make_async_copy(source, target, local_sem.at[local[0]])
        local[0] += 1
        copy.start()
        return copy

    def part(ref, row, rows, column, columns):
        if columns == ref.shape[1]:
            return ref.at[pl.ds(pl.multiple_of(row, 16), rows)]
        return ref.at[pl.ds(pl.multiple_of(row, 16), rows), pl.ds(pl.multiple_of(column, 128), columns)]

    def add(left, right, target, measure=False):
        def body(i, held):
            here = pl.ds(pl.multiple_of(i * 16, 16), 16)
            value = left[here, :]
            if right is not None:
                value = (value.astype(jnp.float32) + right[here, :].astype(jnp.float32)).astype(jnp.bfloat16)
            target[here, :] = value
            if measure:
                value = value.astype(jnp.float32)
                for tile in range(value.shape[1] // 128):
                    piece = value[:, tile * 128:(tile + 1) * 128]
                    held = held + piece * piece
            return held

        held = lax.fori_loop(0, left.shape[0] // 16, body, jnp.zeros((16, 128), jnp.float32))
        if measure:
            squares[0, 0:16] = squares[0, 0:16] + held

    class Unit:
        pass

    states = []
    for index, (rows, columns, begun, spared, crossing) in enumerate(units):
        unit = Unit()
        unit.begun, unit.target, unit.dims, unit.starts = begun, targets[index], splits[index], starts[index]
        unit.spared = spared
        unit.region = [(0, rows, 0, columns)]
        for bit in range(count):
            row, depth, column, width = unit.region[-1]
            if unit.dims[bit] == 0:
                depth //= 2
                row = row + place_bit[bit] * depth
            else:
                width //= 2
                column = column + place_bit[bit] * width
            unit.region.append((row, depth, column, width))
        unit.final, unit.held = take(2)
        unit.came = take(1)[0] if given[index] == 2 else None
        unit.taken = [None] * begun + take(count - begun)
        unit.loads = [move(sources.pop(0), unit.held)]
        unit.crossing = crossing > 0
        if unit.crossing:
            unit.copy = send(("fsdp", 1), sources.pop(0), unit.came)
        elif unit.came is not None:
            unit.loads.append(move(sources.pop(0), unit.came))
        states.append(unit)

    def halves(unit, ref, bit):
        depth, width = ref.shape
        if unit.dims[bit] == 0:
            depth //= 2
            pick = lambda side: part(ref, side * depth, depth, 0, width)
        else:
            width //= 2
            pick = lambda side: part(ref, 0, depth, side * width, width)
        return pick(place_bit[bit]), pick(1 - place_bit[bit])

    def proceed(unit, bit, ref):
        unit.kept, leaving = halves(unit, ref, bit)
        unit.copy = send(("ctx", bit), leaving, unit.taken[bit])

    def hand_out(unit, bit):
        region = part(unit.final, *unit.region[bit + 1])
        unit.copy = send(("ctx", bit), region, region)

    left = [number]

    def settled(unit, own, came):
        add(own, came, part(unit.final, *unit.region[count]), measure=True)
        left[0] -= 1
        hand_out(unit, count - 1)

    def advance(unit, phase):
        unit.copy.wait_recv()
        if phase < unit.begun:
            width = unit.came.shape[1] // len(unit.starts)
            for block, start in enumerate(unit.starts):
                here = part(unit.held, 0, unit.held.shape[0], start, width)
                add(here, part(unit.came, 0, unit.came.shape[0], block * width, width), here)
            proceed(unit, unit.begun, unit.held)
        elif phase < count - 1:
            add(unit.kept, unit.taken[phase], unit.taken[phase])
            proceed(unit, phase + 1, unit.taken[phase])
        elif phase == count - 1:
            settled(unit, unit.kept, unit.taken[phase])
        elif phase < 2 * count - 1 - unit.spared:
            hand_out(unit, 2 * count - 2 - phase)
        else:
            unit.store = move(part(unit.final, *unit.region[unit.spared]), unit.target)

    squared, squares_copy = [-1], [None]

    def exchange_squares():
        step = squared[0] = squared[0] + 1
        if step > 0:
            squares_copy[0].wait_recv()
            squares[step] = squares[step - 1] + from_others[step - 1]
        if step < len(partner):
            squares_copy[0] = send(list(partner)[step], squares.at[step], from_others.at[step])

    squares[0, 0:16] = jnp.zeros((16, 128), jnp.float32)
    squares[0, 16:] = small[...]
    for unit in states:
        for load in unit.loads:
            load.wait()
        if unit.crossing:
            continue
        if unit.begun < count:
            if unit.came is not None:
                add(unit.held, unit.came, unit.held)
            proceed(unit, unit.begun, unit.held)
        else:
            settled(unit, unit.held, unit.came)
    for index, phase in plan(units, count):
        advance(states[index], phase)
        if left[0] == 0 and squared[0] < len(partner):
            exchange_squares()
    while squared[0] < len(partner):
        exchange_squares()
    total[...] = squares[len(partner)]
    for copy in sent:
        copy.wait_send()
    for unit in states:
        unit.store.wait()


def settle(sums, spared, vector, number):
    count, links = len(bits("ctx")), len(bits("ctx")) + len(bits("fsdp"))
    crossing = [getattr(value, "crossing", None) for value in sums]
    units = [
        (value.rows, value.columns, value.begun, less, 0 if sent is None else sent.size)
        for value, less, sent in zip(sums, spared, crossing)
    ]
    tall = -(-vector.shape[0] // 1024) * 8
    small = jnp.pad(vector, (0, tall * 128 - vector.shape[0])).reshape(tall, 128)
    low = jnp.bfloat16
    scratch, sends, sources = [], links, []
    for value, leaving in zip(sums, crossing):
        state = value.state()
        sources += state
        if leaving is not None:
            sources.append(leaving)
            sends += 1
        scratch.append(pltpu.VMEM((value.rows, value.columns), low))
        scratch += len(state) * [pltpu.VMEM(state[0].shape, low)]
        if leaving is not None:
            scratch.append(pltpu.VMEM(leaving.shape, low))
        depth, width = state[0].shape
        for dim in value.splits[value.begun:]:
            depth, width = (depth // 2, width) if dim == 0 else (depth, width // 2)
            scratch.append(pltpu.VMEM((depth, width), low))
        sends += 2 * count - value.begun
    scratch = [
        pltpu.SemaphoreType.DMA((3 * len(units),)),
        pltpu.SemaphoreType.DMA((sends,)),
        pltpu.SemaphoreType.DMA((sends,)),
        pltpu.VMEM((links + 1, 16 + tall, 128), jnp.float32),
        pltpu.VMEM((links, 16 + tall, 128), jnp.float32),
    ] + scratch
    shapes = []
    for value, less in zip(sums, spared):
        rows, columns = value.rows, value.columns
        for dim in value.splits[:less]:
            rows, columns = (rows // 2, columns) if dim == 0 else (rows, columns // 2)
        shapes.append(jax.ShapeDtypeStruct((rows, columns), low))
    *results, total = pl.pallas_call(
        functools.partial(
            settle_kernel,
            units=units,
            splits=[value.splits for value in sums],
            starts=[getattr(value, "starts", None) for value in sums],
            given=[len(value.state()) + (sent is not None) for value, sent in zip(sums, crossing)],
            count=count,
        ),
        out_shape=shapes + [jax.ShapeDtypeStruct((16 + tall, 128), jnp.float32)],
        in_specs=[pl.BlockSpec(memory_space=pl.ANY) for _ in sources]
        + [pl.BlockSpec(memory_space=pltpu.VMEM)],
        out_specs=[pl.BlockSpec(memory_space=pl.ANY) for _ in units]
        + [pl.BlockSpec(memory_space=pltpu.VMEM)],
        scratch_shapes=scratch,
        cost_estimate=pl.CostEstimate(
            flops=0, bytes_accessed=64 * sum(unit[0] * unit[1] * 2 for unit in units), transcendentals=0
        ),
        compiler_params=pltpu.CompilerParams(
            collective_id=number, has_side_effects=True, vmem_limit_bytes=56 * 1024 * 1024
        ),
        name="settle",
    )(*sources, small)
    for index, (value, less) in enumerate(zip(sums, spared)):
        for bit in reversed(range(less)):
            other, dim = swap(results[index], "ctx", bit), value.splits[bit]
            results[index] = jnp.where(
                bit_of("ctx", bit) == 0,
                jnp.concatenate([results[index], other], axis=dim),
                jnp.concatenate([other, results[index]], axis=dim),
            )
    return results, jnp.sum(total[:16]), total[16:].reshape(-1)[: vector.shape[0]]


def gather_kernel(*refs, number, traded, widths, half_place):
    masters, rows_in = refs[:number], refs[number:number + traded]
    fulls, refs = refs[number + traded:2 * number + traded], refs[2 * number + traded:]
    rows_out, own = refs[:traded], refs[traded:traded + number]
    local_sem, send_sem, recv_sem, trade_sem = refs[traded + number:]
    group, place = lax.axis_index("fsdp"), lax.axis_index("ctx")
    core_bit, pair_bit, side = lax.rem(group, 2), lax.rem(group // 2, 2), lax.rem(place, 2)
    core, pair = group + 1 - 2 * core_bit, group + 2 - 4 * pair_bit
    partner = {"core": (core, place), "pair": (pair, place), "side": (group, place + 1 - 2 * side)}
    top = place // half_place
    trader = (core, place + half_place - 2 * half_place * top)
    trades = core_bit != top

    barrier = pltpu.get_barrier_semaphore()
    for other in partner.values():
        pl.semaphore_signal(barrier, inc=1, device_id=other, device_id_type=pl.DeviceIdType.MESH)

    def trading(which):
        return pltpu.make_async_remote_copy(
            src_ref=rows_in[which],
            dst_ref=rows_out[which],
            send_sem=trade_sem.at[which, 0],
            recv_sem=trade_sem.at[which, 1],
            device_id=trader,
            device_id_type=pl.DeviceIdType.MESH,
        )

    def keeping(which):
        return pltpu.make_async_copy(rows_in[which], rows_out[which], trade_sem.at[which, 2])

    @pl.when(trades)
    def _():
        pl.semaphore_signal(barrier, inc=1, device_id=trader, device_id_type=pl.DeviceIdType.MESH)
        pl.semaphore_wait(barrier, len(partner) + 1)
        for which in range(traded):
            trading(which).start()

    @pl.when(jnp.logical_not(trades))
    def _():
        pl.semaphore_wait(barrier, len(partner))
        for which in range(traded):
            keeping(which).start()

    sent = []

    def send(to, source, target):
        copy = pltpu.make_async_remote_copy(
            src_ref=source,
            dst_ref=target,
            send_sem=send_sem.at[len(sent)],
            recv_sem=recv_sem.at[len(sent)],
            device_id=partner[to],
            device_id_type=pl.DeviceIdType.MESH,
        )
        copy.start()
        sent.append(copy)
        return copy

    depth = own[0].shape[0]
    half = depth // 2
    rows = lambda start, count: pl.ds(pl.multiple_of(start, 16), count)

    def cast(index, start):
        def body(i, carry):
            here = rows(start + i * 16, 16)
            own[index][here, :] = masters[index][here, :].astype(jnp.bfloat16)
            return carry

        lax.fori_loop(0, half // 16, body, 0)

    pieces = [
        (index, slice(start, start + width))
        for index, width in enumerate(widths)
        for start in range(0, own[index].shape[1], width)
    ]
    mine, others = side * half, (1 - side) * half
    crossing = []
    for index in range(number):
        cast(index, mine)
        for piece, columns in pieces:
            if piece == index:
                crossing.append(
                    send(
                        "pair",
                        own[index].at[rows(mine, half), columns],
                        fulls[index].at[rows(group * depth + mine, half), columns],
                    )
                )
    local = []
    for index in range(number):
        cast(index, others)
        place_own = fulls[index].at[rows(group * depth, depth)]
        send("core", own[index], place_own)
        local.append(pltpu.make_async_copy(own[index], place_own, local_sem.at[index]))
        local[-1].start()
    passing = []
    for (index, columns), copy in zip(pieces, crossing):
        copy.wait_recv()
        here = fulls[index].at[rows(pair * depth + mine, half), columns]
        passing.append(send("side", here, here))
        send("core", here, here)
    last = []
    for (index, columns), copy in zip(pieces, passing):
        copy.wait_recv()
        here = fulls[index].at[rows(pair * depth + others, half), columns]
        last.append(send("core", here, here))
    for copy in sent:
        if all(copy is not other for other in crossing + passing):
            copy.wait_recv()

    @pl.when(trades)
    def _():
        for which in range(traded):
            trading(which).wait()

    @pl.when(jnp.logical_not(trades))
    def _():
        for which in range(traded):
            keeping(which).wait()

    for copy in sent:
        copy.wait_send()
    for copy in local:
        copy.wait()


def gather(masters, rows, number):
    widths = [next(w for w in (1280, master.shape[1]) if master.shape[1] % w == 0) for master in masters]
    count = len(masters)
    pieces = sum(master.shape[1] // width for master, width in zip(masters, widths))
    low, sends = jnp.bfloat16, 3 * pieces + pieces + count
    return pl.pallas_call(
        functools.partial(
            gather_kernel, number=count, traded=len(rows), widths=widths, half_place=lax.axis_size("ctx") // 2
        ),
        out_shape=[
            jax.ShapeDtypeStruct((value.shape[0] * lax.axis_size("fsdp"), value.shape[1]), low) for value in masters
        ]
        + [jax.ShapeDtypeStruct(value.shape, value.dtype) for value in rows],
        in_specs=[pl.BlockSpec(memory_space=pltpu.VMEM) for _ in masters]
        + [pl.BlockSpec(memory_space=pl.ANY) for _ in rows],
        out_specs=[pl.BlockSpec(memory_space=pl.ANY) for _ in masters + rows],
        scratch_shapes=[pltpu.VMEM(value.shape, low) for value in masters]
        + [
            pltpu.SemaphoreType.DMA((count,)),
            pltpu.SemaphoreType.DMA((sends,)),
            pltpu.SemaphoreType.DMA((sends,)),
            pltpu.SemaphoreType.DMA((len(rows), 3)),
        ],
        cost_estimate=pl.CostEstimate(
            flops=0, bytes_accessed=16 * sum(value.size * 4 for value in masters), transcendentals=0
        ),
        compiler_params=pltpu.CompilerParams(
            collective_id=number, has_side_effects=True, vmem_limit_bytes=56 * 1024 * 1024
        ),
        name="gather",
    )(*masters, *rows)


def gather_plain(master, *others):
    low = master.astype(jnp.bfloat16)
    return lax.all_gather(after(low, *others) if others else low, "fsdp", axis=0, tiled=True)


def gather_vector(vector):
    me, count = lax.axis_index("fsdp"), lax.axis_size("fsdp")
    low = vector.astype(jnp.bfloat16)
    by_distance = jnp.stack(
        [low]
        + [lax.ppermute(low, "fsdp", [(i, i ^ step) for i in range(count)]) for step in range(1, count)]
    )
    return jnp.concatenate(
        [lax.dynamic_index_in_dim(by_distance, me ^ shard, 0, keepdims=False) for shard in range(count)]
    )


def on_device(
    tokens,
    cotangent,
    lengths,
    widths,
    weight_qkv,
    moment_qkv,
    square_qkv,
    weight_out,
    moment_out,
    square_out,
    weight_up,
    moment_up,
    square_up,
    weight_down,
    moment_down,
    square_down,
    vectors,
    moment_vectors,
    square_vectors,
):
    ranks = lax.axis_size("ctx")
    core, top = bit_of("fsdp", 0), lax.axis_index("ctx") // (ranks // 2)
    here = core * (ranks // 2) + lax.rem(lax.axis_index("ctx"), ranks // 2)
    kept = core == top
    lengths, widths = [jnp.where(kept, value, swap(value, "fsdp", 0)) for value in (lengths, widths)]
    full_vector = gather_vector(vectors)
    if lax.axis_size("fsdp") == 4 and weight_qkv.shape[0] % 32 == 0 and weight_out.shape[0] % 32 == 0:
        full_qkv, full_out, own_tokens = gather(
            [weight_qkv, weight_out], [tokens.reshape(-1, tokens.shape[2])], 1
        )
    else:
        own_tokens = jnp.where(kept, tokens, trade(tokens))
        full_qkv, full_out = gather_plain(weight_qkv), gather_plain(weight_out)
    full_up = gather_plain(weight_up, full_out)
    full_down = gather_plain(weight_down, full_out)
    model_width = tokens.shape[2]
    hidden_units = full_up.shape[1]
    gain_one, shift_one, bias_qkv, bias_out, gain_two, shift_two, bias_up, bias_down = split_vector(
        full_vector.astype(jnp.float32), model_width, hidden_units
    )
    row_count = tokens.shape[0]
    slots_here = tokens.shape[1]
    slots_all = slots_here * lax.axis_size("ctx")
    token_count = row_count * slots_here
    local_heads = HEADS // ranks
    row_pos, col_pos, valid_slots, start_of, end_of = layout(lengths, widths, slots_all)
    valid_here = lax.dynamic_slice_in_dim(valid_slots, here * slots_here, slots_here, 1)
    cosine_table, sine_table = rotary_tables(by_block(row_pos, slots_here), by_block(col_pos, slots_here))
    cosine_here = lax.dynamic_index_in_dim(cosine_table, here, 0, keepdims=False)
    sine_here = lax.dynamic_index_in_dim(sine_table, here, 0, keepdims=False)
    low_high = jnp.stack([by_block(start_of, slots_here), by_block(end_of, slots_here)], axis=1)
    tile = slots_here * max(1, min(512 // slots_here, ranks))
    starts = start_of.reshape(row_count, slots_all // tile, tile)
    ends = end_of.reshape(row_count, slots_all // tile, tile)
    plain = (jnp.max(starts, axis=2) == 0) & (jnp.min(ends, axis=2) == slots_all)
    span = jnp.stack(
        [
            jnp.min(starts, axis=2) // tile,
            (jnp.max(ends, axis=2) + tile - 1) // tile,
            plain.astype(jnp.int32),
        ],
        axis=-1,
    ).astype(jnp.int32)
    flat_tokens = own_tokens.reshape(token_count, model_width).astype(jnp.float32)
    scaled_one, root_one = standardize(flat_tokens)
    first_normed = (scaled_one * gain_one + shift_one).astype(jnp.bfloat16)
    joined = (
        jnp.einsum("df,td->ft", full_qkv, first_normed, preferred_element_type=jnp.float32)
        + bias_qkv[:, None]
    )
    pairs = joined[: 2 * model_width].reshape(2, HEADS, 2, HEAD_DIM // 2, token_count)
    lower, upper_half = pairs[:, :, 0], pairs[:, :, 1]
    turned = jnp.stack(
        [lower * cosine_here - upper_half * sine_here, upper_half * cosine_here + lower * sine_here],
        axis=2,
    ).reshape(2 * model_width, token_count)
    heads_out = (
        jnp.concatenate([turned, joined[2 * model_width :]], axis=0)
        .astype(jnp.bfloat16)
        .reshape(3, local_heads, ranks, HEAD_DIM, token_count)
        .transpose(1, 2, 0, 3, 4)
    )
    heads_in = [exchange(heads_out[h]) for h in range(local_heads)]
    attended, lse, mixed = [], [], []
    for h in range(local_heads):
        result, stat = attend(span, heads_in[h], low_high)
        attended.append(result)
        lse.append(stat)
        mixed.append(exchange(result))
    came_cotangent = trade(after(cotangent, attended[0]))
    mixed = jnp.stack(mixed, axis=0).reshape(model_width, token_count)
    hidden = flat_tokens + jnp.einsum("it,io->to", mixed, full_out, preferred_element_type=jnp.float32) + bias_out
    scaled_two, root_two = standardize(hidden)
    second_normed = (scaled_two * gain_two + shift_two).astype(jnp.bfloat16)
    upper = jnp.dot(second_normed, full_up, preferred_element_type=jnp.float32) + bias_up
    sigma = jax.nn.sigmoid(1.702 * upper)
    active = (upper * sigma).astype(jnp.bfloat16)
    result = hidden + jnp.dot(active, full_down, preferred_element_type=jnp.float32) + bias_down
    output = result.astype(jnp.bfloat16).reshape(tokens.shape)
    came_output = trade(output)
    own_cotangent = jnp.where(kept, cotangent, after(came_cotangent, active))
    grad_result = own_cotangent.reshape(token_count, model_width).astype(
        jnp.float32
    ) * valid_here.reshape(token_count, 1).astype(jnp.float32)
    grad_low = grad_result.astype(jnp.bfloat16)
    d_bias_down = jnp.sum(grad_result, axis=0)
    sum_down = Reduction(owner_order(active, 1), grad_low, "ti,to->io", 1)
    grad_low = after(grad_low, sum_down.leave())
    d_active = jnp.einsum("td,fd->tf", grad_low, full_down, preferred_element_type=jnp.float32)
    d_upper = (d_active * (sigma + 1.702 * upper * sigma * (1.0 - sigma))).astype(jnp.bfloat16)
    d_bias_up = jnp.sum(d_upper, axis=0, dtype=jnp.float32)
    d_upper = after(d_upper, sum_down.cross(d_upper))
    sum_up = Reduction(owner_order(second_normed, 1), d_upper, "ti,to->io", 1)
    d_upper = after(d_upper, sum_up.leave())
    d_second = jnp.einsum("tf,df->td", d_upper, full_up, preferred_element_type=jnp.float32)
    d_second = after(d_second, sum_up.cross(d_second))
    d_gain_two = jnp.sum(d_second * scaled_two, axis=0)
    d_shift_two = jnp.sum(d_second, axis=0)
    d_hidden = grad_result + norm_back(d_second, gain_two, scaled_two, root_two)
    d_branch = d_hidden.astype(jnp.bfloat16)
    d_bias_out = jnp.sum(d_branch, axis=0, dtype=jnp.float32)
    sum_out = Reduction(owner_order(mixed, 0), d_branch, "it,to->io", 0)
    d_branch = after(d_branch, sum_out.leave())
    d_mixed = (
        jnp.einsum("to,io->it", d_branch, full_out, preferred_element_type=jnp.float32)
        .astype(jnp.bfloat16)
        .reshape(local_heads, ranks, HEAD_DIM, token_count)
        .transpose(1, 0, 2, 3)
    )
    split = all(
        splits_of(value.shape[0], value.shape[1]) for value in (weight_qkv, weight_out, weight_up, weight_down)
    )
    came_mixed = exchange(d_mixed)
    d_attended = [came_mixed[:, h] for h in range(local_heads)]
    d_attended[0] = after(d_attended[0], sum_out.cross_later(d_mixed), output)
    normed_owners = owner_order(first_normed, 1)
    d_heads, sum_qkv = [], []
    for h in range(local_heads):
        d_heads.append(
            attend_back(
                span, heads_in[h], low_high, attended[h], d_attended[h], lse[h], cosine_table, sine_table
            )
        )
        if h == 0 and split:
            sent = sum_down.leave_ctx(d_heads[0])
            if local_heads > 1:
                d_attended[1] = after(d_attended[1], sent)
    backward = list(d_heads)
    came_output = after(came_output, backward[-1])
    for h in range(local_heads):
        came = after(exchange(d_heads[h]), backward[-1])
        if h > 0:
            sent = [sum_qkv[-1].leave()]
            sent.append(sum_qkv[-1].cross_pair(*sent))
            if split:
                sent.append(sum_down.leave_ctx(*sent))
                sent.append(sum_up.leave_ctx(*sent))
            came = after(came, *sent)
        d_heads[h] = came.transpose(1, 0, 2, 3)
        right = d_heads[h].reshape(3 * ranks * HEAD_DIM, token_count)
        sum_qkv.append(Reduction(normed_owners, right, "ti,ot->io", 1))
    last = sum_qkv[-1].leave()
    d_joined = jnp.stack(d_heads, axis=1).reshape(3 * model_width, token_count)
    d_joined = after(d_joined, last)
    d_bias_qkv = jnp.sum(d_joined, axis=1, dtype=jnp.float32)
    d_first = jnp.einsum("jt,dj->td", d_joined, full_qkv, preferred_element_type=jnp.float32)
    d_first = after(d_first, sum_qkv[-1].cross_pair(d_first, send=not split))
    d_gain_one = jnp.sum(d_first * scaled_one, axis=0)
    d_shift_one = jnp.sum(d_first, axis=0)
    input_grad = (d_hidden + norm_back(d_first, gain_one, scaled_one, root_one)).reshape(
        tokens.shape
    )
    output = jnp.where(kept, output, came_output)
    came_grad = trade(input_grad.astype(jnp.bfloat16))
    d_vectors = jnp.concatenate(
        [
            d_gain_one,
            d_shift_one,
            d_bias_qkv,
            d_bias_out,
            d_gain_two,
            d_shift_two,
            d_bias_up,
            d_bias_down,
        ]
    )
    if split:
        (grad_down, grad_up, grad_qkv, grad_outw), total_squares, total_vectors = settle(
            [sum_down, sum_up, Joined(sum_qkv, 3), sum_out], [0, 0, 1, 1], d_vectors, 0
        )
    else:
        grad_down, grad_up, grad_qkv, grad_outw = [
            lax.psum(add_up(value.parts).astype(jnp.bfloat16), "ctx")
            for value in (sum_down, sum_up, Joined(sum_qkv, 3, False), sum_out)
        ]
        total_squares = lax.psum(
            functools.reduce(
                jnp.add,
                [
                    jnp.sum(jnp.square(grad.astype(jnp.float32)))
                    for grad in (grad_down, grad_up, grad_outw, grad_qkv)
                ],
            ),
            "fsdp",
        )
        total_vectors = lax.psum(d_vectors, EVERYWHERE)
    total_squares = total_squares + jnp.sum(jnp.square(total_vectors))
    grad_vectors = lax.dynamic_slice_in_dim(
        total_vectors, lax.axis_index("fsdp") * vectors.shape[0], vectors.shape[0], 0
    )
    grad_down, grad_up, grad_outw, grad_qkv = [
        grad.astype(jnp.float32) for grad in (grad_down, grad_up, grad_outw, grad_qkv)
    ]
    input_grad = jnp.where(kept, input_grad, after(came_grad, total_squares).astype(jnp.float32))
    grad_norm = jnp.sqrt(total_squares)
    factor = jnp.minimum(1.0, clip_level / grad_norm)
    new_qkv = adam_update(
        weight_qkv, moment_qkv, square_qkv, grad_qkv, factor, rate_matrix, decay_matrix
    )
    new_out = adam_update(
        weight_out, moment_out, square_out, grad_outw, factor, rate_matrix, decay_matrix
    )
    new_up = adam_update(
        weight_up, moment_up, square_up, grad_up, factor, rate_matrix, decay_matrix
    )
    new_down = adam_update(
        weight_down, moment_down, square_down, grad_down, factor, rate_matrix, decay_matrix
    )
    new_vec = adam_update(
        vectors, moment_vectors, square_vectors, grad_vectors, factor, rate_vector, 0.0
    )
    return (
        output,
        input_grad,
        grad_norm,
        new_qkv[0],
        new_qkv[1],
        new_qkv[2],
        new_out[0],
        new_out[1],
        new_out[2],
        new_up[0],
        new_up[1],
        new_up[2],
        new_down[0],
        new_down[1],
        new_down[2],
        new_vec[0],
        new_vec[1],
        new_vec[2],
    )


def solution(mesh):
    placed = (
        P("fsdp", "ctx", None),
        P("fsdp", "ctx", None),
        P("fsdp", None),
        P("fsdp", None),
        P("fsdp", None),
        P("fsdp", None),
        P("fsdp", None),
        P("fsdp", None),
        P("fsdp", None),
        P("fsdp", None),
        P("fsdp", None),
        P("fsdp", None),
        P("fsdp", None),
        P("fsdp", None),
        P("fsdp", None),
        P("fsdp", None),
        P("fsdp"),
        P("fsdp"),
        P("fsdp"),
    )
    return jax.shard_map(
        on_device,
        mesh=mesh,
        in_specs=placed,
        out_specs=(
            P("fsdp", "ctx", None),
            P("fsdp", "ctx", None),
            P(),
            P("fsdp", None),
            P("fsdp", None),
            P("fsdp", None),
            P("fsdp", None),
            P("fsdp", None),
            P("fsdp", None),
            P("fsdp", None),
            P("fsdp", None),
            P("fsdp", None),
            P("fsdp", None),
            P("fsdp", None),
            P("fsdp", None),
            P("fsdp"),
            P("fsdp"),
            P("fsdp"),
        ),
        check_vma=False,
    )
```

```python
import functools

import jax
import jax.numpy as jnp
from jax import lax
from jax.experimental import pallas as pl
from jax.experimental.pallas import tpu as pltpu
from jax.sharding import PartitionSpec as P

HEADS = 16
HEAD_DIM = 80
STEP = 5


eps_norm = 1e-06
beta_one = 0.9
beta_two = 0.999
adam_eps = 1e-08
decay_matrix = 0.05
rate_matrix = 0.04
rate_vector = 0.3
clip_level = 1.0


LOG2E = 1.4426950408889634


EVERYWHERE = ("fsdp", "ctx")


def device(pair, core, top, low):
    half = lax.axis_size("ctx") // 2
    return ((pair * 2 + core) * 2 + top) * half + low


def trade(value):
    pairs = []
    for pair in range(lax.axis_size("fsdp") // 2):
        for low in range(lax.axis_size("ctx") // 2):
            one, other = device(pair, 1, 0, low), device(pair, 0, 1, low)
            pairs += [(one, other), (other, one)]
    return lax.ppermute(value, EVERYWHERE, pairs)


def exchange(source):
    groups = [
        [device(pair, core, top, low) for core in range(2) for low in range(lax.axis_size("ctx") // 2)]
        for pair in range(lax.axis_size("fsdp") // 2)
        for top in range(2)
    ]
    return lax.all_to_all(source, EVERYWHERE, 0, 0, axis_index_groups=groups)


def after(value, *others):
    return lax.optimization_barrier((value,) + others)[0]


def attend_kernel(span, qkv, low_high, out, stat, keys, values, *, size, tile, extent, step_size):
    row, place = pl.program_id(0), pl.program_id(1)
    blocks = extent // size
    group = tile // size
    scale = HEAD_DIM ** (-0.5) * LOG2E

    @pl.when(place == 0)
    def _():
        for b in range(blocks):
            keys[b * size:(b + 1) * size, :] = qkv[b, 1].T
            values[:, b * size:(b + 1) * size] = qkv[b, 2]

    first, last, plain = span[row, place, 0], span[row, place, 1], span[row, place, 2]
    query = jnp.concatenate([qkv[place * group + i, 0] for i in range(group)], axis=1)

    def finish(peak, total, mixed):
        mixed = (mixed / total).astype(jnp.bfloat16)
        lse = peak + jnp.log2(total)
        for i in range(group):
            out[i] = mixed[:, i * size:(i + 1) * size]
            stat[i] = lse[:, i * size:(i + 1) * size]

    def step(start, carry, keep=None):
        peak, total, mixed = carry
        s = jnp.dot(keys[pl.ds(start, step_size), :], query, preferred_element_type=jnp.float32) * scale
        if keep is not None:
            s = jnp.where(keep, s, -1e30)
        top = jnp.maximum(peak, jnp.max(s, axis=0, keepdims=True))
        fade = jnp.exp2(peak - top)
        raised = jnp.exp2(s - top)
        total = total * fade + jnp.sum(raised, axis=0, keepdims=True)
        mixed = mixed * fade + jnp.dot(values[:, pl.ds(start, step_size)], raised.astype(jnp.bfloat16),
                                       preferred_element_type=jnp.float32)
        return top, total, mixed

    begin = (
        jnp.full((1, tile), -1e30, jnp.float32),
        jnp.zeros((1, tile), jnp.float32),
        jnp.zeros((HEAD_DIM, tile), jnp.float32),
    )

    @pl.when(plain == 1)
    def _():
        carry = begin
        for b in range(extent // step_size):
            carry = step(b * step_size, carry)
        finish(*carry)

    @pl.when(plain == 0)
    def _():
        low = jnp.concatenate([low_high[i, 0:1, :] for i in range(group)], axis=1)
        high = jnp.concatenate([low_high[i, 1:2, :] for i in range(group)], axis=1)

        def masked(b, carry):
            start = pl.multiple_of(b * step_size, step_size)
            places = lax.broadcasted_iota(jnp.int32, (step_size, tile), 0) + start
            return step(start, carry, (places >= low) & (places < high))

        finish(*lax.fori_loop(first, last, masked, begin))


def attend(span, qkv, low_high):
    blocks, _, width, lanes = qkv.shape
    rows = span.shape[0]
    size = lanes // rows
    group = blocks // span.shape[1]
    tile = group * size
    grid_spec = pltpu.PrefetchScalarGridSpec(
        num_scalar_prefetch=1,
        grid=(rows, blocks // group),
        in_specs=[
            pl.BlockSpec((blocks, 3, width, size), lambda r, b, s: (0, 0, 0, r)),
            pl.BlockSpec((group, 2, size), lambda r, b, s: (b, 0, r)),
        ],
        out_specs=[
            pl.BlockSpec((group, width, size), lambda r, b, s: (b, 0, r)),
            pl.BlockSpec((group, 1, size), lambda r, b, s: (b, 0, r)),
        ],
        scratch_shapes=[pltpu.VMEM((blocks * size, HEAD_DIM), jnp.bfloat16), pltpu.VMEM((HEAD_DIM, blocks * size), jnp.bfloat16)],
    )
    return pl.pallas_call(
        functools.partial(attend_kernel, size=size, tile=tile, extent=blocks * size, step_size=tile),
        grid_spec=grid_spec,
        out_shape=[
            jax.ShapeDtypeStruct((blocks, width, lanes), jnp.bfloat16),
            jax.ShapeDtypeStruct((blocks, 1, lanes), jnp.float32),
        ],
        cost_estimate=pl.CostEstimate(
            flops=4 * rows * (blocks * size) ** 2 * 256,
            bytes_accessed=5 * blocks * width * lanes * 2,
            transcendentals=rows * (blocks * size) ** 2,
        ),
        compiler_params=pltpu.CompilerParams(vmem_limit_bytes=48 * 1024 * 1024),
        name="attend",
    )(span, qkv, low_high)


def attend_back_kernel(span, qkv, low_high, mixed, d_mixed, stat, cosine, sine, out, keys, values, keys_t, d_keys, d_values,
                       *, size, tile, extent, step_size):
    row, place = pl.program_id(0), pl.program_id(1)
    blocks = extent // size
    group = tile // size
    scale = HEAD_DIM ** (-0.5)
    half = HEAD_DIM // 2

    @pl.when(place == 0)
    def _():
        d_keys[...] = jnp.zeros_like(d_keys)
        d_values[...] = jnp.zeros_like(d_values)
        for b in range(blocks):
            keys[b * size:(b + 1) * size, :] = qkv[b, 1].T
            values[b * size:(b + 1) * size, :] = qkv[b, 2].T
            keys_t[:, b * size:(b + 1) * size] = qkv[b, 1]

    def turn_back(v, cos, sin):
        upper, lower = v[half:], v[:half]
        return jnp.concatenate([lower * cos + upper * sin, upper * cos - lower * sin], axis=0)

    side = lambda parts: jnp.concatenate(parts, axis=1)
    first, last, plain = span[row, place, 0], span[row, place, 1], span[row, place, 2]
    query = side([qkv[place * group + i, 0] for i in range(group)])
    grad = side([d_mixed[i] for i in range(group)])
    query_n, grad_n = query.T, grad.T
    delta = jnp.sum(grad.astype(jnp.float32) * side([mixed[i] for i in range(group)]).astype(jnp.float32), axis=0, keepdims=True)
    lse = side([stat[i] for i in range(group)])

    def step(start, d_query, keep=None):
        here = pl.ds(start, step_size)
        s = jnp.dot(keys[here, :], query, preferred_element_type=jnp.float32)
        d_probs = jnp.dot(values[here, :], grad, preferred_element_type=jnp.float32)
        exact = jnp.exp2(s * (scale * LOG2E) - lse)
        if keep is not None:
            exact = jnp.where(keep, exact, 0.0)
        d_scores = (exact * (d_probs - delta)).astype(jnp.bfloat16)
        d_values[here, :] += jnp.dot(exact.astype(jnp.bfloat16), grad_n, preferred_element_type=jnp.float32)
        d_keys[here, :] += jnp.dot(d_scores, query_n, preferred_element_type=jnp.float32)
        return d_query + jnp.dot(keys_t[:, here], d_scores, preferred_element_type=jnp.float32)

    def finish(d_query):
        for i in range(group):
            b = place * group + i
            out[b, 0] = turn_back(d_query[:, i * size:(i + 1) * size] * scale, cosine[b], sine[b]).astype(jnp.bfloat16)

    begin = jnp.zeros((HEAD_DIM, tile), jnp.float32)

    @pl.when(plain == 1)
    def _():
        d_query = begin
        for b in range(extent // step_size):
            d_query = step(b * step_size, d_query)
        finish(d_query)

    @pl.when(plain == 0)
    def _():
        low = side([low_high[i, 0:1, :] for i in range(group)])
        high = side([low_high[i, 1:2, :] for i in range(group)])

        def masked(b, d_query):
            start = pl.multiple_of(b * step_size, step_size)
            places = lax.broadcasted_iota(jnp.int32, (step_size, tile), 0) + start
            return step(start, d_query, (places >= low) & (places < high))

        finish(lax.fori_loop(first, last, masked, begin))

    @pl.when(place == blocks // group - 1)
    def _():
        for b in range(blocks):
            here = slice(b * size, (b + 1) * size)
            out[b, 1] = turn_back(d_keys[here, :].T * scale, cosine[b], sine[b]).astype(jnp.bfloat16)
            out[b, 2] = d_values[here, :].T.astype(jnp.bfloat16)


def attend_back(span, qkv, low_high, mixed, d_mixed, stat, cosine, sine):
    blocks, _, width, lanes = qkv.shape
    rows = span.shape[0]
    size = lanes // rows
    group = blocks // span.shape[1]
    tile = group * size
    per = lambda r, b, s: (b, 0, r)
    whole = lambda r, b, s: (0, 0, r)
    grid_spec = pltpu.PrefetchScalarGridSpec(
        num_scalar_prefetch=1,
        grid=(rows, blocks // group),
        in_specs=[
            pl.BlockSpec((blocks, 3, width, size), lambda r, b, s: (0, 0, 0, r)),
            pl.BlockSpec((group, 2, size), per),
            pl.BlockSpec((group, width, size), per),
            pl.BlockSpec((group, width, size), per),
            pl.BlockSpec((group, 1, size), per),
            pl.BlockSpec((blocks, HEAD_DIM // 2, size), whole),
            pl.BlockSpec((blocks, HEAD_DIM // 2, size), whole),
        ],
        out_specs=pl.BlockSpec((blocks, 3, width, size), lambda r, b, s: (0, 0, 0, r)),
        scratch_shapes=[
            pltpu.VMEM((blocks * size, HEAD_DIM), jnp.bfloat16),
            pltpu.VMEM((blocks * size, HEAD_DIM), jnp.bfloat16),
            pltpu.VMEM((HEAD_DIM, blocks * size), jnp.bfloat16),
            pltpu.VMEM((blocks * size, HEAD_DIM), jnp.float32),
            pltpu.VMEM((blocks * size, HEAD_DIM), jnp.float32),
        ],
    )
    return pl.pallas_call(
        functools.partial(attend_back_kernel, size=size, tile=tile, extent=blocks * size, step_size=tile),
        grid_spec=grid_spec,
        out_shape=jax.ShapeDtypeStruct(qkv.shape, jnp.bfloat16),
        cost_estimate=pl.CostEstimate(
            flops=10 * rows * (blocks * size) ** 2 * 256,
            bytes_accessed=10 * blocks * width * lanes * 2,
            transcendentals=rows * (blocks * size) ** 2,
        ),
        compiler_params=pltpu.CompilerParams(vmem_limit_bytes=56 * 1024 * 1024),
        name="attend_back",
    )(span, qkv, low_high, mixed, d_mixed, stat, cosine, sine)


def layout(lengths, widths, extent):
    piece_ends = jnp.cumsum(lengths, axis=1)
    piece_starts = piece_ends - lengths
    places = jnp.arange(extent, dtype=jnp.int32)[None, :, None]
    inside = (places >= piece_starts[:, None, :]) & (places < piece_ends[:, None, :])
    pick = lambda table: jnp.sum(jnp.where(inside, table[:, None, :], 0), axis=2)
    filled = piece_ends[:, -1:]
    valid = places[..., 0] < filled
    start_of = jnp.where(valid, pick(piece_starts), filled)
    end_of = jnp.where(valid, pick(piece_ends), extent)
    width_of = jnp.where(valid, pick(widths), 1)
    within = places[..., 0] - start_of
    return within // width_of, within % width_of, valid, start_of, end_of


def by_block(table, size):
    rows, extent = table.shape
    return table.reshape(rows, extent // size, size).transpose(1, 0, 2).reshape(extent // size, rows * size)


def rotary_tables(row_pos, col_pos):
    quarter = HEAD_DIM // 4
    inverse = 10000.0 ** (-(2.0 * jnp.arange(quarter, dtype=jnp.float32)) / (HEAD_DIM // 2))
    angles = jnp.concatenate(
        [
            row_pos.astype(jnp.float32)[:, None, :] * inverse[None, :, None],
            col_pos.astype(jnp.float32)[:, None, :] * inverse[None, :, None],
        ],
        axis=1,
    )
    return (jnp.cos(angles), jnp.sin(angles))


def split_vector(vector, width, hidden_units):
    return (
        vector[:width],
        vector[width : 2 * width],
        vector[2 * width : 5 * width],
        vector[5 * width : 6 * width],
        vector[6 * width : 7 * width],
        vector[7 * width : 8 * width],
        vector[8 * width : 8 * width + hidden_units],
        vector[8 * width + hidden_units :],
    )


def standardize(inputs):
    center = inputs - jnp.mean(inputs, axis=-1, keepdims=True)
    root_inverse = lax.rsqrt(jnp.mean(center * center, axis=-1, keepdims=True) + eps_norm)
    return (center * root_inverse, root_inverse)


def norm_back(d_norm, gain_vector, scaled, root_inverse):
    effect = d_norm * gain_vector
    inner = jnp.mean(effect, axis=-1, keepdims=True)
    along = jnp.mean(effect * scaled, axis=-1, keepdims=True)
    return root_inverse * (effect - inner - scaled * along)


def adam_update(weight, moment, square, grad, factor, rate, decay):
    clipped = grad * factor
    moment = beta_one * moment + (1.0 - beta_one) * clipped
    square = beta_two * square + (1.0 - beta_two) * clipped * clipped
    fixed_moment = moment / (1.0 - beta_one**STEP)
    fixed_square = square / (1.0 - beta_two**STEP)
    weight = weight - rate * (fixed_moment / (jnp.sqrt(fixed_square) + adam_eps) + decay * weight)
    return (weight, moment, square)


def swap(value, axis, bit):
    count = lax.axis_size(axis)
    return lax.ppermute(value, axis, [(i, i ^ (1 << bit)) for i in range(count)])


def bit_of(axis, bit):
    return lax.rem(lax.axis_index(axis) // (1 << bit), 2)


def bits(axis):
    return range(lax.axis_size(axis).bit_length() - 1)


def owner_order(value, dim):
    count = lax.axis_size("fsdp")
    depth = value.shape[dim] // count
    core = bit_of("fsdp", 0)
    return jnp.concatenate(
        [
            lax.dynamic_slice_in_dim(value, (2 * pair + side) * depth, depth, dim)
            for side in (1 - core, core)
            for pair in range(count // 2)
        ],
        axis=dim,
    )


def add_up(parts):
    return functools.reduce(jnp.add, [part.astype(jnp.float32) for part in parts])


class Reduction:
    def __init__(self, left, right, form, dim):
        self.left, self.right, self.form, self.dim = left, right, form, dim
        self.total = left.shape[dim]
        self.rows = self.total // lax.axis_size("fsdp")
        self.columns = right.shape[0 if form[3] == "o" else 1]
        self.splits = splits_of(self.rows, self.columns)
        self.begun = 0

    def product(self, start, stop, *others):
        left = after(self.left, *others) if others else self.left
        return jnp.einsum(
            self.form,
            lax.slice_in_dim(left, start, stop, axis=self.dim),
            self.right,
            preferred_element_type=jnp.float32,
        )

    def leave(self):
        sent = self.product(0, self.total // 2).astype(jnp.bfloat16)
        self.came = swap(sent, "fsdp", 0)
        return sent

    def cross(self, *others):
        came = after(self.came, *others) if others else self.came
        kept = add_up([self.product(self.total // 2, self.total, *others), came]).astype(jnp.bfloat16)
        pairs, places = lax.axis_size("fsdp") // 2, lax.axis_size("ctx")
        wide = self.splits is not None and self.splits[0] == 0
        step = 2 if wide else 1
        groups = [
            [(2 * pair + core) * places + place + bit for pair in range(pairs) for bit in range(step)]
            for core in range(2)
            for place in range(0, places, step)
        ]
        self.parts = [
            lax.psum_scatter(kept, EVERYWHERE, scatter_dimension=0, tiled=True, axis_index_groups=groups)
        ]
        self.begun = step - 1
        return kept

    def cross_later(self, *others):
        if lax.axis_size("fsdp") != 4 or self.splits is None:
            return self.cross(*others)
        came = after(self.came, *others) if others else self.came
        kept = add_up([self.product(self.total // 2, self.total), came]).astype(jnp.bfloat16)
        mine = bit_of("fsdp", 1) * self.rows
        self.parts = [lax.dynamic_slice_in_dim(kept, mine, self.rows, 0)]
        self.crossing = lax.dynamic_slice_in_dim(kept, self.rows - mine, self.rows, 0)
        self.starts = [0]
        return kept

    def cross_pair(self, *others, send=True):
        if lax.axis_size("fsdp") != 4:
            return self.cross(*others)
        came = after(self.came, *others) if others else self.came
        mine = bit_of("fsdp", 1) * self.rows
        theirs = self.rows - mine
        pick = lambda start: add_up(
            [
                jnp.einsum(
                    self.form,
                    lax.dynamic_slice_in_dim(self.left, self.total // 2 + start, self.rows, self.dim),
                    self.right,
                    preferred_element_type=jnp.float32,
                ),
                lax.dynamic_slice_in_dim(came, start, self.rows, 0),
            ]
        ).astype(jnp.bfloat16)
        sent = pick(theirs)
        self.parts = [pick(mine), swap(sent, "fsdp", 1) if send else sent]
        return sent

    def leave_ctx(self, *others):
        if others:
            self.parts[-1] = after(self.parts[-1], *others)
        dim = self.splits[self.begun]
        half = self.parts[0].shape[dim] // 2
        mine = bit_of("ctx", self.begun)
        pick = lambda side: [lax.dynamic_slice_in_dim(part, side * half, half, dim) for part in self.parts]
        sent = add_up(pick(1 - mine)).astype(jnp.bfloat16)
        own = add_up(pick(mine)).astype(jnp.bfloat16)
        self.parts = [own, swap(sent, "ctx", self.begun)]
        self.begun += 1
        return sent

    def state(self):
        return self.parts


class Joined:
    def __init__(self, sums, blocks, crosses=True):
        width = sums[0].columns // blocks
        self.rows, self.columns = sums[0].rows, sums[0].columns * len(sums)
        self.splits = splits_of(self.rows, self.columns)
        self.begun = sums[0].begun
        whole = [add_up(value.parts).astype(jnp.bfloat16) for value in sums]
        if crosses:
            whole[-1] = sums[-1].parts[0]
        self.parts = [
            jnp.concatenate(
                [value[:, b * width : (b + 1) * width] for b in range(blocks) for value in whole], axis=1
            )
        ]
        self.crossing = sums[-1].parts[1] if crosses and len(sums[-1].parts) > 1 else None
        self.starts = [(b * len(sums) + len(sums) - 1) * width for b in range(blocks)]

    def state(self):
        return self.parts


def splits_of(rows, columns):
    dims = []
    for _ in bits("ctx"):
        if rows % 32 == 0:
            rows //= 2
            dims.append(0)
        elif columns % 256 == 0:
            columns //= 2
            dims.append(1)
        else:
            return None
    return dims


def plan(units, count):
    links, done, ready = {}, [], []

    def loads(bit, size):
        if bit < 2:
            return {bit: size}
        return {1: size, bit: size * 2 ** (bit - 1)}

    for unit, (rows, columns, begun, spared, crossing) in enumerate(units):
        phases = [loads(bit, rows * columns / 2 ** (bit + 1)) for bit in range(count)]
        phases = phases + phases[::-1][: count - spared] + [{"x": crossing}]
        ready.append((0.0, unit, begun - 1 if crossing else begun, phases))
    start = lambda item: max([item[0]] + [links.get(link, 0.0) for link in item[3][item[2]]])
    while ready:
        ready.sort(key=lambda item: (start(item), item[1]))
        item = ready.pop(0)
        _, unit, phase, phases = item
        begin = start(item)
        for link, size in phases[phase].items():
            links[link] = begin + size
        end = begin + max(phases[phase].values()) + 20000
        done.append((end, unit, phase))
        if phase + 2 < len(phases):
            ready.append((end, unit, phase + 1, phases))
    return [(unit, phase) for _, unit, phase in sorted(done)]


def settle_kernel(*refs, units, splits, starts, given, count):
    number = len(units)
    arrays = sum(given)
    sources, small, targets, total = (
        list(refs[:arrays]), refs[arrays], refs[arrays + 1:arrays + 1 + number], refs[arrays + 1 + number]
    )
    scratch = list(refs[arrays + 2 + number:])
    take = lambda wanted: [scratch.pop(0) for _ in range(wanted)]
    group, place = lax.axis_index("fsdp"), lax.axis_index("ctx")
    group_bit = [lax.rem(group // 2**b, 2) for b in bits("fsdp")]
    place_bit = [lax.rem(place // 2**b, 2) for b in range(count)]
    partner = {("ctx", b): (group, place + (1 - 2 * place_bit[b]) * 2**b) for b in range(count)}
    partner.update({("fsdp", b): (group + (1 - 2 * bit) * 2**b, place) for b, bit in enumerate(group_bit)})

    barrier = pltpu.get_barrier_semaphore()
    for other in partner.values():
        pl.semaphore_signal(barrier, inc=1, device_id=other, device_id_type=pl.DeviceIdType.MESH)
    pl.semaphore_wait(barrier, len(partner))

    local_sem, send_sem, recv_sem, squares, from_others = take(5)
    sent, local = [], [0]

    def send(link, source, target):
        copy = pltpu.make_async_remote_copy(
            src_ref=source,
            dst_ref=target,
            send_sem=send_sem.at[len(sent)],
            recv_sem=recv_sem.at[len(sent)],
            device_id=partner[link],
            device_id_type=pl.DeviceIdType.MESH,
        )
        copy.start()
        sent.append(copy)
        return copy

    def move(source, target):
        copy = pltpu.make_async_copy(source, target, local_sem.at[local[0]])
        local[0] += 1
        copy.start()
        return copy

    def part(ref, row, rows, column, columns):
        if columns == ref.shape[1]:
            return ref.at[pl.ds(pl.multiple_of(row, 16), rows)]
        return ref.at[pl.ds(pl.multiple_of(row, 16), rows), pl.ds(pl.multiple_of(column, 128), columns)]

    def add(left, right, target, measure=False):
        def body(i, held):
            here = pl.ds(pl.multiple_of(i * 16, 16), 16)
            value = left[here, :]
            if right is not None:
                value = (value.astype(jnp.float32) + right[here, :].astype(jnp.float32)).astype(jnp.bfloat16)
            target[here, :] = value
            if measure:
                value = value.astype(jnp.float32)
                for tile in range(value.shape[1] // 128):
                    piece = value[:, tile * 128:(tile + 1) * 128]
                    held = held + piece * piece
            return held

        held = lax.fori_loop(0, left.shape[0] // 16, body, jnp.zeros((16, 128), jnp.float32))
        if measure:
            squares[0, 0:16] = squares[0, 0:16] + held

    class Unit:
        pass

    states = []
    for index, (rows, columns, begun, spared, crossing) in enumerate(units):
        unit = Unit()
        unit.begun, unit.target, unit.dims, unit.starts = begun, targets[index], splits[index], starts[index]
        unit.spared = spared
        unit.region = [(0, rows, 0, columns)]
        for bit in range(count):
            row, depth, column, width = unit.region[-1]
            if unit.dims[bit] == 0:
                depth //= 2
                row = row + place_bit[bit] * depth
            else:
                width //= 2
                column = column + place_bit[bit] * width
            unit.region.append((row, depth, column, width))
        unit.final, unit.held = take(2)
        unit.came = take(1)[0] if given[index] == 2 else None
        unit.taken = [None] * begun + take(count - begun)
        unit.loads = [move(sources.pop(0), unit.held)]
        unit.crossing = crossing > 0
        if unit.crossing:
            unit.copy = send(("fsdp", 1), sources.pop(0), unit.came)
        elif unit.came is not None:
            unit.loads.append(move(sources.pop(0), unit.came))
        states.append(unit)

    def halves(unit, ref, bit):
        depth, width = ref.shape
        if unit.dims[bit] == 0:
            depth //= 2
            pick = lambda side: part(ref, side * depth, depth, 0, width)
        else:
            width //= 2
            pick = lambda side: part(ref, 0, depth, side * width, width)
        return pick(place_bit[bit]), pick(1 - place_bit[bit])

    def proceed(unit, bit, ref):
        unit.kept, leaving = halves(unit, ref, bit)
        unit.copy = send(("ctx", bit), leaving, unit.taken[bit])

    def hand_out(unit, bit):
        region = part(unit.final, *unit.region[bit + 1])
        unit.copy = send(("ctx", bit), region, region)

    left = [number]

    def settled(unit, own, came):
        add(own, came, part(unit.final, *unit.region[count]), measure=True)
        left[0] -= 1
        hand_out(unit, count - 1)

    def advance(unit, phase):
        unit.copy.wait_recv()
        if phase < unit.begun:
            width = unit.came.shape[1] // len(unit.starts)
            for block, start in enumerate(unit.starts):
                here = part(unit.held, 0, unit.held.shape[0], start, width)
                add(here, part(unit.came, 0, unit.came.shape[0], block * width, width), here)
            proceed(unit, unit.begun, unit.held)
        elif phase < count - 1:
            add(unit.kept, unit.taken[phase], unit.taken[phase])
            proceed(unit, phase + 1, unit.taken[phase])
        elif phase == count - 1:
            settled(unit, unit.kept, unit.taken[phase])
        elif phase < 2 * count - 1 - unit.spared:
            hand_out(unit, 2 * count - 2 - phase)
        else:
            unit.store = move(part(unit.final, *unit.region[unit.spared]), unit.target)

    squared, squares_copy = [-1], [None]

    def exchange_squares():
        step = squared[0] = squared[0] + 1
        if step > 0:
            squares_copy[0].wait_recv()
            squares[step] = squares[step - 1] + from_others[step - 1]
        if step < len(partner):
            squares_copy[0] = send(list(partner)[step], squares.at[step], from_others.at[step])

    squares[0, 0:16] = jnp.zeros((16, 128), jnp.float32)
    squares[0, 16:] = small[...]
    for unit in states:
        for load in unit.loads:
            load.wait()
        if unit.crossing:
            continue
        if unit.begun < count:
            if unit.came is not None:
                add(unit.held, unit.came, unit.held)
            proceed(unit, unit.begun, unit.held)
        else:
            settled(unit, unit.held, unit.came)
    for index, phase in plan(units, count):
        advance(states[index], phase)
        if left[0] == 0 and squared[0] < len(partner):
            exchange_squares()
    while squared[0] < len(partner):
        exchange_squares()
    total[...] = squares[len(partner)]
    for copy in sent:
        copy.wait_send()
    for unit in states:
        unit.store.wait()


def settle(sums, spared, vector, number):
    count, links = len(bits("ctx")), len(bits("ctx")) + len(bits("fsdp"))
    crossing = [getattr(value, "crossing", None) for value in sums]
    units = [
        (value.rows, value.columns, value.begun, less, 0 if sent is None else sent.size)
        for value, less, sent in zip(sums, spared, crossing)
    ]
    tall = -(-vector.shape[0] // 1024) * 8
    small = jnp.pad(vector, (0, tall * 128 - vector.shape[0])).reshape(tall, 128)
    low = jnp.bfloat16
    scratch, sends, sources = [], links, []
    for value, leaving in zip(sums, crossing):
        state = value.state()
        sources += state
        if leaving is not None:
            sources.append(leaving)
            sends += 1
        scratch.append(pltpu.VMEM((value.rows, value.columns), low))
        scratch += len(state) * [pltpu.VMEM(state[0].shape, low)]
        if leaving is not None:
            scratch.append(pltpu.VMEM(leaving.shape, low))
        depth, width = state[0].shape
        for dim in value.splits[value.begun:]:
            depth, width = (depth // 2, width) if dim == 0 else (depth, width // 2)
            scratch.append(pltpu.VMEM((depth, width), low))
        sends += 2 * count - value.begun
    scratch = [
        pltpu.SemaphoreType.DMA((3 * len(units),)),
        pltpu.SemaphoreType.DMA((sends,)),
        pltpu.SemaphoreType.DMA((sends,)),
        pltpu.VMEM((links + 1, 16 + tall, 128), jnp.float32),
        pltpu.VMEM((links, 16 + tall, 128), jnp.float32),
    ] + scratch
    shapes = []
    for value, less in zip(sums, spared):
        rows, columns = value.rows, value.columns
        for dim in value.splits[:less]:
            rows, columns = (rows // 2, columns) if dim == 0 else (rows, columns // 2)
        shapes.append(jax.ShapeDtypeStruct((rows, columns), low))
    *results, total = pl.pallas_call(
        functools.partial(
            settle_kernel,
            units=units,
            splits=[value.splits for value in sums],
            starts=[getattr(value, "starts", None) for value in sums],
            given=[len(value.state()) + (sent is not None) for value, sent in zip(sums, crossing)],
            count=count,
        ),
        out_shape=shapes + [jax.ShapeDtypeStruct((16 + tall, 128), jnp.float32)],
        in_specs=[pl.BlockSpec(memory_space=pl.ANY) for _ in sources]
        + [pl.BlockSpec(memory_space=pltpu.VMEM)],
        out_specs=[pl.BlockSpec(memory_space=pl.ANY) for _ in units]
        + [pl.BlockSpec(memory_space=pltpu.VMEM)],
        scratch_shapes=scratch,
        cost_estimate=pl.CostEstimate(
            flops=0, bytes_accessed=64 * sum(unit[0] * unit[1] * 2 for unit in units), transcendentals=0
        ),
        compiler_params=pltpu.CompilerParams(
            collective_id=number, has_side_effects=True, vmem_limit_bytes=56 * 1024 * 1024
        ),
        name="settle",
    )(*sources, small)
    for index, (value, less) in enumerate(zip(sums, spared)):
        for bit in reversed(range(less)):
            other, dim = swap(results[index], "ctx", bit), value.splits[bit]
            results[index] = jnp.where(
                bit_of("ctx", bit) == 0,
                jnp.concatenate([results[index], other], axis=dim),
                jnp.concatenate([other, results[index]], axis=dim),
            )
    return results, jnp.sum(total[:16]), total[16:].reshape(-1)[: vector.shape[0]]


def gather_kernel(*refs, number, traded, widths, half_place):
    masters, rows_in = refs[:number], refs[number:number + traded]
    fulls, refs = refs[number + traded:2 * number + traded], refs[2 * number + traded:]
    rows_out, own = refs[:traded], refs[traded:traded + number]
    local_sem, send_sem, recv_sem, trade_sem = refs[traded + number:]
    group, place = lax.axis_index("fsdp"), lax.axis_index("ctx")
    core_bit, pair_bit, side = lax.rem(group, 2), lax.rem(group // 2, 2), lax.rem(place, 2)
    core, pair = group + 1 - 2 * core_bit, group + 2 - 4 * pair_bit
    partner = {"core": (core, place), "pair": (pair, place), "side": (group, place + 1 - 2 * side)}
    top = place // half_place
    trader = (core, place + half_place - 2 * half_place * top)
    trades = core_bit != top

    barrier = pltpu.get_barrier_semaphore()
    for other in partner.values():
        pl.semaphore_signal(barrier, inc=1, device_id=other, device_id_type=pl.DeviceIdType.MESH)

    def trading(which):
        return pltpu.make_async_remote_copy(
            src_ref=rows_in[which],
            dst_ref=rows_out[which],
            send_sem=trade_sem.at[which, 0],
            recv_sem=trade_sem.at[which, 1],
            device_id=trader,
            device_id_type=pl.DeviceIdType.MESH,
        )

    def keeping(which):
        return pltpu.make_async_copy(rows_in[which], rows_out[which], trade_sem.at[which, 2])

    @pl.when(trades)
    def _():
        pl.semaphore_signal(barrier, inc=1, device_id=trader, device_id_type=pl.DeviceIdType.MESH)
        pl.semaphore_wait(barrier, len(partner) + 1)
        for which in range(traded):
            trading(which).start()

    @pl.when(jnp.logical_not(trades))
    def _():
        pl.semaphore_wait(barrier, len(partner))
        for which in range(traded):
            keeping(which).start()

    sent = []

    def send(to, source, target):
        copy = pltpu.make_async_remote_copy(
            src_ref=source,
            dst_ref=target,
            send_sem=send_sem.at[len(sent)],
            recv_sem=recv_sem.at[len(sent)],
            device_id=partner[to],
            device_id_type=pl.DeviceIdType.MESH,
        )
        copy.start()
        sent.append(copy)
        return copy

    depth = own[0].shape[0]
    half = depth // 2
    rows = lambda start, count: pl.ds(pl.multiple_of(start, 16), count)

    def cast(index, start):
        def body(i, carry):
            here = rows(start + i * 16, 16)
            own[index][here, :] = masters[index][here, :].astype(jnp.bfloat16)
            return carry

        lax.fori_loop(0, half // 16, body, 0)

    pieces = [
        (index, slice(start, start + width))
        for index, width in enumerate(widths)
        for start in range(0, own[index].shape[1], width)
    ]
    mine, others = side * half, (1 - side) * half
    crossing = []
    for index in range(number):
        cast(index, mine)
        for piece, columns in pieces:
            if piece == index:
                crossing.append(
                    send(
                        "pair",
                        own[index].at[rows(mine, half), columns],
                        fulls[index].at[rows(group * depth + mine, half), columns],
                    )
                )
    local = []
    for index in range(number):
        cast(index, others)
        place_own = fulls[index].at[rows(group * depth, depth)]
        send("core", own[index], place_own)
        local.append(pltpu.make_async_copy(own[index], place_own, local_sem.at[index]))
        local[-1].start()
    passing = []
    for (index, columns), copy in zip(pieces, crossing):
        copy.wait_recv()
        here = fulls[index].at[rows(pair * depth + mine, half), columns]
        passing.append(send("side", here, here))
        send("core", here, here)
    last = []
    for (index, columns), copy in zip(pieces, passing):
        copy.wait_recv()
        here = fulls[index].at[rows(pair * depth + others, half), columns]
        last.append(send("core", here, here))
    for copy in sent:
        if all(copy is not other for other in crossing + passing):
            copy.wait_recv()

    @pl.when(trades)
    def _():
        for which in range(traded):
            trading(which).wait()

    @pl.when(jnp.logical_not(trades))
    def _():
        for which in range(traded):
            keeping(which).wait()

    for copy in sent:
        copy.wait_send()
    for copy in local:
        copy.wait()


def gather(masters, rows, number):
    widths = [next(w for w in (1280, master.shape[1]) if master.shape[1] % w == 0) for master in masters]
    count = len(masters)
    pieces = sum(master.shape[1] // width for master, width in zip(masters, widths))
    low, sends = jnp.bfloat16, 3 * pieces + pieces + count
    return pl.pallas_call(
        functools.partial(
            gather_kernel, number=count, traded=len(rows), widths=widths, half_place=lax.axis_size("ctx") // 2
        ),
        out_shape=[
            jax.ShapeDtypeStruct((value.shape[0] * lax.axis_size("fsdp"), value.shape[1]), low) for value in masters
        ]
        + [jax.ShapeDtypeStruct(value.shape, value.dtype) for value in rows],
        in_specs=[pl.BlockSpec(memory_space=pltpu.VMEM) for _ in masters]
        + [pl.BlockSpec(memory_space=pl.ANY) for _ in rows],
        out_specs=[pl.BlockSpec(memory_space=pl.ANY) for _ in masters + rows],
        scratch_shapes=[pltpu.VMEM(value.shape, low) for value in masters]
        + [
            pltpu.SemaphoreType.DMA((count,)),
            pltpu.SemaphoreType.DMA((sends,)),
            pltpu.SemaphoreType.DMA((sends,)),
            pltpu.SemaphoreType.DMA((len(rows), 3)),
        ],
        cost_estimate=pl.CostEstimate(
            flops=0, bytes_accessed=16 * sum(value.size * 4 for value in masters), transcendentals=0
        ),
        compiler_params=pltpu.CompilerParams(
            collective_id=number, has_side_effects=True, vmem_limit_bytes=56 * 1024 * 1024
        ),
        name="gather",
    )(*masters, *rows)


def gather_plain(master, *others):
    low = master.astype(jnp.bfloat16)
    return lax.all_gather(after(low, *others) if others else low, "fsdp", axis=0, tiled=True)


def gather_vector(vector):
    me, count = lax.axis_index("fsdp"), lax.axis_size("fsdp")
    low = vector.astype(jnp.bfloat16)
    by_distance = jnp.stack(
        [low]
        + [lax.ppermute(low, "fsdp", [(i, i ^ step) for i in range(count)]) for step in range(1, count)]
    )
    return jnp.concatenate(
        [lax.dynamic_index_in_dim(by_distance, me ^ shard, 0, keepdims=False) for shard in range(count)]
    )


def on_device(
    tokens,
    cotangent,
    lengths,
    widths,
    weight_qkv,
    moment_qkv,
    square_qkv,
    weight_out,
    moment_out,
    square_out,
    weight_up,
    moment_up,
    square_up,
    weight_down,
    moment_down,
    square_down,
    vectors,
    moment_vectors,
    square_vectors,
):
    ranks = lax.axis_size("ctx")
    core, top = bit_of("fsdp", 0), lax.axis_index("ctx") // (ranks // 2)
    here = core * (ranks // 2) + lax.rem(lax.axis_index("ctx"), ranks // 2)
    kept = core == top
    lengths, widths = [jnp.where(kept, value, swap(value, "fsdp", 0)) for value in (lengths, widths)]
    full_vector = gather_vector(vectors)
    if lax.axis_size("fsdp") == 4 and weight_qkv.shape[0] % 32 == 0 and weight_out.shape[0] % 32 == 0:
        full_qkv, full_out, own_tokens = gather(
            [weight_qkv, weight_out], [tokens.reshape(-1, tokens.shape[2])], 1
        )
    else:
        own_tokens = jnp.where(kept, tokens, trade(tokens))
        full_qkv, full_out = gather_plain(weight_qkv), gather_plain(weight_out)
    full_up = gather_plain(weight_up, full_out)
    full_down = gather_plain(weight_down, full_out)
    model_width = tokens.shape[2]
    hidden_units = full_up.shape[1]
    gain_one, shift_one, bias_qkv, bias_out, gain_two, shift_two, bias_up, bias_down = split_vector(
        full_vector.astype(jnp.float32), model_width, hidden_units
    )
    row_count = tokens.shape[0]
    slots_here = tokens.shape[1]
    slots_all = slots_here * lax.axis_size("ctx")
    token_count = row_count * slots_here
    local_heads = HEADS // ranks
    row_pos, col_pos, valid_slots, start_of, end_of = layout(lengths, widths, slots_all)
    valid_here = lax.dynamic_slice_in_dim(valid_slots, here * slots_here, slots_here, 1)
    cosine_table, sine_table = rotary_tables(by_block(row_pos, slots_here), by_block(col_pos, slots_here))
    cosine_here = lax.dynamic_index_in_dim(cosine_table, here, 0, keepdims=False)
    sine_here = lax.dynamic_index_in_dim(sine_table, here, 0, keepdims=False)
    low_high = jnp.stack([by_block(start_of, slots_here), by_block(end_of, slots_here)], axis=1)
    tile = slots_here * max(1, min(512 // slots_here, ranks))
    starts = start_of.reshape(row_count, slots_all // tile, tile)
    ends = end_of.reshape(row_count, slots_all // tile, tile)
    plain = (jnp.max(starts, axis=2) == 0) & (jnp.min(ends, axis=2) == slots_all)
    span = jnp.stack(
        [
            jnp.min(starts, axis=2) // tile,
            (jnp.max(ends, axis=2) + tile - 1) // tile,
            plain.astype(jnp.int32),
        ],
        axis=-1,
    ).astype(jnp.int32)
    flat_tokens = own_tokens.reshape(token_count, model_width).astype(jnp.float32)
    scaled_one, root_one = standardize(flat_tokens)
    first_normed = (scaled_one * gain_one + shift_one).astype(jnp.bfloat16)
    joined = (
        jnp.einsum("df,td->ft", full_qkv, first_normed, preferred_element_type=jnp.float32)
        + bias_qkv[:, None]
    )
    pairs = joined[: 2 * model_width].reshape(2, HEADS, 2, HEAD_DIM // 2, token_count)
    lower, upper_half = pairs[:, :, 0], pairs[:, :, 1]
    turned = jnp.stack(
        [lower * cosine_here - upper_half * sine_here, upper_half * cosine_here + lower * sine_here],
        axis=2,
    ).reshape(2 * model_width, token_count)
    heads_out = (
        jnp.concatenate([turned, joined[2 * model_width :]], axis=0)
        .astype(jnp.bfloat16)
        .reshape(3, local_heads, ranks, HEAD_DIM, token_count)
        .transpose(1, 2, 0, 3, 4)
    )
    heads_in = [exchange(heads_out[h]) for h in range(local_heads)]
    attended, lse, mixed = [], [], []
    for h in range(local_heads):
        result, stat = attend(span, heads_in[h], low_high)
        attended.append(result)
        lse.append(stat)
        mixed.append(exchange(result))
    came_cotangent = trade(after(cotangent, attended[0]))
    mixed = jnp.stack(mixed, axis=0).reshape(model_width, token_count)
    hidden = flat_tokens + jnp.einsum("it,io->to", mixed, full_out, preferred_element_type=jnp.float32) + bias_out
    scaled_two, root_two = standardize(hidden)
    second_normed = (scaled_two * gain_two + shift_two).astype(jnp.bfloat16)
    upper = jnp.dot(second_normed, full_up, preferred_element_type=jnp.float32) + bias_up
    sigma = jax.nn.sigmoid(1.702 * upper)
    active = (upper * sigma).astype(jnp.bfloat16)
    result = hidden + jnp.dot(active, full_down, preferred_element_type=jnp.float32) + bias_down
    output = result.astype(jnp.bfloat16).reshape(tokens.shape)
    own_cotangent = jnp.where(kept, cotangent, after(came_cotangent, active))
    grad_result = own_cotangent.reshape(token_count, model_width).astype(
        jnp.float32
    ) * valid_here.reshape(token_count, 1).astype(jnp.float32)
    grad_low = grad_result.astype(jnp.bfloat16)
    d_bias_down = jnp.sum(grad_result, axis=0)
    sum_down = Reduction(owner_order(active, 1), grad_low, "ti,to->io", 1)
    grad_low = after(grad_low, sum_down.leave())
    d_active = jnp.einsum("td,fd->tf", grad_low, full_down, preferred_element_type=jnp.float32)
    d_upper = (d_active * (sigma + 1.702 * upper * sigma * (1.0 - sigma))).astype(jnp.bfloat16)
    d_bias_up = jnp.sum(d_upper, axis=0, dtype=jnp.float32)
    d_upper = after(d_upper, sum_down.cross(d_upper))
    sum_up = Reduction(owner_order(second_normed, 1), d_upper, "ti,to->io", 1)
    d_upper = after(d_upper, sum_up.leave())
    d_second = jnp.einsum("tf,df->td", d_upper, full_up, preferred_element_type=jnp.float32)
    d_second = after(d_second, sum_up.cross(d_second))
    d_gain_two = jnp.sum(d_second * scaled_two, axis=0)
    d_shift_two = jnp.sum(d_second, axis=0)
    d_hidden = grad_result + norm_back(d_second, gain_two, scaled_two, root_two)
    d_branch = d_hidden.astype(jnp.bfloat16)
    d_bias_out = jnp.sum(d_branch, axis=0, dtype=jnp.float32)
    sum_out = Reduction(owner_order(mixed, 0), d_branch, "it,to->io", 0)
    d_branch = after(d_branch, sum_out.leave())
    d_mixed = (
        jnp.einsum("to,io->it", d_branch, full_out, preferred_element_type=jnp.float32)
        .astype(jnp.bfloat16)
        .reshape(local_heads, ranks, HEAD_DIM, token_count)
        .transpose(1, 0, 2, 3)
    )
    split = all(
        splits_of(value.shape[0], value.shape[1]) for value in (weight_qkv, weight_out, weight_up, weight_down)
    )
    came_mixed = exchange(d_mixed)
    d_attended = [came_mixed[:, h] for h in range(local_heads)]
    d_attended[0] = after(d_attended[0], sum_out.cross_later(d_mixed), output)
    normed_owners = owner_order(first_normed, 1)
    d_heads, sum_qkv = [], []
    for h in range(local_heads):
        d_heads.append(
            attend_back(
                span, heads_in[h], low_high, attended[h], d_attended[h], lse[h], cosine_table, sine_table
            )
        )
        if h == 0 and split:
            sent = sum_down.leave_ctx(d_heads[0])
            if local_heads > 1:
                d_attended[1] = after(d_attended[1], sent)
    backward = list(d_heads)
    for h in range(local_heads):
        came = after(exchange(d_heads[h]), backward[-1])
        if h > 0:
            sent = [sum_qkv[-1].leave()]
            sent.append(sum_qkv[-1].cross_pair(*sent))
            if split:
                sent.append(sum_down.leave_ctx(*sent))
                sent.append(sum_up.leave_ctx(*sent))
            came = after(came, *sent)
        d_heads[h] = came.transpose(1, 0, 2, 3)
        right = d_heads[h].reshape(3 * ranks * HEAD_DIM, token_count)
        sum_qkv.append(Reduction(normed_owners, right, "ti,ot->io", 1))
    last = sum_qkv[-1].leave()
    d_joined = jnp.stack(d_heads, axis=1).reshape(3 * model_width, token_count)
    d_joined = after(d_joined, last)
    d_bias_qkv = jnp.sum(d_joined, axis=1, dtype=jnp.float32)
    d_first = jnp.einsum("jt,dj->td", d_joined, full_qkv, preferred_element_type=jnp.float32)
    d_first = after(d_first, sum_qkv[-1].cross_pair(d_first, send=not split))
    d_gain_one = jnp.sum(d_first * scaled_one, axis=0)
    d_shift_one = jnp.sum(d_first, axis=0)
    input_grad = (d_hidden + norm_back(d_first, gain_one, scaled_one, root_one)).reshape(
        tokens.shape
    )
    low_grad = input_grad.astype(jnp.bfloat16)
    d_vectors = jnp.concatenate(
        [
            d_gain_one,
            d_shift_one,
            d_bias_qkv,
            d_bias_out,
            d_gain_two,
            d_shift_two,
            d_bias_up,
            d_bias_down,
        ]
    )
    if split:
        (grad_up, grad_qkv, grad_down, grad_outw), total_squares, total_vectors = settle(
            [sum_up, Joined(sum_qkv, 3), sum_down, sum_out], [0, 1, 0, 1], after(d_vectors, low_grad), 0
        )
    else:
        grad_down, grad_up, grad_qkv, grad_outw = [
            lax.psum(add_up(value.parts).astype(jnp.bfloat16), "ctx")
            for value in (sum_down, sum_up, Joined(sum_qkv, 3, False), sum_out)
        ]
        total_squares = lax.psum(
            functools.reduce(
                jnp.add,
                [
                    jnp.sum(jnp.square(grad.astype(jnp.float32)))
                    for grad in (grad_down, grad_up, grad_outw, grad_qkv)
                ],
            ),
            "fsdp",
        )
        total_vectors = lax.psum(d_vectors, EVERYWHERE)
    total_squares = total_squares + jnp.sum(jnp.square(total_vectors))
    grad_vectors = lax.dynamic_slice_in_dim(
        total_vectors, lax.axis_index("fsdp") * vectors.shape[0], vectors.shape[0], 0
    )
    grad_down, grad_up, grad_outw, grad_qkv = [
        grad.astype(jnp.float32) for grad in (grad_down, grad_up, grad_outw, grad_qkv)
    ]
    came_output = trade(after(output, total_squares))
    output = jnp.where(kept, output, came_output)
    came_grad = trade(after(low_grad, total_squares))
    input_grad = jnp.where(kept, input_grad, came_grad.astype(jnp.float32))
    grad_norm = jnp.sqrt(total_squares)
    factor = jnp.minimum(1.0, clip_level / grad_norm)
    new_qkv = adam_update(
        weight_qkv, moment_qkv, square_qkv, grad_qkv, factor, rate_matrix, decay_matrix
    )
    new_out = adam_update(
        weight_out, moment_out, square_out, grad_outw, factor, rate_matrix, decay_matrix
    )
    new_up = adam_update(
        weight_up, moment_up, square_up, grad_up, factor, rate_matrix, decay_matrix
    )
    new_down = adam_update(
        weight_down, moment_down, square_down, grad_down, factor, rate_matrix, decay_matrix
    )
    new_vec = adam_update(
        vectors, moment_vectors, square_vectors, grad_vectors, factor, rate_vector, 0.0
    )
    return (
        output,
        input_grad,
        grad_norm,
        new_qkv[0],
        new_qkv[1],
        new_qkv[2],
        new_out[0],
        new_out[1],
        new_out[2],
        new_up[0],
        new_up[1],
        new_up[2],
        new_down[0],
        new_down[1],
        new_down[2],
        new_vec[0],
        new_vec[1],
        new_vec[2],
    )


def solution(mesh):
    placed = (
        P("fsdp", "ctx", None),
        P("fsdp", "ctx", None),
        P("fsdp", None),
        P("fsdp", None),
        P("fsdp", None),
        P("fsdp", None),
        P("fsdp", None),
        P("fsdp", None),
        P("fsdp", None),
        P("fsdp", None),
        P("fsdp", None),
        P("fsdp", None),
        P("fsdp", None),
        P("fsdp", None),
        P("fsdp", None),
        P("fsdp", None),
        P("fsdp"),
        P("fsdp"),
        P("fsdp"),
    )
    return jax.shard_map(
        on_device,
        mesh=mesh,
        in_specs=placed,
        out_specs=(
            P("fsdp", "ctx", None),
            P("fsdp", "ctx", None),
            P(),
            P("fsdp", None),
            P("fsdp", None),
            P("fsdp", None),
            P("fsdp", None),
            P("fsdp", None),
            P("fsdp", None),
            P("fsdp", None),
            P("fsdp", None),
            P("fsdp", None),
            P("fsdp", None),
            P("fsdp", None),
            P("fsdp", None),
            P("fsdp"),
            P("fsdp"),
            P("fsdp"),
        ),
        check_vma=False,
    )
```

```python
import functools

import jax
import jax.numpy as jnp
from jax import lax
from jax.experimental import pallas as pl
from jax.experimental.pallas import tpu as pltpu
from jax.sharding import PartitionSpec as P

HEADS = 16
HEAD_DIM = 80
STEP = 5


eps_norm = 1e-06
beta_one = 0.9
beta_two = 0.999
adam_eps = 1e-08
decay_matrix = 0.05
rate_matrix = 0.04
rate_vector = 0.3
clip_level = 1.0


LOG2E = 1.4426950408889634


EVERYWHERE = ("fsdp", "ctx")


def device(pair, core, top, low):
    half = lax.axis_size("ctx") // 2
    return ((pair * 2 + core) * 2 + top) * half + low


def trade(value):
    pairs = []
    for pair in range(lax.axis_size("fsdp") // 2):
        for low in range(lax.axis_size("ctx") // 2):
            one, other = device(pair, 1, 0, low), device(pair, 0, 1, low)
            pairs += [(one, other), (other, one)]
    return lax.ppermute(value, EVERYWHERE, pairs)


def exchange(source):
    groups = [
        [device(pair, core, top, low) for core in range(2) for low in range(lax.axis_size("ctx") // 2)]
        for pair in range(lax.axis_size("fsdp") // 2)
        for top in range(2)
    ]
    return lax.all_to_all(source, EVERYWHERE, 0, 0, axis_index_groups=groups)


def after(value, *others):
    return lax.optimization_barrier((value,) + others)[0]


def attend_kernel(span, qkv, low_high, out, stat, keys, values, *, size, tile, extent, step_size):
    row, place = pl.program_id(0), pl.program_id(1)
    blocks = extent // size
    group = tile // size
    scale = HEAD_DIM ** (-0.5) * LOG2E

    @pl.when(place == 0)
    def _():
        for b in range(blocks):
            keys[b * size:(b + 1) * size, :] = qkv[b, 1].T
            values[:, b * size:(b + 1) * size] = qkv[b, 2]

    first, last, plain = span[row, place, 0], span[row, place, 1], span[row, place, 2]
    query = jnp.concatenate([qkv[place * group + i, 0] for i in range(group)], axis=1)

    def finish(peak, total, mixed):
        mixed = (mixed / total).astype(jnp.bfloat16)
        lse = peak + jnp.log2(total)
        for i in range(group):
            out[i] = mixed[:, i * size:(i + 1) * size]
            stat[i] = lse[:, i * size:(i + 1) * size]

    def step(start, carry, keep=None):
        peak, total, mixed = carry
        s = jnp.dot(keys[pl.ds(start, step_size), :], query, preferred_element_type=jnp.float32) * scale
        if keep is not None:
            s = jnp.where(keep, s, -1e30)
        top = jnp.maximum(peak, jnp.max(s, axis=0, keepdims=True))
        fade = jnp.exp2(peak - top)
        raised = jnp.exp2(s - top)
        total = total * fade + jnp.sum(raised, axis=0, keepdims=True)
        mixed = mixed * fade + jnp.dot(values[:, pl.ds(start, step_size)], raised.astype(jnp.bfloat16),
                                       preferred_element_type=jnp.float32)
        return top, total, mixed

    begin = (
        jnp.full((1, tile), -1e30, jnp.float32),
        jnp.zeros((1, tile), jnp.float32),
        jnp.zeros((HEAD_DIM, tile), jnp.float32),
    )

    @pl.when(plain == 1)
    def _():
        carry = begin
        for b in range(extent // step_size):
            carry = step(b * step_size, carry)
        finish(*carry)

    @pl.when(plain == 0)
    def _():
        low = jnp.concatenate([low_high[i, 0:1, :] for i in range(group)], axis=1)
        high = jnp.concatenate([low_high[i, 1:2, :] for i in range(group)], axis=1)

        def masked(b, carry):
            start = pl.multiple_of(b * step_size, step_size)
            places = lax.broadcasted_iota(jnp.int32, (step_size, tile), 0) + start
            return step(start, carry, (places >= low) & (places < high))

        finish(*lax.fori_loop(first, last, masked, begin))


def attend(span, qkv, low_high):
    blocks, _, width, lanes = qkv.shape
    rows = span.shape[0]
    size = lanes // rows
    group = blocks // span.shape[1]
    tile = group * size
    grid_spec = pltpu.PrefetchScalarGridSpec(
        num_scalar_prefetch=1,
        grid=(rows, blocks // group),
        in_specs=[
            pl.BlockSpec((blocks, 3, width, size), lambda r, b, s: (0, 0, 0, r)),
            pl.BlockSpec((group, 2, size), lambda r, b, s: (b, 0, r)),
        ],
        out_specs=[
            pl.BlockSpec((group, width, size), lambda r, b, s: (b, 0, r)),
            pl.BlockSpec((group, 1, size), lambda r, b, s: (b, 0, r)),
        ],
        scratch_shapes=[pltpu.VMEM((blocks * size, HEAD_DIM), jnp.bfloat16), pltpu.VMEM((HEAD_DIM, blocks * size), jnp.bfloat16)],
    )
    return pl.pallas_call(
        functools.partial(attend_kernel, size=size, tile=tile, extent=blocks * size, step_size=tile),
        grid_spec=grid_spec,
        out_shape=[
            jax.ShapeDtypeStruct((blocks, width, lanes), jnp.bfloat16),
            jax.ShapeDtypeStruct((blocks, 1, lanes), jnp.float32),
        ],
        cost_estimate=pl.CostEstimate(
            flops=4 * rows * (blocks * size) ** 2 * 256,
            bytes_accessed=5 * blocks * width * lanes * 2,
            transcendentals=rows * (blocks * size) ** 2,
        ),
        compiler_params=pltpu.CompilerParams(vmem_limit_bytes=48 * 1024 * 1024),
        name="attend",
    )(span, qkv, low_high)


def attend_back_kernel(span, qkv, low_high, mixed, d_mixed, stat, cosine, sine, out, keys, values, keys_t, d_keys, d_values,
                       *, size, tile, extent, step_size):
    row, place = pl.program_id(0), pl.program_id(1)
    blocks = extent // size
    group = tile // size
    scale = HEAD_DIM ** (-0.5)
    half = HEAD_DIM // 2

    @pl.when(place == 0)
    def _():
        d_keys[...] = jnp.zeros_like(d_keys)
        d_values[...] = jnp.zeros_like(d_values)
        for b in range(blocks):
            keys[b * size:(b + 1) * size, :] = qkv[b, 1].T
            values[b * size:(b + 1) * size, :] = qkv[b, 2].T
            keys_t[:, b * size:(b + 1) * size] = qkv[b, 1]

    def turn_back(v, cos, sin):
        upper, lower = v[half:], v[:half]
        return jnp.concatenate([lower * cos + upper * sin, upper * cos - lower * sin], axis=0)

    side = lambda parts: jnp.concatenate(parts, axis=1)
    first, last, plain = span[row, place, 0], span[row, place, 1], span[row, place, 2]
    query = side([qkv[place * group + i, 0] for i in range(group)])
    grad = side([d_mixed[i] for i in range(group)])
    query_n, grad_n = query.T, grad.T
    delta = jnp.sum(grad.astype(jnp.float32) * side([mixed[i] for i in range(group)]).astype(jnp.float32), axis=0, keepdims=True)
    lse = side([stat[i] for i in range(group)])

    def step(start, d_query, keep=None):
        here = pl.ds(start, step_size)
        s = jnp.dot(keys[here, :], query, preferred_element_type=jnp.float32)
        d_probs = jnp.dot(values[here, :], grad, preferred_element_type=jnp.float32)
        exact = jnp.exp2(s * (scale * LOG2E) - lse)
        if keep is not None:
            exact = jnp.where(keep, exact, 0.0)
        d_scores = (exact * (d_probs - delta)).astype(jnp.bfloat16)
        d_values[here, :] += jnp.dot(exact.astype(jnp.bfloat16), grad_n, preferred_element_type=jnp.float32)
        d_keys[here, :] += jnp.dot(d_scores, query_n, preferred_element_type=jnp.float32)
        return d_query + jnp.dot(keys_t[:, here], d_scores, preferred_element_type=jnp.float32)

    def finish(d_query):
        for i in range(group):
            b = place * group + i
            out[b, 0] = turn_back(d_query[:, i * size:(i + 1) * size] * scale, cosine[b], sine[b]).astype(jnp.bfloat16)

    begin = jnp.zeros((HEAD_DIM, tile), jnp.float32)

    @pl.when(plain == 1)
    def _():
        d_query = begin
        for b in range(extent // step_size):
            d_query = step(b * step_size, d_query)
        finish(d_query)

    @pl.when(plain == 0)
    def _():
        low = side([low_high[i, 0:1, :] for i in range(group)])
        high = side([low_high[i, 1:2, :] for i in range(group)])

        def masked(b, d_query):
            start = pl.multiple_of(b * step_size, step_size)
            places = lax.broadcasted_iota(jnp.int32, (step_size, tile), 0) + start
            return step(start, d_query, (places >= low) & (places < high))

        finish(lax.fori_loop(first, last, masked, begin))

    @pl.when(place == blocks // group - 1)
    def _():
        for b in range(blocks):
            here = slice(b * size, (b + 1) * size)
            out[b, 1] = turn_back(d_keys[here, :].T * scale, cosine[b], sine[b]).astype(jnp.bfloat16)
            out[b, 2] = d_values[here, :].T.astype(jnp.bfloat16)


def attend_back(span, qkv, low_high, mixed, d_mixed, stat, cosine, sine):
    blocks, _, width, lanes = qkv.shape
    rows = span.shape[0]
    size = lanes // rows
    group = blocks // span.shape[1]
    tile = group * size
    per = lambda r, b, s: (b, 0, r)
    whole = lambda r, b, s: (0, 0, r)
    grid_spec = pltpu.PrefetchScalarGridSpec(
        num_scalar_prefetch=1,
        grid=(rows, blocks // group),
        in_specs=[
            pl.BlockSpec((blocks, 3, width, size), lambda r, b, s: (0, 0, 0, r)),
            pl.BlockSpec((group, 2, size), per),
            pl.BlockSpec((group, width, size), per),
            pl.BlockSpec((group, width, size), per),
            pl.BlockSpec((group, 1, size), per),
            pl.BlockSpec((blocks, HEAD_DIM // 2, size), whole),
            pl.BlockSpec((blocks, HEAD_DIM // 2, size), whole),
        ],
        out_specs=pl.BlockSpec((blocks, 3, width, size), lambda r, b, s: (0, 0, 0, r)),
        scratch_shapes=[
            pltpu.VMEM((blocks * size, HEAD_DIM), jnp.bfloat16),
            pltpu.VMEM((blocks * size, HEAD_DIM), jnp.bfloat16),
            pltpu.VMEM((HEAD_DIM, blocks * size), jnp.bfloat16),
            pltpu.VMEM((blocks * size, HEAD_DIM), jnp.float32),
            pltpu.VMEM((blocks * size, HEAD_DIM), jnp.float32),
        ],
    )
    return pl.pallas_call(
        functools.partial(attend_back_kernel, size=size, tile=tile, extent=blocks * size, step_size=tile),
        grid_spec=grid_spec,
        out_shape=jax.ShapeDtypeStruct(qkv.shape, jnp.bfloat16),
        cost_estimate=pl.CostEstimate(
            flops=10 * rows * (blocks * size) ** 2 * 256,
            bytes_accessed=10 * blocks * width * lanes * 2,
            transcendentals=rows * (blocks * size) ** 2,
        ),
        compiler_params=pltpu.CompilerParams(vmem_limit_bytes=56 * 1024 * 1024),
        name="attend_back",
    )(span, qkv, low_high, mixed, d_mixed, stat, cosine, sine)


def layout(lengths, widths, extent):
    piece_ends = jnp.cumsum(lengths, axis=1)
    piece_starts = piece_ends - lengths
    places = jnp.arange(extent, dtype=jnp.int32)[None, :, None]
    inside = (places >= piece_starts[:, None, :]) & (places < piece_ends[:, None, :])
    pick = lambda table: jnp.sum(jnp.where(inside, table[:, None, :], 0), axis=2)
    filled = piece_ends[:, -1:]
    valid = places[..., 0] < filled
    start_of = jnp.where(valid, pick(piece_starts), filled)
    end_of = jnp.where(valid, pick(piece_ends), extent)
    width_of = jnp.where(valid, pick(widths), 1)
    within = places[..., 0] - start_of
    return within // width_of, within % width_of, valid, start_of, end_of


def by_block(table, size):
    rows, extent = table.shape
    return table.reshape(rows, extent // size, size).transpose(1, 0, 2).reshape(extent // size, rows * size)


def rotary_tables(row_pos, col_pos):
    quarter = HEAD_DIM // 4
    inverse = 10000.0 ** (-(2.0 * jnp.arange(quarter, dtype=jnp.float32)) / (HEAD_DIM // 2))
    angles = jnp.concatenate(
        [
            row_pos.astype(jnp.float32)[:, None, :] * inverse[None, :, None],
            col_pos.astype(jnp.float32)[:, None, :] * inverse[None, :, None],
        ],
        axis=1,
    )
    return (jnp.cos(angles), jnp.sin(angles))


def split_vector(vector, width, hidden_units):
    return (
        vector[:width],
        vector[width : 2 * width],
        vector[2 * width : 5 * width],
        vector[5 * width : 6 * width],
        vector[6 * width : 7 * width],
        vector[7 * width : 8 * width],
        vector[8 * width : 8 * width + hidden_units],
        vector[8 * width + hidden_units :],
    )


def standardize(inputs):
    center = inputs - jnp.mean(inputs, axis=-1, keepdims=True)
    root_inverse = lax.rsqrt(jnp.mean(center * center, axis=-1, keepdims=True) + eps_norm)
    return (center * root_inverse, root_inverse)


def norm_back(d_norm, gain_vector, scaled, root_inverse):
    effect = d_norm * gain_vector
    inner = jnp.mean(effect, axis=-1, keepdims=True)
    along = jnp.mean(effect * scaled, axis=-1, keepdims=True)
    return root_inverse * (effect - inner - scaled * along)


def adam_update(weight, moment, square, grad, factor, rate, decay):
    clipped = grad * factor
    moment = beta_one * moment + (1.0 - beta_one) * clipped
    square = beta_two * square + (1.0 - beta_two) * clipped * clipped
    fixed_moment = moment / (1.0 - beta_one**STEP)
    fixed_square = square / (1.0 - beta_two**STEP)
    weight = weight - rate * (fixed_moment / (jnp.sqrt(fixed_square) + adam_eps) + decay * weight)
    return (weight, moment, square)


def swap(value, axis, bit):
    count = lax.axis_size(axis)
    return lax.ppermute(value, axis, [(i, i ^ (1 << bit)) for i in range(count)])


def bit_of(axis, bit):
    return lax.rem(lax.axis_index(axis) // (1 << bit), 2)


def bits(axis):
    return range(lax.axis_size(axis).bit_length() - 1)


def owner_order(value, dim):
    count = lax.axis_size("fsdp")
    depth = value.shape[dim] // count
    core = bit_of("fsdp", 0)
    return jnp.concatenate(
        [
            lax.dynamic_slice_in_dim(value, (2 * pair + side) * depth, depth, dim)
            for side in (1 - core, core)
            for pair in range(count // 2)
        ],
        axis=dim,
    )


def add_up(parts):
    return functools.reduce(jnp.add, [part.astype(jnp.float32) for part in parts])


class Reduction:
    def __init__(self, left, right, form, dim):
        self.left, self.right, self.form, self.dim = left, right, form, dim
        self.total = left.shape[dim]
        self.rows = self.total // lax.axis_size("fsdp")
        self.columns = right.shape[0 if form[3] == "o" else 1]
        self.splits = splits_of(self.rows, self.columns)
        self.begun = 0

    def product(self, start, stop, *others):
        left = after(self.left, *others) if others else self.left
        return jnp.einsum(
            self.form,
            lax.slice_in_dim(left, start, stop, axis=self.dim),
            self.right,
            preferred_element_type=jnp.float32,
        )

    def leave(self):
        sent = self.product(0, self.total // 2).astype(jnp.bfloat16)
        self.came = swap(sent, "fsdp", 0)
        return sent

    def cross(self, *others):
        came = after(self.came, *others) if others else self.came
        kept = add_up([self.product(self.total // 2, self.total, *others), came]).astype(jnp.bfloat16)
        pairs, places = lax.axis_size("fsdp") // 2, lax.axis_size("ctx")
        wide = self.splits is not None and self.splits[0] == 0
        step = 2 if wide else 1
        groups = [
            [(2 * pair + core) * places + place + bit for pair in range(pairs) for bit in range(step)]
            for core in range(2)
            for place in range(0, places, step)
        ]
        self.parts = [
            lax.psum_scatter(kept, EVERYWHERE, scatter_dimension=0, tiled=True, axis_index_groups=groups)
        ]
        self.begun = step - 1
        return kept

    def cross_later(self, *others):
        if lax.axis_size("fsdp") != 4 or self.splits is None:
            return self.cross(*others)
        came = after(self.came, *others) if others else self.came
        kept = add_up([self.product(self.total // 2, self.total), came]).astype(jnp.bfloat16)
        mine = bit_of("fsdp", 1) * self.rows
        self.parts = [lax.dynamic_slice_in_dim(kept, mine, self.rows, 0)]
        self.crossing = lax.dynamic_slice_in_dim(kept, self.rows - mine, self.rows, 0)
        self.starts = [0]
        return kept

    def cross_pair(self, *others, send=True):
        if lax.axis_size("fsdp") != 4:
            return self.cross(*others)
        came = after(self.came, *others) if others else self.came
        mine = bit_of("fsdp", 1) * self.rows
        theirs = self.rows - mine
        pick = lambda start: add_up(
            [
                jnp.einsum(
                    self.form,
                    lax.dynamic_slice_in_dim(self.left, self.total // 2 + start, self.rows, self.dim),
                    self.right,
                    preferred_element_type=jnp.float32,
                ),
                lax.dynamic_slice_in_dim(came, start, self.rows, 0),
            ]
        ).astype(jnp.bfloat16)
        sent = pick(theirs)
        self.parts = [pick(mine), swap(sent, "fsdp", 1) if send else sent]
        return sent

    def leave_ctx(self, *others):
        if others:
            self.parts[-1] = after(self.parts[-1], *others)
        dim = self.splits[self.begun]
        half = self.parts[0].shape[dim] // 2
        mine = bit_of("ctx", self.begun)
        pick = lambda side: [lax.dynamic_slice_in_dim(part, side * half, half, dim) for part in self.parts]
        sent = add_up(pick(1 - mine)).astype(jnp.bfloat16)
        own = add_up(pick(mine)).astype(jnp.bfloat16)
        self.parts = [own, swap(sent, "ctx", self.begun)]
        self.begun += 1
        return sent

    def state(self):
        return self.parts


class Joined:
    def __init__(self, sums, blocks, crosses=True):
        width = sums[0].columns // blocks
        self.rows, self.columns = sums[0].rows, sums[0].columns * len(sums)
        self.splits = splits_of(self.rows, self.columns)
        self.begun = sums[0].begun
        whole = [add_up(value.parts).astype(jnp.bfloat16) for value in sums]
        if crosses:
            whole[-1] = sums[-1].parts[0]
        self.parts = [
            jnp.concatenate(
                [value[:, b * width : (b + 1) * width] for b in range(blocks) for value in whole], axis=1
            )
        ]
        self.crossing = sums[-1].parts[1] if crosses and len(sums[-1].parts) > 1 else None
        self.starts = [(b * len(sums) + len(sums) - 1) * width for b in range(blocks)]

    def state(self):
        return self.parts


def splits_of(rows, columns):
    dims = []
    for _ in bits("ctx"):
        if rows % 32 == 0:
            rows //= 2
            dims.append(0)
        elif columns % 256 == 0:
            columns //= 2
            dims.append(1)
        else:
            return None
    return dims


def plan(units, count):
    links, done, ready = {}, [], []

    def loads(bit, size):
        if bit < 2:
            return {bit: size}
        return {1: size, bit: size * 2 ** (bit - 1)}

    for unit, (rows, columns, begun, spared, crossing) in enumerate(units):
        phases = [loads(bit, rows * columns / 2 ** (bit + 1)) for bit in range(count)]
        phases = phases + phases[::-1][: count - spared] + [{"x": crossing}]
        ready.append((0.0, unit, begun - 1 if crossing else begun, phases))
    start = lambda item: max([item[0]] + [links.get(link, 0.0) for link in item[3][item[2]]])
    while ready:
        ready.sort(key=lambda item: (start(item), item[1]))
        item = ready.pop(0)
        _, unit, phase, phases = item
        begin = start(item)
        for link, size in phases[phase].items():
            links[link] = begin + size
        end = begin + max(phases[phase].values()) + 20000
        done.append((end, unit, phase))
        if phase + 2 < len(phases):
            ready.append((end, unit, phase + 1, phases))
    return [(unit, phase) for _, unit, phase in sorted(done)]


def settle_kernel(*refs, units, splits, starts, given, count):
    number = len(units)
    arrays = sum(given)
    sources, small, targets, total = (
        list(refs[:arrays]), refs[arrays], refs[arrays + 1:arrays + 1 + number], refs[arrays + 1 + number]
    )
    scratch = list(refs[arrays + 2 + number:])
    take = lambda wanted: [scratch.pop(0) for _ in range(wanted)]
    group, place = lax.axis_index("fsdp"), lax.axis_index("ctx")
    group_bit = [lax.rem(group // 2**b, 2) for b in bits("fsdp")]
    place_bit = [lax.rem(place // 2**b, 2) for b in range(count)]
    partner = {("ctx", b): (group, place + (1 - 2 * place_bit[b]) * 2**b) for b in range(count)}
    partner.update({("fsdp", b): (group + (1 - 2 * bit) * 2**b, place) for b, bit in enumerate(group_bit)})

    barrier = pltpu.get_barrier_semaphore()
    for other in partner.values():
        pl.semaphore_signal(barrier, inc=1, device_id=other, device_id_type=pl.DeviceIdType.MESH)
    pl.semaphore_wait(barrier, len(partner))

    local_sem, send_sem, recv_sem, squares, from_others = take(5)
    sent, local = [], [0]

    def send(link, source, target):
        copy = pltpu.make_async_remote_copy(
            src_ref=source,
            dst_ref=target,
            send_sem=send_sem.at[len(sent)],
            recv_sem=recv_sem.at[len(sent)],
            device_id=partner[link],
            device_id_type=pl.DeviceIdType.MESH,
        )
        copy.start()
        sent.append(copy)
        return copy

    def move(source, target):
        copy = pltpu.make_async_copy(source, target, local_sem.at[local[0]])
        local[0] += 1
        copy.start()
        return copy

    def part(ref, row, rows, column, columns):
        if columns == ref.shape[1]:
            return ref.at[pl.ds(pl.multiple_of(row, 16), rows)]
        return ref.at[pl.ds(pl.multiple_of(row, 16), rows), pl.ds(pl.multiple_of(column, 128), columns)]

    def add(left, right, target, measure=False):
        def body(i, held):
            here = pl.ds(pl.multiple_of(i * 16, 16), 16)
            value = left[here, :]
            if right is not None:
                value = (value.astype(jnp.float32) + right[here, :].astype(jnp.float32)).astype(jnp.bfloat16)
            target[here, :] = value
            if measure:
                value = value.astype(jnp.float32)
                for tile in range(value.shape[1] // 128):
                    piece = value[:, tile * 128:(tile + 1) * 128]
                    held = held + piece * piece
            return held

        held = lax.fori_loop(0, left.shape[0] // 16, body, jnp.zeros((16, 128), jnp.float32))
        if measure:
            squares[0, 0:16] = squares[0, 0:16] + held

    class Unit:
        pass

    states = []
    for index, (rows, columns, begun, spared, crossing) in enumerate(units):
        unit = Unit()
        unit.begun, unit.target, unit.dims, unit.starts = begun, targets[index], splits[index], starts[index]
        unit.spared = spared
        unit.region = [(0, rows, 0, columns)]
        for bit in range(count):
            row, depth, column, width = unit.region[-1]
            if unit.dims[bit] == 0:
                depth //= 2
                row = row + place_bit[bit] * depth
            else:
                width //= 2
                column = column + place_bit[bit] * width
            unit.region.append((row, depth, column, width))
        unit.final, unit.held = take(2)
        unit.came = take(1)[0] if given[index] == 2 else None
        unit.taken = [None] * begun + take(count - begun)
        unit.loads = [move(sources.pop(0), unit.held)]
        unit.crossing = crossing > 0
        if unit.crossing:
            unit.copy = send(("fsdp", 1), sources.pop(0), unit.came)
        elif unit.came is not None:
            unit.loads.append(move(sources.pop(0), unit.came))
        states.append(unit)

    def halves(unit, ref, bit):
        depth, width = ref.shape
        if unit.dims[bit] == 0:
            depth //= 2
            pick = lambda side: part(ref, side * depth, depth, 0, width)
        else:
            width //= 2
            pick = lambda side: part(ref, 0, depth, side * width, width)
        return pick(place_bit[bit]), pick(1 - place_bit[bit])

    def proceed(unit, bit, ref):
        unit.kept, leaving = halves(unit, ref, bit)
        unit.copy = send(("ctx", bit), leaving, unit.taken[bit])

    def hand_out(unit, bit):
        region = part(unit.final, *unit.region[bit + 1])
        unit.copy = send(("ctx", bit), region, region)

    left = [number]

    def settled(unit, own, came):
        add(own, came, part(unit.final, *unit.region[count]), measure=True)
        left[0] -= 1
        hand_out(unit, count - 1)

    def advance(unit, phase):
        unit.copy.wait_recv()
        if phase < unit.begun:
            width = unit.came.shape[1] // len(unit.starts)
            for block, start in enumerate(unit.starts):
                here = part(unit.held, 0, unit.held.shape[0], start, width)
                add(here, part(unit.came, 0, unit.came.shape[0], block * width, width), here)
            proceed(unit, unit.begun, unit.held)
        elif phase < count - 1:
            add(unit.kept, unit.taken[phase], unit.taken[phase])
            proceed(unit, phase + 1, unit.taken[phase])
        elif phase == count - 1:
            settled(unit, unit.kept, unit.taken[phase])
        elif phase < 2 * count - 1 - unit.spared:
            hand_out(unit, 2 * count - 2 - phase)
        else:
            unit.store = move(part(unit.final, *unit.region[unit.spared]), unit.target)

    squared, squares_copy = [-1], [None]

    def exchange_squares():
        step = squared[0] = squared[0] + 1
        if step > 0:
            squares_copy[0].wait_recv()
            squares[step] = squares[step - 1] + from_others[step - 1]
        if step < len(partner):
            squares_copy[0] = send(list(partner)[step], squares.at[step], from_others.at[step])

    squares[0, 0:16] = jnp.zeros((16, 128), jnp.float32)
    squares[0, 16:] = small[...]
    for unit in states:
        for load in unit.loads:
            load.wait()
        if unit.crossing:
            continue
        if unit.begun < count:
            if unit.came is not None:
                add(unit.held, unit.came, unit.held)
            proceed(unit, unit.begun, unit.held)
        else:
            settled(unit, unit.held, unit.came)
    for index, phase in plan(units, count):
        advance(states[index], phase)
        if left[0] == 0 and squared[0] < len(partner):
            exchange_squares()
    while squared[0] < len(partner):
        exchange_squares()
    total[...] = squares[len(partner)]
    for copy in sent:
        copy.wait_send()
    for unit in states:
        unit.store.wait()


def settle(sums, spared, vector, number):
    count, links = len(bits("ctx")), len(bits("ctx")) + len(bits("fsdp"))
    crossing = [getattr(value, "crossing", None) for value in sums]
    units = [
        (value.rows, value.columns, value.begun, less, 0 if sent is None else sent.size)
        for value, less, sent in zip(sums, spared, crossing)
    ]
    tall = -(-vector.shape[0] // 1024) * 8
    small = jnp.pad(vector, (0, tall * 128 - vector.shape[0])).reshape(tall, 128)
    low = jnp.bfloat16
    scratch, sends, sources = [], links, []
    for value, leaving in zip(sums, crossing):
        state = value.state()
        sources += state
        if leaving is not None:
            sources.append(leaving)
            sends += 1
        scratch.append(pltpu.VMEM((value.rows, value.columns), low))
        scratch += len(state) * [pltpu.VMEM(state[0].shape, low)]
        if leaving is not None:
            scratch.append(pltpu.VMEM(leaving.shape, low))
        depth, width = state[0].shape
        for dim in value.splits[value.begun:]:
            depth, width = (depth // 2, width) if dim == 0 else (depth, width // 2)
            scratch.append(pltpu.VMEM((depth, width), low))
        sends += 2 * count - value.begun
    scratch = [
        pltpu.SemaphoreType.DMA((3 * len(units),)),
        pltpu.SemaphoreType.DMA((sends,)),
        pltpu.SemaphoreType.DMA((sends,)),
        pltpu.VMEM((links + 1, 16 + tall, 128), jnp.float32),
        pltpu.VMEM((links, 16 + tall, 128), jnp.float32),
    ] + scratch
    shapes = []
    for value, less in zip(sums, spared):
        rows, columns = value.rows, value.columns
        for dim in value.splits[:less]:
            rows, columns = (rows // 2, columns) if dim == 0 else (rows, columns // 2)
        shapes.append(jax.ShapeDtypeStruct((rows, columns), low))
    *results, total = pl.pallas_call(
        functools.partial(
            settle_kernel,
            units=units,
            splits=[value.splits for value in sums],
            starts=[getattr(value, "starts", None) for value in sums],
            given=[len(value.state()) + (sent is not None) for value, sent in zip(sums, crossing)],
            count=count,
        ),
        out_shape=shapes + [jax.ShapeDtypeStruct((16 + tall, 128), jnp.float32)],
        in_specs=[pl.BlockSpec(memory_space=pl.ANY) for _ in sources]
        + [pl.BlockSpec(memory_space=pltpu.VMEM)],
        out_specs=[pl.BlockSpec(memory_space=pl.ANY) for _ in units]
        + [pl.BlockSpec(memory_space=pltpu.VMEM)],
        scratch_shapes=scratch,
        cost_estimate=pl.CostEstimate(
            flops=0, bytes_accessed=64 * sum(unit[0] * unit[1] * 2 for unit in units), transcendentals=0
        ),
        compiler_params=pltpu.CompilerParams(
            collective_id=number, has_side_effects=True, vmem_limit_bytes=56 * 1024 * 1024
        ),
        name="settle",
    )(*sources, small)
    for index, (value, less) in enumerate(zip(sums, spared)):
        for bit in reversed(range(less)):
            other, dim = swap(results[index], "ctx", bit), value.splits[bit]
            results[index] = jnp.where(
                bit_of("ctx", bit) == 0,
                jnp.concatenate([results[index], other], axis=dim),
                jnp.concatenate([other, results[index]], axis=dim),
            )
    return results, jnp.sum(total[:16]), total[16:].reshape(-1)[: vector.shape[0]]


def gather_kernel(*refs, number, traded, widths, half_place):
    masters, rows_in = refs[:number], refs[number:number + traded]
    fulls, refs = refs[number + traded:2 * number + traded], refs[2 * number + traded:]
    rows_out, own = refs[:traded], refs[traded:traded + number]
    local_sem, send_sem, recv_sem, trade_sem = refs[traded + number:]
    group, place = lax.axis_index("fsdp"), lax.axis_index("ctx")
    core_bit, pair_bit, side = lax.rem(group, 2), lax.rem(group // 2, 2), lax.rem(place, 2)
    core, pair = group + 1 - 2 * core_bit, group + 2 - 4 * pair_bit
    partner = {"core": (core, place), "pair": (pair, place), "side": (group, place + 1 - 2 * side)}
    top = place // half_place
    trader = (core, place + half_place - 2 * half_place * top)
    trades = core_bit != top

    barrier = pltpu.get_barrier_semaphore()
    for other in partner.values():
        pl.semaphore_signal(barrier, inc=1, device_id=other, device_id_type=pl.DeviceIdType.MESH)

    def trading(which):
        return pltpu.make_async_remote_copy(
            src_ref=rows_in[which],
            dst_ref=rows_out[which],
            send_sem=trade_sem.at[which, 0],
            recv_sem=trade_sem.at[which, 1],
            device_id=trader,
            device_id_type=pl.DeviceIdType.MESH,
        )

    def keeping(which):
        return pltpu.make_async_copy(rows_in[which], rows_out[which], trade_sem.at[which, 2])

    @pl.when(trades)
    def _():
        pl.semaphore_signal(barrier, inc=1, device_id=trader, device_id_type=pl.DeviceIdType.MESH)
        pl.semaphore_wait(barrier, len(partner) + 1)
        for which in range(traded):
            trading(which).start()

    @pl.when(jnp.logical_not(trades))
    def _():
        pl.semaphore_wait(barrier, len(partner))
        for which in range(traded):
            keeping(which).start()

    sent = []

    def send(to, source, target):
        copy = pltpu.make_async_remote_copy(
            src_ref=source,
            dst_ref=target,
            send_sem=send_sem.at[len(sent)],
            recv_sem=recv_sem.at[len(sent)],
            device_id=partner[to],
            device_id_type=pl.DeviceIdType.MESH,
        )
        copy.start()
        sent.append(copy)
        return copy

    depth = own[0].shape[0]
    half = depth // 2
    rows = lambda start, count: pl.ds(pl.multiple_of(start, 16), count)

    def cast(index, start):
        def body(i, carry):
            here = rows(start + i * 16, 16)
            own[index][here, :] = masters[index][here, :].astype(jnp.bfloat16)
            return carry

        lax.fori_loop(0, half // 16, body, 0)

    pieces = [
        (index, slice(start, start + width))
        for index, width in enumerate(widths)
        for start in range(0, own[index].shape[1], width)
    ]
    mine, others = side * half, (1 - side) * half
    crossing = []
    for index in range(number):
        cast(index, mine)
        for piece, columns in pieces:
            if piece == index:
                crossing.append(
                    send(
                        "pair",
                        own[index].at[rows(mine, half), columns],
                        fulls[index].at[rows(group * depth + mine, half), columns],
                    )
                )
    local = []
    for index in range(number):
        cast(index, others)
        place_own = fulls[index].at[rows(group * depth, depth)]
        send("core", own[index], place_own)
        local.append(pltpu.make_async_copy(own[index], place_own, local_sem.at[index]))
        local[-1].start()
    passing = []
    for (index, columns), copy in zip(pieces, crossing):
        copy.wait_recv()
        here = fulls[index].at[rows(pair * depth + mine, half), columns]
        passing.append(send("side", here, here))
        send("core", here, here)
    last = []
    for (index, columns), copy in zip(pieces, passing):
        copy.wait_recv()
        here = fulls[index].at[rows(pair * depth + others, half), columns]
        last.append(send("core", here, here))
    for copy in sent:
        if all(copy is not other for other in crossing + passing):
            copy.wait_recv()

    @pl.when(trades)
    def _():
        for which in range(traded):
            trading(which).wait()

    @pl.when(jnp.logical_not(trades))
    def _():
        for which in range(traded):
            keeping(which).wait()

    for copy in sent:
        copy.wait_send()
    for copy in local:
        copy.wait()


def gather(masters, rows, number):
    widths = [next(w for w in (1280, master.shape[1]) if master.shape[1] % w == 0) for master in masters]
    count = len(masters)
    pieces = sum(master.shape[1] // width for master, width in zip(masters, widths))
    low, sends = jnp.bfloat16, 3 * pieces + pieces + count
    return pl.pallas_call(
        functools.partial(
            gather_kernel, number=count, traded=len(rows), widths=widths, half_place=lax.axis_size("ctx") // 2
        ),
        out_shape=[
            jax.ShapeDtypeStruct((value.shape[0] * lax.axis_size("fsdp"), value.shape[1]), low) for value in masters
        ]
        + [jax.ShapeDtypeStruct(value.shape, value.dtype) for value in rows],
        in_specs=[pl.BlockSpec(memory_space=pltpu.VMEM) for _ in masters]
        + [pl.BlockSpec(memory_space=pl.ANY) for _ in rows],
        out_specs=[pl.BlockSpec(memory_space=pl.ANY) for _ in masters + rows],
        scratch_shapes=[pltpu.VMEM(value.shape, low) for value in masters]
        + [
            pltpu.SemaphoreType.DMA((count,)),
            pltpu.SemaphoreType.DMA((sends,)),
            pltpu.SemaphoreType.DMA((sends,)),
            pltpu.SemaphoreType.DMA((len(rows), 3)),
        ],
        cost_estimate=pl.CostEstimate(
            flops=0, bytes_accessed=16 * sum(value.size * 4 for value in masters), transcendentals=0
        ),
        compiler_params=pltpu.CompilerParams(
            collective_id=number, has_side_effects=True, vmem_limit_bytes=56 * 1024 * 1024
        ),
        name="gather",
    )(*masters, *rows)


def gather_plain(master, *others):
    low = master.astype(jnp.bfloat16)
    return lax.all_gather(after(low, *others) if others else low, "fsdp", axis=0, tiled=True)


def gather_vector(vector):
    me, count = lax.axis_index("fsdp"), lax.axis_size("fsdp")
    low = vector.astype(jnp.bfloat16)
    by_distance = jnp.stack(
        [low]
        + [lax.ppermute(low, "fsdp", [(i, i ^ step) for i in range(count)]) for step in range(1, count)]
    )
    return jnp.concatenate(
        [lax.dynamic_index_in_dim(by_distance, me ^ shard, 0, keepdims=False) for shard in range(count)]
    )


def on_device(
    tokens,
    cotangent,
    lengths,
    widths,
    weight_qkv,
    moment_qkv,
    square_qkv,
    weight_out,
    moment_out,
    square_out,
    weight_up,
    moment_up,
    square_up,
    weight_down,
    moment_down,
    square_down,
    vectors,
    moment_vectors,
    square_vectors,
):
    ranks = lax.axis_size("ctx")
    core, top = bit_of("fsdp", 0), lax.axis_index("ctx") // (ranks // 2)
    here = core * (ranks // 2) + lax.rem(lax.axis_index("ctx"), ranks // 2)
    kept = core == top
    lengths, widths = [jnp.where(kept, value, swap(value, "fsdp", 0)) for value in (lengths, widths)]
    full_vector = gather_vector(vectors)
    if lax.axis_size("fsdp") == 4 and weight_qkv.shape[0] % 32 == 0 and weight_out.shape[0] % 32 == 0:
        full_qkv, full_out, own_tokens = gather(
            [weight_qkv, weight_out], [tokens.reshape(-1, tokens.shape[2])], 1
        )
    else:
        own_tokens = jnp.where(kept, tokens, trade(tokens))
        full_qkv, full_out = gather_plain(weight_qkv), gather_plain(weight_out)
    full_up = gather_plain(weight_up, full_out)
    full_down = gather_plain(weight_down, full_out)
    model_width = tokens.shape[2]
    hidden_units = full_up.shape[1]
    gain_one, shift_one, bias_qkv, bias_out, gain_two, shift_two, bias_up, bias_down = split_vector(
        full_vector.astype(jnp.float32), model_width, hidden_units
    )
    row_count = tokens.shape[0]
    slots_here = tokens.shape[1]
    slots_all = slots_here * lax.axis_size("ctx")
    token_count = row_count * slots_here
    local_heads = HEADS // ranks
    row_pos, col_pos, valid_slots, start_of, end_of = layout(lengths, widths, slots_all)
    valid_here = lax.dynamic_slice_in_dim(valid_slots, here * slots_here, slots_here, 1)
    cosine_table, sine_table = rotary_tables(by_block(row_pos, slots_here), by_block(col_pos, slots_here))
    cosine_here = lax.dynamic_index_in_dim(cosine_table, here, 0, keepdims=False)
    sine_here = lax.dynamic_index_in_dim(sine_table, here, 0, keepdims=False)
    low_high = jnp.stack([by_block(start_of, slots_here), by_block(end_of, slots_here)], axis=1)
    tile = slots_here * max(1, min(512 // slots_here, ranks))
    starts = start_of.reshape(row_count, slots_all // tile, tile)
    ends = end_of.reshape(row_count, slots_all // tile, tile)
    plain = (jnp.max(starts, axis=2) == 0) & (jnp.min(ends, axis=2) == slots_all)
    span = jnp.stack(
        [
            jnp.min(starts, axis=2) // tile,
            (jnp.max(ends, axis=2) + tile - 1) // tile,
            plain.astype(jnp.int32),
        ],
        axis=-1,
    ).astype(jnp.int32)
    flat_tokens = own_tokens.reshape(token_count, model_width).astype(jnp.float32)
    scaled_one, root_one = standardize(flat_tokens)
    first_normed = (scaled_one * gain_one + shift_one).astype(jnp.bfloat16)
    joined = (
        jnp.einsum("df,td->ft", full_qkv, first_normed, preferred_element_type=jnp.float32)
        + bias_qkv[:, None]
    )
    pairs = joined[: 2 * model_width].reshape(2, HEADS, 2, HEAD_DIM // 2, token_count)
    lower, upper_half = pairs[:, :, 0], pairs[:, :, 1]
    turned = jnp.stack(
        [lower * cosine_here - upper_half * sine_here, upper_half * cosine_here + lower * sine_here],
        axis=2,
    ).reshape(2 * model_width, token_count)
    heads_out = (
        jnp.concatenate([turned, joined[2 * model_width :]], axis=0)
        .astype(jnp.bfloat16)
        .reshape(3, local_heads, ranks, HEAD_DIM, token_count)
        .transpose(1, 2, 0, 3, 4)
    )
    heads_in = [exchange(heads_out[h]) for h in range(local_heads)]
    attended, lse, mixed = [], [], []
    for h in range(local_heads):
        result, stat = attend(span, heads_in[h], low_high)
        attended.append(result)
        lse.append(stat)
        mixed.append(exchange(result))
    came_cotangent = trade(after(cotangent, attended[0]))
    mixed = jnp.stack(mixed, axis=0).reshape(model_width, token_count)
    hidden = flat_tokens + jnp.einsum("it,io->to", mixed, full_out, preferred_element_type=jnp.float32) + bias_out
    scaled_two, root_two = standardize(hidden)
    second_normed = (scaled_two * gain_two + shift_two).astype(jnp.bfloat16)
    upper = jnp.dot(second_normed, full_up, preferred_element_type=jnp.float32) + bias_up
    sigma = jax.nn.sigmoid(1.702 * upper)
    active = (upper * sigma).astype(jnp.bfloat16)
    result = hidden + jnp.dot(active, full_down, preferred_element_type=jnp.float32) + bias_down
    output = result.astype(jnp.bfloat16).reshape(tokens.shape)
    own_cotangent = jnp.where(kept, cotangent, after(came_cotangent, active))
    grad_result = own_cotangent.reshape(token_count, model_width).astype(
        jnp.float32
    ) * valid_here.reshape(token_count, 1).astype(jnp.float32)
    grad_low = grad_result.astype(jnp.bfloat16)
    d_bias_down = jnp.sum(grad_result, axis=0)
    sum_down = Reduction(owner_order(active, 1), grad_low, "ti,to->io", 1)
    grad_low = after(grad_low, sum_down.leave())
    d_active = jnp.einsum("td,fd->tf", grad_low, full_down, preferred_element_type=jnp.float32)
    d_upper = (d_active * (sigma + 1.702 * upper * sigma * (1.0 - sigma))).astype(jnp.bfloat16)
    d_bias_up = jnp.sum(d_upper, axis=0, dtype=jnp.float32)
    d_upper = after(d_upper, sum_down.cross(d_upper))
    sum_up = Reduction(owner_order(second_normed, 1), d_upper, "ti,to->io", 1)
    d_upper = after(d_upper, sum_up.leave())
    d_second = jnp.einsum("tf,df->td", d_upper, full_up, preferred_element_type=jnp.float32)
    d_second = after(d_second, sum_up.cross(d_second))
    d_gain_two = jnp.sum(d_second * scaled_two, axis=0)
    d_shift_two = jnp.sum(d_second, axis=0)
    d_hidden = grad_result + norm_back(d_second, gain_two, scaled_two, root_two)
    d_branch = d_hidden.astype(jnp.bfloat16)
    d_bias_out = jnp.sum(d_branch, axis=0, dtype=jnp.float32)
    sum_out = Reduction(owner_order(mixed, 0), d_branch, "it,to->io", 0)
    d_branch = after(d_branch, sum_out.leave())
    d_mixed = (
        jnp.einsum("to,io->it", d_branch, full_out, preferred_element_type=jnp.float32)
        .astype(jnp.bfloat16)
        .reshape(local_heads, ranks, HEAD_DIM, token_count)
        .transpose(1, 0, 2, 3)
    )
    split = all(
        splits_of(value.shape[0], value.shape[1]) for value in (weight_qkv, weight_out, weight_up, weight_down)
    )
    came_mixed = exchange(d_mixed)
    d_attended = [came_mixed[:, h] for h in range(local_heads)]
    d_attended[0] = after(d_attended[0], sum_out.cross_later(d_mixed), output)
    normed_owners = owner_order(first_normed, 1)
    d_heads, sum_qkv = [], []
    for h in range(local_heads):
        d_heads.append(
            attend_back(
                span, heads_in[h], low_high, attended[h], d_attended[h], lse[h], cosine_table, sine_table
            )
        )
        if h == 0 and split:
            sent = sum_down.leave_ctx(d_heads[0])
            if local_heads > 1:
                d_attended[1] = after(d_attended[1], sent)
    backward = list(d_heads)
    for h in range(local_heads):
        came = after(exchange(d_heads[h]), backward[-1])
        if h > 0:
            sent = [sum_qkv[-1].leave()]
            sent.append(sum_qkv[-1].cross_pair(*sent))
            if split:
                sent.append(sum_down.leave_ctx(*sent))
            came = after(came, *sent)
        d_heads[h] = came.transpose(1, 0, 2, 3)
        right = d_heads[h].reshape(3 * ranks * HEAD_DIM, token_count)
        sum_qkv.append(Reduction(normed_owners, right, "ti,ot->io", 1))
    last = sum_qkv[-1].leave()
    d_joined = jnp.stack(d_heads, axis=1).reshape(3 * model_width, token_count)
    d_joined = after(d_joined, last)
    d_bias_qkv = jnp.sum(d_joined, axis=1, dtype=jnp.float32)
    d_first = jnp.einsum("jt,dj->td", d_joined, full_qkv, preferred_element_type=jnp.float32)
    d_first = after(d_first, sum_qkv[-1].cross_pair(d_first, send=not split))
    d_gain_one = jnp.sum(d_first * scaled_one, axis=0)
    d_shift_one = jnp.sum(d_first, axis=0)
    input_grad = (d_hidden + norm_back(d_first, gain_one, scaled_one, root_one)).reshape(
        tokens.shape
    )
    low_grad = input_grad.astype(jnp.bfloat16)
    d_vectors = jnp.concatenate(
        [
            d_gain_one,
            d_shift_one,
            d_bias_qkv,
            d_bias_out,
            d_gain_two,
            d_shift_two,
            d_bias_up,
            d_bias_down,
        ]
    )
    if split:
        (grad_up, grad_qkv, grad_down, grad_outw), total_squares, total_vectors = settle(
            [sum_up, Joined(sum_qkv, 3), sum_down, sum_out], [0, 1, 0, 1], after(d_vectors, low_grad), 0
        )
    else:
        grad_down, grad_up, grad_qkv, grad_outw = [
            lax.psum(add_up(value.parts).astype(jnp.bfloat16), "ctx")
            for value in (sum_down, sum_up, Joined(sum_qkv, 3, False), sum_out)
        ]
        total_squares = lax.psum(
            functools.reduce(
                jnp.add,
                [
                    jnp.sum(jnp.square(grad.astype(jnp.float32)))
                    for grad in (grad_down, grad_up, grad_outw, grad_qkv)
                ],
            ),
            "fsdp",
        )
        total_vectors = lax.psum(d_vectors, EVERYWHERE)
    total_squares = total_squares + jnp.sum(jnp.square(total_vectors))
    grad_vectors = lax.dynamic_slice_in_dim(
        total_vectors, lax.axis_index("fsdp") * vectors.shape[0], vectors.shape[0], 0
    )
    grad_down, grad_up, grad_outw, grad_qkv = [
        grad.astype(jnp.float32) for grad in (grad_down, grad_up, grad_outw, grad_qkv)
    ]
    came_output = trade(after(output, total_squares))
    output = jnp.where(kept, output, came_output)
    came_grad = trade(after(low_grad, total_squares))
    input_grad = jnp.where(kept, input_grad, came_grad.astype(jnp.float32))
    grad_norm = jnp.sqrt(total_squares)
    factor = jnp.minimum(1.0, clip_level / grad_norm)
    new_qkv = adam_update(
        weight_qkv, moment_qkv, square_qkv, grad_qkv, factor, rate_matrix, decay_matrix
    )
    new_out = adam_update(
        weight_out, moment_out, square_out, grad_outw, factor, rate_matrix, decay_matrix
    )
    new_up = adam_update(
        weight_up, moment_up, square_up, grad_up, factor, rate_matrix, decay_matrix
    )
    new_down = adam_update(
        weight_down, moment_down, square_down, grad_down, factor, rate_matrix, decay_matrix
    )
    new_vec = adam_update(
        vectors, moment_vectors, square_vectors, grad_vectors, factor, rate_vector, 0.0
    )
    return (
        output,
        input_grad,
        grad_norm,
        new_qkv[0],
        new_qkv[1],
        new_qkv[2],
        new_out[0],
        new_out[1],
        new_out[2],
        new_up[0],
        new_up[1],
        new_up[2],
        new_down[0],
        new_down[1],
        new_down[2],
        new_vec[0],
        new_vec[1],
        new_vec[2],
    )


def solution(mesh):
    placed = (
        P("fsdp", "ctx", None),
        P("fsdp", "ctx", None),
        P("fsdp", None),
        P("fsdp", None),
        P("fsdp", None),
        P("fsdp", None),
        P("fsdp", None),
        P("fsdp", None),
        P("fsdp", None),
        P("fsdp", None),
        P("fsdp", None),
        P("fsdp", None),
        P("fsdp", None),
        P("fsdp", None),
        P("fsdp", None),
        P("fsdp", None),
        P("fsdp"),
        P("fsdp"),
        P("fsdp"),
    )
    return jax.shard_map(
        on_device,
        mesh=mesh,
        in_specs=placed,
        out_specs=(
            P("fsdp", "ctx", None),
            P("fsdp", "ctx", None),
            P(),
            P("fsdp", None),
            P("fsdp", None),
            P("fsdp", None),
            P("fsdp", None),
            P("fsdp", None),
            P("fsdp", None),
            P("fsdp", None),
            P("fsdp", None),
            P("fsdp", None),
            P("fsdp", None),
            P("fsdp", None),
            P("fsdp", None),
            P("fsdp"),
            P("fsdp"),
            P("fsdp"),
        ),
        check_vma=False,
    )
```
